32 devices in a mesh: section: 2 (over x), dp: 16 (over z, y, core).
Axes of the slice: x: 2, y: 2, z: 4, core: 2. Of those that a mesh axis runs over, the one named last changes fastest.
Arguments:
- acts: float32 [2, 2, 16, 256, 768], P('section', None, 'dp'), may hold values from -6 to 6
- w_attn: bfloat16 [2, 768, 3072], P('section', 'dp'), may hold values from -4 to 4, as said below
- w_extra: bfloat16 [2, 768, 1536], P('section', 'dp'), may hold values from -4 to 4, as said below
- w_in: bfloat16 [2, 768, 4096], P('section', 'dp'), may hold values from -0.21875 to 0.21875
- w_out: bfloat16 [2, 2048, 768], P('section', 'dp'), may hold values from -0.125 to 0.125
- gains: bfloat16 [2, 3, 768], P('section', None, 'dp'), may hold values from 0.099609375 to 1.8984375
- segments: int32 [2, 16, 256], P(None, 'dp'), may hold values from 0 to 7, never falling along the last dimension, each value on 1 to 64 neighbouring positions
- cotangent: float32 [2, 2, 16, 256, 768], P('section', None, 'dp'), may hold values from -6 to 6
Outputs:
- outputs: float32 [2, 2, 16, 256, 768], P('section', None, 'dp')
- input_grad: float32 [2, 2, 16, 256, 768], P('section', None, 'dp')
- grad_attn: float32 [2, 768, 3072], P('section', 'dp')
- grad_extra: float32 [2, 768, 1536], P('section', 'dp')
- grad_in: float32 [2, 768, 4096], P('section', 'dp')
- grad_out: float32 [2, 2048, 768], P('section', 'dp')
- grad_gains: float32 [2, 3, 768], P('section', None, 'dp')
The draws below stay inside these ranges and needn't reach their ends.
Inputs may be any that keep to these rules, and one draw needn't show every extreme that they name: `segments`: along each decoder row the answer numbers never fall; each answer spans 1 to 64 tokens. `w_attn`: independent entries. `w_extra`: independent entries.
All inputs are finite; a program needn't handle non-finite values.
Results may differ from the reference program's by a relative error of at most 0.015.
Values may be sent and summed in bfloat16 or wider, within the bound.
A program may use at most 448 MiB of HBM per device.

```python
import math
import jax
import jax.numpy as jnp
import numpy as np
from jax import lax

D = 768
HEADS = 12
HDIM = 64
FF = 2048
SEQ = 256
MICRO = 2
IMAGES = 16


def draw_w_attn(key, part):
    key = jax.random.fold_in(key, 11)
    normal_draw = jax.random.normal(key, (2, D, 4 * D), jnp.float32)
    column = lax.broadcasted_iota(jnp.int32, (2, D, 4 * D), 2)
    factor = jnp.where(column >= 3 * D, 10.0, 1.0) / jnp.sqrt(jnp.float32(D))
    return jnp.clip(normal_draw * factor, -4.0, 4.0).astype(jnp.bfloat16)


def draw_w_extra(key, part):
    key = jax.random.fold_in(key, 23)
    normal_draw = jax.random.normal(key, (2, D, 2 * D), jnp.float32)
    column = lax.broadcasted_iota(jnp.int32, (2, D, 2 * D), 2)
    layer_slot = lax.broadcasted_iota(jnp.int32, (2, D, 2 * D), 0)
    factor = jnp.where((column >= D) & (layer_slot == 1), 10.0, 1.0) / jnp.sqrt(jnp.float32(D))
    return jnp.clip(normal_draw * factor, -4.0, 4.0).astype(jnp.bfloat16)


def levels(rng, shape, pieces, low, high):
    level = 1.0
    for axis_at, parts in pieces:
        heights = jax.random.uniform(jax.random.fold_in(jax.random.fold_in(rng, 6), axis_at), (parts,), jnp.float32, low / len(pieces), high / len(pieces))
        level = level * jnp.repeat(jnp.exp(heights), shape[axis_at] // parts).reshape((-1,) + (1,) * (len(shape) - 1 - axis_at))
    return level


def profile(count, total, bound, lean):
    loads = [(1 << 20) // math.isqrt(grade ** lean) + 1 for grade in range(2, count + 1)]
    rest, given = total - bound - (count - 1), [1] * (count - 1)
    while rest > 0:
        movable = [i for i in range(count - 1) if given[i] < bound]
        whole, remaining = sum([loads[i] for i in movable]), rest
        for i in movable:
            more = min(bound - given[i], max(1, remaining * loads[i] // whole), rest)
            given[i] = given[i] + more
            rest = rest - more
    return np.array([bound] + given)


def uneven(rng, count, total, bound, slope):
    if count == 2:
        one = jax.random.randint(rng, (), max(1, total - bound), min(bound, total - 1) + 1)
        return jnp.stack([one, total - one])
    lengths = jnp.asarray(profile(count, total, bound, slope), jnp.int32)
    twos = (count - 1) // 2
    source_of, receiver = lengths[1:1 + 2 * twos:2], lengths[2:2 + 2 * twos:2]
    margin = jnp.minimum(source_of - 1, bound - receiver)
    moved = jax.random.randint(jax.random.fold_in(rng, 1), (twos,), 0, 1 << 20) % (margin + 1)
    lengths = lengths.at[1:1 + 2 * twos:2].set(source_of - moved).at[2:2 + 2 * twos:2].set(receiver + moved)
    return lengths[jax.random.permutation(jax.random.fold_in(rng, 2), count)]


def noise(stream_key, dims, width, bound, pieces=(), held_as=jnp.bfloat16):
    loudness = levels(stream_key, dims, pieces, -0.22, 0.18) if pieces else 1.0
    values = jax.random.normal(stream_key, dims, jnp.float32) * width * loudness
    return jnp.minimum(jnp.maximum(values, -bound), bound).astype(held_as)


def setup_inputs(seed: int = 0) -> dict:
    splits = jax.random.split(jax.random.key(seed), 9)
    return {
        "acts": noise(splits[0], (2, MICRO, IMAGES, SEQ, D), 1.0, 6.0, ((0, 2), (2, 16)), jnp.float32),
        "w_attn": draw_w_attn(jax.random.fold_in(splits[8], 71), 0),
        "w_extra": draw_w_extra(jax.random.fold_in(splits[8], 71), 0),
        "w_in": noise(splits[3], (2, D, 2 * FF), D ** -0.5, 0.21875, ((0, 2), (1, 16))),
        "w_out": noise(splits[4], (2, FF, D), FF ** -0.5, 0.125, ((0, 2), (1, 16))),
        "gains": jnp.clip(1.0 + 0.18 * jax.random.normal(splits[5], (2, 3, D), jnp.float32), 0.099609375, 1.8984375).astype(jnp.bfloat16),
        "segments": jax.vmap(lambda own: jnp.searchsorted(jnp.cumsum(uneven(own, 8, SEQ, SEQ // 4, 0)), jnp.arange(SEQ), side="right"))(jax.random.split(splits[6], MICRO * IMAGES)).reshape((MICRO, IMAGES, SEQ)).astype(jnp.int32),
        "cotangent": noise(splits[7], (2, MICRO, IMAGES, SEQ, D), 1.0, 6.0, ((0, 2), (2, 16)), jnp.float32),
    }


@jax.custom_vjp
def low(v):
    return lax.optimization_barrier(v.astype(jnp.bfloat16)).astype(jnp.float32)

@jax.custom_vjp
def low_back(v):
    return v

def low_keep(v):
    return (low(v), None)

def low_pass(kept, grad):
    return (grad,)

def back_keep(v):
    return (v, None)

def back_low(kept, grad):
    return (low(grad),)
low.defvjp(low_keep, low_pass)
low_back.defvjp(back_keep, back_low)

def rms_norm(activations, gain_row):
    return activations * lax.rsqrt(lax.optimization_barrier(jnp.mean(activations * activations, axis=-1, keepdims=True)) + 1e-06) * gain_row

def projection(left_side, weight):
    return low_back(jnp.dot(left_side, weight, precision=lax.Precision.HIGHEST))

def heads_of(activations):
    return activations.reshape(activations.shape[0], HEADS, HDIM)

def attend(queries, keys_in, values, allowed):
    raw_logits = jnp.einsum('qhd,khd->hqk', heads_of(queries), heads_of(keys_in), precision=lax.Precision.HIGHEST)
    logits = low_back(raw_logits) * HDIM ** (-0.5)
    if allowed is not None:
        logits = jnp.where(allowed[None], logits, -1e+30)
    row_peak = lax.optimization_barrier(jnp.max(logits, axis=-1, keepdims=True))
    weights = jnp.exp(logits - row_peak)
    softmax_out = weights / lax.optimization_barrier(jnp.sum(weights, axis=-1, keepdims=True))
    mixed_heads = jnp.einsum('hqk,khd->qhd', low(softmax_out), heads_of(values), precision=lax.Precision.HIGHEST)
    return low(low_back(mixed_heads.reshape(queries.shape[0], D)))

def self_attention(inputs, gain_row, w_attn, allowed):
    normed = low(rms_norm(inputs, gain_row))
    packed = low(projection(normed, w_attn[:, :3 * D]))
    mixed_heads = attend(packed[:, :D], packed[:, D:2 * D], packed[:, 2 * D:], allowed)
    return inputs + projection(mixed_heads, w_attn[:, 3 * D:])

def feed_forward(inputs, gain_row, w_in, w_out):
    normed = low(rms_norm(inputs, gain_row))
    gated = projection(normed, w_in)
    hidden = low(jax.nn.gelu(gated[:, :FF], approximate=True) * gated[:, FF:])
    return inputs + projection(hidden, w_out)

def encoder_layer(inputs, params):
    w_attn, w_extra, w_in, w_out, gain_rows = params
    middle = self_attention(inputs, gain_rows[0], w_attn, None)
    result = feed_forward(middle, gain_rows[1], w_in, w_out)
    cross_kv = low(projection(low(rms_norm(result, gain_rows[2])), w_extra))
    return (result, cross_kv)

def decoder_layer(inputs, cross_kv, segment_ids, params):
    w_attn, w_extra, w_in, w_out, gain_rows = params
    positions = jnp.arange(SEQ)
    allowed = (segment_ids[:, None] == segment_ids[None, :]) & (positions[None, :] <= positions[:, None])
    middle = self_attention(inputs, gain_rows[0], w_attn, allowed)
    queries = low(projection(low(rms_norm(middle, gain_rows[2])), w_extra[:, :D]))
    mixed_heads = attend(queries, cross_kv[:, :D], cross_kv[:, D:], None)
    after_cross = middle + projection(mixed_heads, w_extra[:, D:])
    return feed_forward(after_cross, gain_rows[1], w_in, w_out)

def reference(acts, w_attn, w_extra, w_in, w_out, gains, segments, cotangent):
    params = tuple((weight.astype(jnp.float32) for weight in (w_attn, w_extra, w_in, w_out, gains)))
    image_count = MICRO * IMAGES

    def forward(inputs, params):
        encoder_params = tuple((weight[0] for weight in params))
        decoder_params = tuple((weight[1] for weight in params))

        @jax.checkpoint
        def one_image(carried, image_item):
            enc_rows, dec_rows, segment_ids = image_item
            enc_result, cross_kv = encoder_layer(enc_rows, encoder_params)
            dec_result = decoder_layer(dec_rows, cross_kv, segment_ids, decoder_params)
            return (carried, (enc_result, dec_result))
        _, (enc_all, dec_all) = lax.scan(one_image, None, (inputs[0].reshape(image_count, SEQ, D), inputs[1].reshape(image_count, SEQ, D), segments.reshape(image_count, SEQ)))
        return jnp.stack([enc_all.reshape(MICRO, IMAGES, SEQ, D), dec_all.reshape(MICRO, IMAGES, SEQ, D)])
    outputs, pull_back = jax.vjp(forward, acts, params)
    input_grad, gradients = pull_back(cotangent)
    return (outputs, input_grad, gradients[0], gradients[1], gradients[2], gradients[3], gradients[4])
```

```python
import jax
import jax.numpy as jnp
from jax import lax
from jax.experimental import pallas as pl
from jax.experimental.pallas import tpu as pltpu
from jax.sharding import PartitionSpec as P

D=768; HEADS=12; HDIM=64; FF=2048; SEQ=256; MICRO=2
ROWS=MICRO*SEQ
BF=jnp.bfloat16; F32=jnp.float32
QKV, OP, XA, XB, WIN, KV = 0, 3*D, 4*D, 5*D, 6*D, 6*D+2*FF
WIDE = KV + 2*D
NN=(((1,),(0,)),((),())); NT=(((1,),(1,)),((),()))

def mul(start, k): return pl.multiple_of(start, k)
def dot(a,b,dims=NN): return lax.dot_general(a,b,dims,preferred_element_type=F32)

def wide_cols(wa, start, size):
    return wa[:, :, :, :, pl.ds(start, size)].reshape(D, size)

def rms_rows(v):
    return lax.rsqrt(jnp.mean(v*v, axis=-1, keepdims=True) + 1e-6)

def norm_forward(v_ref, gain, n_ref, first=0, count=ROWS):
    @pl.loop(0, count//64)
    def _(i):
        rows=pl.ds(mul(first+i*64,64),64)
        v=v_ref[rows,:]
        n_ref[rows,:]=(v*rms_rows(v)*gain).astype(BF)

def norm_backward(v_ref, gain, dn_ref, g_ref, dgain_ref, slot, first=0, count=ROWS):
    def body(i, acc):
        rows=pl.ds(mul(first+i*64,64),64)
        v=v_ref[rows,:]; dn=dn_ref[rows,:]
        r=rms_rows(v)
        t=dn*gain
        vr=v*r
        g_ref[rows,:]+= r*(t - vr*jnp.mean(t*vr,axis=-1,keepdims=True))
        return acc+jnp.sum(dn*vr,axis=0,keepdims=True)
    acc=lax.fori_loop(0,count//64,body,jnp.zeros((1,D),F32))
    dgain_ref[slot:slot+1,:]+=acc

def transpose_to(src_ref, dst_ref, first=0, count=ROWS):
    cols=src_ref.shape[1]
    @pl.loop(0, cols//128)
    def _(j):
        cs=pl.ds(mul(j*128,128),128)
        dst_ref[cs, pl.ds(first,count)] = src_ref[pl.ds(first,count),cs].T

def project(n_ref, wa, wcol, out_ref, ocol, total, tile, first=0, count=ROWS):
    @pl.loop(0, total//tile)
    def _(j):
        w=wide_cols(wa, mul(wcol+j*tile,128), tile)
        out_ref[pl.ds(first,count), pl.ds(mul(ocol+j*tile,128),tile)] = dot(n_ref[pl.ds(first,count),:], w).astype(out_ref.dtype)

def project_add(a_ref, wa, wcol, base_ref, out_ref, tile, first=0, count=ROWS):
    rows=pl.ds(first,count)
    @pl.loop(0, D//tile)
    def _(j):
        w=wide_cols(wa, mul(wcol+j*tile,128), tile)
        cs=pl.ds(mul(j*tile,128),tile)
        out_ref[rows,cs] = base_ref[rows,cs]+dot(a_ref[rows,:], w)

def back_project(g_ref, gcol, wa, wcol, total, tile, acc_ref, first=0, count=ROWS, fresh=True):
    rows=pl.ds(first,count)
    def part(j):
        w=wide_cols(wa, mul(wcol+j*tile,128), tile)
        return dot(g_ref[rows, pl.ds(mul(gcol+j*tile,128),tile)], w, NT)
    if fresh:
        acc_ref[rows,:]=part(0)
    @pl.loop(1 if fresh else 0, total//tile)
    def _(j):
        acc_ref[rows,:]+=part(j)

def attend_forward(q_ref, qc, k_ref, kc, v_ref, vc, o_ref, oT_ref, mask_ref, start, stop):
    @pl.loop(start, stop)
    def _(i):
        img=i//6; p=i%6
        rows=pl.ds(mul(img*SEQ,SEQ),SEQ)
        def cols(base): return pl.ds(mul(base+p*128,128),128)
        q2=q_ref[rows,cols(qc)]*jnp.asarray(0.125,BF)
        k2=k_ref[rows,cols(kc)]
        vT=v_ref[rows,cols(vc)].T
        lane=lax.broadcasted_iota(jnp.int32,(SEQ,128),1)//64
        parts=[]
        for a in range(2):
            ka=jnp.where(lane==a,k2,jnp.zeros_like(k2))
            s=dot(ka,q2,NT)
            if mask_ref is not None:
                s=jnp.where(mask_ref[img].astype(F32)>0,s,-1e30)
            e=jnp.exp(s-jnp.max(s,axis=0,keepdims=True))
            w=(e*(1.0/jnp.sum(e,axis=0,keepdims=True))).astype(BF)
            parts.append(dot(vT[a*64:(a+1)*64],w))
        oT=jnp.concatenate(parts,axis=0).astype(BF)
        oT_ref[pl.ds(mul(p*128,128),128),rows]=oT
        o_ref[rows,cols(0)]=oT.T

def attend_backward(q_ref, qc, k_ref, kc, v_ref, vc, d_ref, mask_ref, dq_ref, dqc, dk_ref, dkc, dv_ref, dvc, start, stop):
    @pl.loop(start, stop)
    def _(i):
        img=i//6; p=i%6
        rows=pl.ds(mul(img*SEQ,SEQ),SEQ)
        def cols(base): return pl.ds(mul(base+p*128,128),128)
        q2=q_ref[rows,cols(qc)]
        qs=q2*jnp.asarray(0.125,BF)
        k2=k_ref[rows,cols(kc)]
        v2=v_ref[rows,cols(vc)]
        d2=d_ref[rows,cols(0)]
        kT=k2.T
        lane=lax.broadcasted_iota(jnp.int32,(SEQ,128),1)//64
        dqT=[]; dk=[]; dv=[]
        for a in range(2):
            mine=lane==a
            s=dot(jnp.where(mine,k2,jnp.zeros_like(k2)),qs,NT)
            if mask_ref is not None:
                s=jnp.where(mask_ref[img].astype(F32)>0,s,-1e30)
            e=jnp.exp(s-jnp.max(s,axis=0,keepdims=True))
            w=e*(1.0/jnp.sum(e,axis=0,keepdims=True))
            dw=dot(jnp.where(mine,v2,jnp.zeros_like(v2)),d2,NT)
            wd=w*dw
            ds=((wd-w*jnp.sum(wd,axis=0,keepdims=True))*0.125).astype(BF)
            dv.append(dot(w.astype(BF),d2))
            dk.append(dot(ds,q2))
            dqT.append(dot(kT[a*64:(a+1)*64],ds))
        dq_ref[rows,cols(dqc)]=jnp.concatenate(dqT,axis=0).astype(BF).T
        dk_ref[rows,cols(dkc)]=jnp.where(lane==0,dk[0],dk[1]).astype(BF)
        dv_ref[rows,cols(dvc)]=jnp.where(lane==0,dv[0],dv[1]).astype(BF)

C0=0.7978845608028654; C1=0.044715
def gated_forward(n_ref, wa, gu_ref, hid_ref, start, stop, first=0, count=ROWS, tile=256):
    rows=pl.ds(first,count)
    @pl.loop(start, stop)
    def _(j):
        lo=pl.ds(mul(j*tile,tile),tile); hi=pl.ds(mul(FF+j*tile,tile),tile)
        gate=dot(n_ref[rows,:], wide_cols(wa, mul(WIN+j*tile,128), tile))
        up=dot(n_ref[rows,:], wide_cols(wa, mul(WIN+FF+j*tile,128), tile))
        t=jnp.tanh(C0*(gate+C1*gate*gate*gate))
        hid_ref[rows,lo]=((0.5*gate*(1.0+t))*up).astype(BF)
        gu_ref[rows,lo]=gate.astype(BF)
        gu_ref[rows,hi]=up.astype(BF)

def down_forward(hid_ref, wo, base_ref, out_ref, first=0, count=ROWS):
    rows=pl.ds(first,count)
    def part(j):
        return dot(hid_ref[rows,pl.ds(mul(j*256,256),256)], wo[j//2,j%2].reshape(256,D))
    out_ref[rows,:]=base_ref[rows,:]+part(0)
    @pl.loop(1, FF//256)
    def _(j):
        out_ref[rows,:]+=part(j)

def gated_backward(gb_ref, wo, gu_ref, start, stop, first=0, count=ROWS, tile=256):
    rows=pl.ds(first,count)
    @pl.loop(start, stop)
    def _(j):
        lo=pl.ds(mul(j*tile,tile),tile); hi=pl.ds(mul(FF+j*tile,tile),tile)
        dh=dot(gb_ref[rows,:], wo[j//2,j%2].reshape(256,D), NT)
        gate=gu_ref[rows,lo].astype(F32); up=gu_ref[rows,hi].astype(F32)
        sq=gate*gate
        t=jnp.tanh(C0*(gate+C1*gate*sq))
        h=0.5*(1.0+t)
        slope=h+0.5*gate*(1.0-t*t)*(C0+(3*C0*C1)*sq)
        gu_ref[rows,lo]=(dh*up*slope).astype(BF)
        gu_ref[rows,hi]=(dh*(gate*h)).astype(BF)

def half_rows(nT_ref, c):
    return jnp.concatenate([nT_ref[pl.ds(mul((2*j+c)*48,16),48),:] for j in range(8)],axis=0)


MESH = pl.DeviceIdType.MESH
BIG = 1152

LINE = (
    ("attn", 0, "wide", QKV, 1152),
    ("attn", 1152, "wide", QKV + 1152, 1152),
    ("attn", 3 * D, "wide", OP, D),
    ("in", 0, "wide", WIN, 1024),
    ("in", FF, "wide", WIN + FF, 1024),
    ("in", 1024, "wide", WIN + 1024, 1024),
    ("in", FF + 1024, "wide", WIN + FF + 1024, 1024),
    ("out", 0, "tall", 0, 384),
    ("out", 384, "tall", 384, 384),
)
PAIR = (("extra", 0, 512), ("extra", 512, 512), ("extra", 1024, 512))
SUMS = {
    "out0": ("tall", 0, 384), "out1": ("tall", 384, 384),
    "in0": ("wide", WIN, 1024), "in1": ("wide", WIN + 1024, 1024),
    "in2": ("wide", WIN + FF, 1024), "in3": ("wide", WIN + FF + 1024, 1024),
    "x0": ("wide", XA, D), "x1": ("wide", XB, D),
    "k0": ("wide", KV, D), "k1": ("wide", KV + D, D),
    "o": ("wide", OP, D),
    "q0": ("wide", QKV, 1152), "q1": ("wide", QKV + 1152, 1152),
}
SUM_NAMES = tuple(SUMS)
OUT_OF = {
    "out0": ("out", 0), "out1": ("out", 384), "in0": ("in", 0), "in1": ("in", 1024), "in2": ("in", FF), "in3": ("in", FF + 1024),
    "x0": ("extra", 0), "x1": ("extra", D), "o": ("attn", 3 * D), "q0": ("attn", 0), "q1": ("attn", 1152),
}
FREE = {"out": 0, "in": 1, "x": 2, "k": 3, "o": 4, "q": 5}


def scratch_list():
    V, DMA, REG = pltpu.VMEM, pltpu.SemaphoreType.DMA, pltpu.SemaphoreType.REGULAR
    n, m, s = len(LINE), len(PAIR), len(SUMS)
    return dict(
        wide=V((4, 2, 2, 48, WIDE), BF), tall=V((4, 2, 2, 128, D), BF),
        y_wide=V((4, 48, WIDE), BF), y_tall=V((4, 128, D), BF),
        z_wide=V((3, 48, WIDE), BF), z_tall=V((3, 128, D), BF),
        stage=V((2, 4, 2, 48, BIG), BF), stage_tall=V((4, 2, 128, D), BF),
        fin=V((2, 48, BIG), F32), fin_tall=V((2, 128, 384), F32),
        x=V((ROWS, D), F32), mid=V((ROWS, D), F32), late=V((ROWS, D), F32), g=V((ROWS, D), F32), acc=V((ROWS, D), F32),
        n1=V((ROWS, D), BF), n2=V((ROWS, D), BF), n3=V((ROWS, D), BF), xin=V((ROWS, D), BF), nT=V((D, ROWS), BF),
        qkv=V((ROWS, 3 * D), BF), ao=V((ROWS, D), BF), aoT=V((D, ROWS), BF),
        xq=V((ROWS, D), BF), kv=V((ROWS, 2 * D), BF), cm=V((ROWS, D), BF), cmT=V((D, ROWS), BF),
        gu=V((ROWS, 2 * FF), BF), hid=V((ROWS, FF), BF), gb=V((ROWS, D), BF),
        mask=V((MICRO, SEQ, SEQ), BF), xsend=V((ROWS, D), BF),
        gz=V((4, 8, D), F32), gy=V((2, 8, D), F32), gc=V((2, 8, D), F32), gain=V((8, D), F32),
        dgain=V((8, D), F32), hz=V((4, 8, D), F32), hy=V((2, 8, D), F32), hc=V((2, 8, D), F32),
        s_in=DMA((4,)), s_own=DMA((n + m,)),
        s_rs=DMA((n + m, 3)), s_rr=DMA((n + m, 3)), s_ls=DMA((n + m, 3)), s_lr=DMA((n + m, 3)),
        s_ys=DMA((n + m, 4)), s_yr=DMA((n + m, 4)), s_cs=DMA((n + 2 * m,)), s_cr=DMA((n + 2 * m,)),
        s_xs=DMA((m,)), s_xr=DMA((m,)), s_ms=DMA((MICRO,)), s_mr=DMA((MICRO,)),
        s_gs=DMA((2, 5)), s_gr=DMA((2, 5)),
        t_cs=DMA((s,)), t_cr=DMA((s,)), t_ys=DMA((s,)), t_yr=DMA((s,)), t_zs=DMA((s, 3)), t_zr=DMA((s, 3)),
        t_xs=DMA((2,)), t_xr=DMA((2,)), t_out=DMA((s,)), s_out=DMA((3,)),
        free=REG((len(FREE),)),
    )


def whole_kernel(*refs):
    (acts_h, cot_h, attn_h, extra_h, in_h, out_h, gain_in, seg_in) = refs[:8]
    (res_o, grad_o, attn_o, extra_o, gin_o, gout_o, gain_o) = refs[8:15]
    R = type("Refs", (), {})()
    for name, ref in zip(scratch_list(), refs[15:]):
        setattr(R, name, ref)
    src = {"attn": attn_h, "extra": extra_h, "in": in_h, "out": out_h}
    dst = {"attn": attn_o, "extra": extra_o, "in": gin_o, "out": gout_o}
    buf = {"wide": R.wide, "tall": R.tall}
    ybuf = {"wide": R.y_wide, "tall": R.y_tall}
    zbuf = {"wide": R.z_wide, "tall": R.z_tall}

    section = lax.axis_index("section")
    me = lax.axis_index("dp")
    z, y, c = me // 4, (me // 2) % 2, me % 2
    first, second = section == 0, section == 1
    at = lambda zz, yy, cc: {"dp": zz * 4 + yy * 2 + cc}
    right, left = at(lax.rem(z + 1, 4), y, c), at(lax.rem(z + 3, 4), y, c)
    z_peer = [at(lax.rem(z + k, 4), y, c) for k in (1, 2, 3)]
    y_peer, c_peer, x_peer = at(z, 1 - y, c), at(z, y, 1 - c), {"section": 1 - section}

    def remote(a, b, ss, rs, dev):
        return pltpu.make_async_remote_copy(a, b, ss, rs, device_id=dev, device_id_type=MESH)

    def local(a, b, s):
        return pltpu.make_async_copy(a, b, s)

    def when(cond, fn):
        pl.when(cond)(fn)

    barrier = pltpu.get_barrier_semaphore()
    everyone = z_peer + [y_peer, c_peer, x_peer]
    for peer in everyone:
        pl.semaphore_signal(barrier, inc=1, device_id=peer, device_id_type=MESH)
    pl.semaphore_wait(barrier, len(everyone))

    n, m = len(LINE), len(PAIR)
    xoff = jnp.where(first, KV, XA)

    def spot(i):
        if i < n:
            arg, lo, name, col, size = LINE[i]
            return buf[name], pl.ds(col, size), src[arg].at[:, pl.ds(lo, size)]
        arg, lo, size = PAIR[i - n]
        return R.wide, pl.ds(mul(xoff + lo, 128), size), src[arg].at[:, pl.ds(lo, size)]

    def own_copy(i):
        b, cs, h = spot(i)
        return local(h, b.at[z, y, c, :, cs], R.s_own.at[i])

    def line_block(i, zz):
        b, cs, h = spot(i)
        return b.at[zz, y, c, :, cs] if i < n else b.at[zz, :, c, :, cs]

    def go_right(i, s):
        _, _, h = spot(i)
        d = line_block(i, z - s)
        return remote(h if s == 0 and i < n else d, d, R.s_rs.at[i, s], R.s_rr.at[i, s], right)

    def go_left(i, s):
        _, _, h = spot(i)
        d = line_block(i, z + s)
        return remote(h if s == 0 and i < n else d, d, R.s_ls.at[i, s], R.s_lr.at[i, s], left)

    def from_left(i, s):
        d = line_block(i, z - s)
        return remote(d, d, R.s_rs.at[i, s - 1], R.s_rr.at[i, s - 1], left)

    def from_right(i, s):
        d = line_block(i, z + s)
        return remote(d, d, R.s_ls.at[i, s - 1], R.s_lr.at[i, s - 1], right)

    def across(i, zz, own=False):
        b, cs, h = spot(i)
        d = b.at[zz, y, c, :, cs]
        return remote(h if own else d, d, R.s_ys.at[i, zz if i < n else 0], R.s_yr.at[i, zz if i < n else 0], y_peer)

    def across_in(i, zz):
        b, cs, h = spot(i)
        d = b.at[zz, 1 - y, c, :, cs]
        k = zz if i < n else 0
        return remote(d, d, R.s_ys.at[i, k], R.s_yr.at[i, k], y_peer)

    def core_in(i):
        b, cs, h = spot(i)
        d = b.at[:, :, 1 - c, :, cs]
        return remote(d, d, R.s_cs.at[i], R.s_cr.at[i], c_peer)

    def to_core(i):
        b, cs, h = spot(i)
        return remote(b.at[:, :, c, :, cs], b.at[:, :, c, :, cs], R.s_cs.at[i], R.s_cr.at[i], c_peer)

    def kv_cols(i):
        return pl.ds(KV + PAIR[i][1], PAIR[i][2])

    def kv_over(i):
        d = R.wide.at[:, :, c, :, kv_cols(i)]
        return remote(d, d, R.s_xs.at[i], R.s_xr.at[i], x_peer)

    def kv_core(i):
        d = R.wide.at[:, :, c, :, kv_cols(i)]
        return remote(d, d, R.s_cs.at[n + m + i], R.s_cr.at[n + m + i], c_peer)

    def kv_core_in(i):
        d = R.wide.at[:, :, 1 - c, :, kv_cols(i)]
        return remote(d, d, R.s_cs.at[n + m + i], R.s_cr.at[n + m + i], c_peer)

    def begin(i):
        own_copy(i).start()
        if i < n:
            when(z < 3, lambda: go_right(i, 0).start())
            when(z > 0, lambda: go_left(i, 0).start())
        across(i, z, True).start()

    def pair_turn(i):
        own_copy(i).wait()
        across_in(i, z).wait_recv()
        when(z < 3, lambda: go_right(i, 0).start())
        when(z > 0, lambda: go_left(i, 0).start())

    def hop(i, s):
        def lower():
            from_left(i, s).wait_recv()
            if s < 3:
                when(z < 3, lambda: go_right(i, s).start())
            if i < n:
                across(i, z - s).start()

        def upper():
            from_right(i, s).wait_recv()
            if s < 3:
                when(z > 0, lambda: go_left(i, s).start())
            if i < n:
                across(i, z + s).start()

        when(z >= s, lower)
        when(z + s <= 3, upper)

    def line_done(i):
        if i < n:
            own_copy(i).wait()
            for zz in range(4):
                across_in(i, zz).wait_recv()
            to_core(i).start()
        else:
            when(second, lambda: to_core(i).start())
            when(first, lambda: kv_over(i - n).start())

    def have(i):
        if i < n:
            core_in(i).wait_recv()
        else:
            when(second, lambda: core_in(i).wait_recv())

    def kv_turn(i):
        kv_over(i).wait_recv()
        kv_core(i).start()

    def sent(i):
        for s in range(3):
            when((z >= s) & (z < 3), lambda: go_right(i, s).wait_send())
            when((z + s <= 3) & (z > 0), lambda: go_left(i, s).wait_send())
        for zz in range(4 if i < n else 1):
            across(i, zz).wait_send()
        if i < n:
            to_core(i).wait_send()
        else:
            when(second, lambda: to_core(i).wait_send())
            when(second, lambda: kv_core(i - n).wait_send())
            when(first, lambda: kv_over(i - n).wait_send())

    def tick(t):
        for j in range(m):
            if t == 2 * j:
                begin(n + j)
            if t == 2 * j + 1:
                pair_turn(n + j)
            for s in (1, 2, 3):
                if t == 2 * j + 1 + s:
                    hop(n + j, s)
            if t == 2 * j + 5:
                line_done(n + j)
        if t < n:
            begin(t)
        for s in (1, 2, 3):
            if 0 <= t - s < n:
                hop(t - s, s)
        if 0 <= t - 4 < n:
            line_done(t - 4)

    gain_own = local(gain_in, R.gz.at[z], R.s_in.at[0])
    gain_own.start()
    x_in = local(acts_h, R.x, R.s_in.at[1])
    x_in.start()
    g_in = local(cot_h, R.g, R.s_in.at[2])
    g_in.start()

    def small_z(own_ref, slots, row):
        return [remote(own_ref, slots.at[z], R.s_gs.at[row, k], R.s_gr.at[row, k], z_peer[k]) for k in range(3)]

    def small_pair(slots, row, k, dev):
        return remote(slots.at[0], slots.at[1], R.s_gs.at[row, k], R.s_gr.at[row, k], dev)

    gzc = small_z(gain_in, R.gz, 0)
    for q in gzc:
        q.start()
    tick(0)
    gain_own.wait()
    for q in gzc:
        q.wait_recv()
    R.gy[0] = (R.gz[0] + R.gz[1]) + (R.gz[2] + R.gz[3])
    q = small_pair(R.gy, 0, 3, y_peer)
    q.start()
    tick(1)
    q.wait()
    R.gc[0] = R.gy[0] + R.gy[1]
    q = small_pair(R.gc, 0, 4, c_peer)
    q.start()
    q.wait()
    R.gain[...] = R.gc[0] + R.gc[1]
    for q in gzc:
        q.wait_send()
    gain = lambda k: R.gain[k : k + 1, :]

    ones = jnp.where(first, 1.0, 0.0)
    for img in range(MICRO):
        row = jnp.broadcast_to(seg_in[img : img + 1, :].astype(F32), (SEQ, SEQ))
        key = lax.broadcasted_iota(jnp.int32, (SEQ, SEQ), 0)
        query = lax.broadcasted_iota(jnp.int32, (SEQ, SEQ), 1)
        allowed = jnp.where((row.T == row) & (key <= query), 1.0, ones)
        R.mask[img] = allowed.astype(BF)
    R.dgain[...] = jnp.zeros_like(R.dgain)

    x_in.wait()
    norm_forward(R.x, gain(0), R.n1)
    for t in range(2, 7):
        tick(t)
    have(0), have(1)
    project(R.n1, R.wide, QKV, R.qkv, 0, 3 * D, 768)

    def self_attention(a, b):
        attend_forward(R.qkv, 0, R.qkv, D, R.qkv, 2 * D, R.ao, R.aoT, R.mask, a, b)

    self_attention(0, 4)
    tick(7)
    self_attention(4, 8)
    have(2)
    tick(8)
    self_attention(8, 12)
    project_add(R.ao, R.wide, OP, R.x, R.mid, 384)
    tick(9)

    def enc_tiles(a, b):
        when(first, lambda: gated_forward(R.n2, R.wide, R.gu, R.hid, a, b))

    when(first, lambda: norm_forward(R.mid, gain(1), R.n2))
    when(second, lambda: norm_forward(R.mid, gain(2), R.n3))
    have(3), have(4)
    enc_tiles(0, 2)
    tick(10)
    enc_tiles(2, 4)
    have(5)
    tick(11)
    have(6)
    enc_tiles(4, 8)
    tick(12)
    have(7)

    def message(img):
        rows = pl.ds(img * SEQ, SEQ)
        return remote(R.xsend.at[rows], R.xin.at[rows], R.s_ms.at[img], R.s_mr.at[img], x_peer)

    def down(base, out, cols):
        for lo in cols:
            cs = pl.ds(lo, 384)
            R_w = R.tall[:, :, :, :, cs].reshape(FF, 384)
            out[:, cs] = base[:, cs] + dot(R.hid[...], R_w)

    when(first, lambda: down(R.mid, R.late, (0,)))
    have(8)

    def enc_tail():
        down(R.mid, R.late, (384,))
        for img in range(MICRO):
            norm_forward(R.late, gain(2), R.xsend, img * SEQ, SEQ)
            message(img).start()

    when(first, enc_tail)
    for j in range(m):
        have(n + j)
    when(second, lambda: [kv_turn(j) for j in range(m)] and None)
    for i in range(n + m):
        sent(i)

    res_copy = local(R.late, res_o, R.s_out.at[0])

    def dec_forward():
        project(R.n3, R.wide, XA, R.xq, 0, D, 384)
        for j in range(m):
            kv_core_in(j).wait_recv()
        for img in range(MICRO):
            message(img).wait_recv()
            project(R.xin, R.wide, KV, R.kv, 0, 2 * D, 768, img * SEQ, SEQ)
            attend_forward(R.xq, 0, R.kv, 0, R.kv, D, R.cm, R.cmT, None, img * 6, img * 6 + 6)
        project_add(R.cm, R.wide, XB, R.mid, R.late, 384)
        norm_forward(R.late, gain(1), R.n2)
        gated_forward(R.n2, R.wide, R.gu, R.hid, 0, 8)

    when(second, dec_forward)

    def sum_spot(name):
        b, lo, size = SUMS[name]
        return SUM_NAMES.index(name), b, pl.ds(lo, size), size

    stage_of = {}

    def core_copy(name):
        k, b, cs, size = sum_spot(name)
        if b == "tall":
            s = R.stage_tall.at[:, :, :, cs]
        else:
            s = R.stage.at[stage_of[name], :, :, :, pl.ds(0, size)]
        return remote(s, buf[b].at[:, :, c, :, cs], R.t_cs.at[k], R.t_cr.at[k], c_peer)

    def y_copy(name):
        k, b, cs, size = sum_spot(name)
        return remote(buf[b].at[:, 1 - y, c, :, cs], ybuf[b].at[:, :, cs], R.t_ys.at[k], R.t_yr.at[k], y_peer)

    def z_copies(name):
        k, b, cs, size = sum_spot(name)
        return [
            remote(buf[b].at[lax.rem(z + j + 1, 4), y, c, :, cs], zbuf[b].at[j, :, cs], R.t_zs.at[k, j], R.t_zr.at[k, j], z_peer[j])
            for j in range(3)
        ]

    def release(name):
        pl.semaphore_signal(R.free.at[FREE[name]], inc=1, device_id=c_peer, device_id_type=MESH)

    def claim(name):
        pl.semaphore_wait(R.free.at[FREE[name]], 1)

    order = []

    def grad_wide(name, nT, g_ref, gcol, tile):
        k, b, cs, size = sum_spot(name)
        lo = SUMS[name][1]
        slot = len(order) % 2
        if len(order) >= 2:
            core_copy(order[-2]).wait_send()
        stage_of[name] = slot
        order.append(name)
        lhs = half_rows(nT, 1 - c)

        @pl.loop(0, size // tile)
        def _(j):
            w = dot(lhs, g_ref[:, pl.ds(mul(gcol + j * tile, 128), tile)]).astype(BF)
            R.stage[slot, :, :, :, pl.ds(mul(j * tile, 128), tile)] = w.reshape(4, 2, 48, tile)

        core_copy(name).start()
        mine = half_rows(nT, c)

        @pl.loop(0, size // tile)
        def _(j):
            w = dot(mine, g_ref[:, pl.ds(mul(gcol + j * tile, 128), tile)]).astype(BF)
            R.wide[:, :, c, :, pl.ds(mul(lo + j * tile, 128), tile)] = w.reshape(4, 2, 48, tile)

    def drain():
        for name in order[-2:]:
            core_copy(name).wait_send()
        order.clear()

    def grad_tall():
        def rows_of(j, cc):
            units = pl.ds(mul((2 * j + cc) * 128, 128), 128)
            return dot(R.hid[:, units].T, R.gb[...]).astype(BF)

        @pl.loop(0, 8)
        def _(j):
            R.stage_tall[j // 2, j % 2] = rows_of(j, 1 - c)

        core_copy("out0").start()
        core_copy("out1").start()

        @pl.loop(0, 8)
        def _(j):
            R.tall[j // 2, j % 2, c] = rows_of(j, c)

    def core_stage(name, pass_on=True):
        k, b, cs, size = sum_spot(name)
        w = buf[b]
        landed = w.at[:, :, 1 - c, :, cs]
        remote(landed, landed, R.t_cs.at[k], R.t_cr.at[k], c_peer).wait_recv()

        @pl.loop(0, 8)
        def _(j):
            own = w[j // 2, j % 2, c, :, cs].astype(F32)
            w[j // 2, j % 2, c, :, cs] = (own + w[j // 2, j % 2, 1 - c, :, cs].astype(F32)).astype(BF)

        if pass_on:
            y_copy(name).start()

    def y_stage(name):
        k, b, cs, size = sum_spot(name)
        y_copy(name).wait_recv()
        w, r = buf[b], ybuf[b]

        @pl.loop(0, 4)
        def _(j):
            w[j, y, c, :, cs] = (w[j, y, c, :, cs].astype(F32) + r[j, :, cs].astype(F32)).astype(BF)

        for q in z_copies(name):
            q.start()

    finished = []

    def out_copy(name):
        k, b, cs, size = sum_spot(name)
        arg, lo = OUT_OF[name]
        kind = [f for f in finished if SUMS[f][0] == b]
        slot = kind.index(name) % 2
        f = R.fin_tall.at[slot] if b == "tall" else R.fin.at[slot, :, pl.ds(0, size)]
        return local(f, dst[arg].at[:, pl.ds(lo, size)], R.t_out.at[k])

    def z_stage(name):
        k, b, cs, size = sum_spot(name)
        for q in z_copies(name):
            q.wait_recv()
        kind = [f for f in finished if SUMS[f][0] == b]
        slot = len(kind) % 2
        if len(kind) >= 2:
            out_copy(kind[-2]).wait()
        finished.append(name)
        r = zbuf[b]
        total = (buf[b][z, y, c, :, cs].astype(F32) + r[0, :, cs].astype(F32)) + (
            r[1, :, cs].astype(F32) + r[2, :, cs].astype(F32)
        )
        if b == "tall":
            R.fin_tall[slot] = total
        else:
            R.fin[slot, :, pl.ds(0, size)] = total
        out_copy(name).start()

    def over_copy(j):
        k, b, cs, size = sum_spot(("k0", "k1")[j])
        return remote(
            R.wide.at[:, :, c, :, cs], R.wide.at[:, :, c, :, pl.ds(XA + j * D, D)], R.t_xs.at[j], R.t_xr.at[j], x_peer
        )

    def round_g():
        R.gb[...] = R.g[...].astype(BF)

    g_in.wait()

    def enc_entry():
        for img in range(MICRO):
            message(img).wait_send()
        res_copy.start()
        for img in range(MICRO):
            message(img).wait_recv()
        R.acc[...] = R.xin[...].astype(F32)
        norm_backward(R.late, gain(2), R.acc, R.g, R.dgain, 2)

    when(first, enc_entry)
    round_g()
    def dec_late():
        down(R.late, R.acc, (0, 384))

    dec_res_copy = local(R.acc, res_o, R.s_out.at[0])

    def dec_result():
        dec_late()
        dec_res_copy.start()

    when(second, dec_result)
    gated_backward(R.gb, R.tall, R.gu, 0, 8)
    release("out")
    claim("out")
    grad_tall()
    when(second, lambda: dec_res_copy.wait())
    back_project(R.gu, 0, R.wide, WIN, 2 * FF, 512, R.acc)
    release("in")
    core_stage("out0")
    core_stage("out1")
    when(first, lambda: res_copy.wait())
    when(first, lambda: norm_backward(R.mid, gain(1), R.acc, R.g, R.dgain, 1))
    when(second, lambda: norm_backward(R.late, gain(1), R.acc, R.g, R.dgain, 1))
    transpose_to(R.n2, R.nT)
    claim("in")
    grad_wide("in0", R.nT, R.gu, 0, 512)
    grad_wide("in1", R.nT, R.gu, 1024, 512)
    core_stage("in0")
    grad_wide("in2", R.nT, R.gu, FF, 512)
    core_stage("in1")
    grad_wide("in3", R.nT, R.gu, FF + 1024, 512)
    core_stage("in2")
    round_g()

    def project_back(g_ref, wcol, out_ref):
        out_ref[...] = dot(g_ref[...], wide_cols(R.wide, wcol, D), NT).astype(BF)

    def dec_cross():
        project_back(R.gb, XB, R.xsend)
        for img in range(MICRO):
            attend_backward(
                R.xq, 0, R.kv, 0, R.kv, D, R.xsend, None, R.xq, 0, R.kv, 0, R.kv, D, img * 6, img * 6 + 6
            )
            back_project(R.kv, 0, R.wide, KV, 2 * D, 768, R.acc, img * SEQ, SEQ)
            rows = pl.ds(img * SEQ, SEQ)
            R.xsend[rows, :] = R.acc[rows, :].astype(BF)
            message(img).start()

    when(second, dec_cross)
    core_stage("in3")
    y_stage("out0")
    y_stage("out1")

    def dec_cross_grads():
        release("k")
        transpose_to(R.xin, R.nT)
        claim("k")
        grad_wide("k0", R.nT, R.kv, 0, 384)
        grad_wide("k1", R.nT, R.kv, D, 384)
        back_project(R.xq, 0, R.wide, XA, D, 768, R.acc)
        release("x")
        core_stage("k0", False)
        over_copy(0).start()
        core_stage("k1", False)
        over_copy(1).start()
        transpose_to(R.n3, R.nT)
        claim("x")
        grad_wide("x0", R.nT, R.xq, 0, 384)
        grad_wide("x1", R.cmT, R.gb, 0, 384)
        norm_backward(R.mid, gain(2), R.acc, R.g, R.dgain, 2)
        core_stage("x0")
        core_stage("x1")
        for img in range(MICRO):
            message(img).wait_send()
        drain()
        round_g()

    drain()
    when(second, dec_cross_grads)
    y_stage("in0")

    project_back(R.gb, OP, R.ao)
    release("o")
    attend_backward(R.qkv, 0, R.qkv, D, R.qkv, 2 * D, R.ao, R.mask, R.qkv, 0, R.qkv, D, R.qkv, 2 * D, 0, 6)
    y_stage("in1")
    attend_backward(R.qkv, 0, R.qkv, D, R.qkv, 2 * D, R.ao, R.mask, R.qkv, 0, R.qkv, D, R.qkv, 2 * D, 6, 12)
    back_project(R.qkv, 0, R.wide, QKV, 3 * D, 768, R.acc)
    release("q")
    y_stage("in2")
    claim("o")
    grad_wide("o", R.aoT, R.gb, 0, 384)
    transpose_to(R.n1, R.nT)
    claim("q")
    grad_wide("q0", R.nT, R.qkv, 0, 384)
    core_stage("o")
    grad_wide("q1", R.nT, R.qkv, 1152, 384)
    core_stage("q0")
    core_stage("q1")
    norm_backward(R.x, gain(0), R.acc, R.g, R.dgain, 0)
    grad_copy = local(R.g, grad_o, R.s_out.at[1])
    grad_copy.start()

    def enc_x():
        for j in range(2):
            over_copy(j).wait_recv()
            y_copy(("x0", "x1")[j]).start()

    when(first, enc_x)

    R.hc[0] = R.dgain[...]
    q = small_pair(R.hc, 1, 4, c_peer)
    q.start()
    q.wait()
    R.hy[0] = R.hc[0] + R.hc[1]
    q = small_pair(R.hy, 1, 3, y_peer)
    q.start()
    q.wait()
    R.gain[...] = R.hy[0] + R.hy[1]
    hzc = small_z(R.gain, R.hz, 1)
    for q in hzc:
        q.start()

    y_stage("in3")
    z_stage("out0")
    z_stage("out1")
    y_stage("x0")
    z_stage("in0")
    y_stage("x1")
    z_stage("in1")
    y_stage("o")
    z_stage("in2")
    z_stage("in3")
    y_stage("q0")
    z_stage("x0")
    z_stage("x1")
    y_stage("q1")
    z_stage("o")
    z_stage("q0")
    z_stage("q1")
    for q in hzc:
        q.wait()
    R.hz[z] = R.gain[...]
    R.dgain[...] = (R.hz[0] + R.hz[1]) + (R.hz[2] + R.hz[3])
    gain_copy = local(R.dgain, gain_o, R.s_out.at[2])
    gain_copy.start()
    for name in ("out0", "out1"):
        core_copy(name).wait_send()
    drain()
    for name in finished:
        y_copy(name).wait_send()
        for q in z_copies(name):
            q.wait_send()
    when(second, lambda: [over_copy(j).wait_send() for j in range(2)] and None)
    for b in ("tall", "wide"):
        for name in [f for f in finished if SUMS[f][0] == b][-2:]:
            out_copy(name).wait()
    grad_copy.wait()
    gain_copy.wait()


def from_behind(block, axis, distance):
    devices = range(lax.axis_size(axis))
    route = [(i - distance, i) for i in devices if i - distance in devices]
    return lax.ppermute(block, axis, route)


def rms_norm(activations, gain_row):
    return (
        activations
        * lax.rsqrt(jnp.mean(activations * activations, axis=-1, keepdims=True) + 1e-06)
        * gain_row
    )


def product(left_side, right_side):
    return jnp.dot(left_side, right_side, preferred_element_type=jnp.float32)


def weight_grad(left_side, right_side):
    return jnp.einsum("sd,se->de", left_side, right_side, preferred_element_type=jnp.float32)


def input_back(gradient, weight):
    return jnp.einsum("se,de->sd", gradient, weight, preferred_element_type=jnp.float32)


def norm_back(activations, gain_row, gradient):
    _, pull_back = jax.vjp(rms_norm, activations, gain_row)
    return pull_back(gradient)


def heads_of(activations):
    return activations.reshape(activations.shape[0], HEADS, HDIM)


def logits_of(queries, keys_in, allowed):
    raw_logits = jnp.einsum(
        "qhd,khd->hqk", heads_of(queries), heads_of(keys_in), preferred_element_type=jnp.float32
    ) * HDIM ** (-0.5)
    if allowed is None:
        return raw_logits
    return jnp.where(allowed[None], raw_logits, -1e30)


def attend_plain(queries, keys_in, values, allowed):
    logits = logits_of(queries, keys_in, allowed)
    row_peak = jnp.max(logits, axis=-1, keepdims=True)
    weights = jnp.exp(logits - row_peak)
    row_total = jnp.sum(weights, axis=-1, keepdims=True)
    softmax_out = (weights / row_total).astype(jnp.bfloat16)
    mixed_heads = jnp.einsum(
        "hqk,khd->qhd", softmax_out, heads_of(values), preferred_element_type=jnp.float32
    )
    return (
        mixed_heads.reshape(queries.shape[0], D).astype(jnp.bfloat16),
        row_peak + jnp.log(row_total),
    )


def attend_plain_back(queries, keys_in, values, allowed, log_total, grad_mixed):
    softmax_out = jnp.exp(logits_of(queries, keys_in, allowed) - log_total)
    grad_heads = heads_of(grad_mixed)
    grad_softmax = jnp.einsum(
        "qhd,khd->hqk", grad_heads, heads_of(values), preferred_element_type=jnp.float32
    )
    grad_values = jnp.einsum(
        "hqk,qhd->khd",
        softmax_out.astype(jnp.bfloat16),
        grad_heads,
        preferred_element_type=jnp.float32,
    )
    inner_sum = jnp.sum(softmax_out * grad_softmax, axis=-1, keepdims=True)
    grad_logits = (softmax_out * (grad_softmax - inner_sum) * HDIM ** (-0.5)).astype(jnp.bfloat16)
    grad_queries = jnp.einsum(
        "hqk,khd->qhd", grad_logits, heads_of(keys_in), preferred_element_type=jnp.float32
    )
    grad_keys = jnp.einsum(
        "hqk,qhd->khd", grad_logits, heads_of(queries), preferred_element_type=jnp.float32
    )
    query_count = queries.shape[0]
    key_count = keys_in.shape[0]
    return (
        grad_queries.reshape(query_count, D),
        grad_keys.reshape(key_count, D),
        grad_values.reshape(key_count, D),
    )


def self_forward(inputs, gain_row, w_attn, allowed):
    normed = rms_norm(inputs, gain_row).astype(jnp.bfloat16)
    packed = product(normed, w_attn[:, : 3 * D]).astype(jnp.bfloat16)
    mixed_heads, log_total = attend_plain(
        packed[:, :D], packed[:, D : 2 * D], packed[:, 2 * D :], allowed
    )
    return (
        inputs + product(mixed_heads, w_attn[:, 3 * D :]),
        (normed, packed, mixed_heads, log_total),
    )


def self_backward(inputs, gain_row, w_attn, allowed, kept_values, grad_result):
    normed, packed, mixed_heads, log_total = kept_values
    grad_low = grad_result.astype(jnp.bfloat16)
    grad_proj = weight_grad(mixed_heads, grad_low)
    grad_mixed = input_back(grad_low, w_attn[:, 3 * D :]).astype(jnp.bfloat16)
    grad_queries, grad_keys, grad_values = attend_plain_back(
        packed[:, :D], packed[:, D : 2 * D], packed[:, 2 * D :], allowed, log_total, grad_mixed
    )
    grad_packed = jnp.concatenate([grad_queries, grad_keys, grad_values], axis=1).astype(
        jnp.bfloat16
    )
    grad_qkv = weight_grad(normed, grad_packed)
    grad_inputs, grad_gain = norm_back(
        inputs, gain_row, input_back(grad_packed, w_attn[:, : 3 * D])
    )
    return (grad_result + grad_inputs, grad_gain, jnp.concatenate([grad_qkv, grad_proj], axis=1))


def gated_unit(gated):
    return jax.nn.gelu(gated[:, :FF], approximate=True) * gated[:, FF:]


def ffn_forward(inputs, gain_row, w_in, w_out):
    normed = rms_norm(inputs, gain_row).astype(jnp.bfloat16)
    gated = product(normed, w_in)
    hidden = gated_unit(gated).astype(jnp.bfloat16)
    return (inputs + product(hidden, w_out), (normed, gated, hidden))


def ffn_backward(inputs, gain_row, w_in, w_out, kept_values, grad_result):
    normed, gated, hidden = kept_values
    grad_low = grad_result.astype(jnp.bfloat16)
    grad_wout = weight_grad(hidden, grad_low)
    _, pull_back = jax.vjp(gated_unit, gated)
    grad_gated = pull_back(input_back(grad_low, w_out))[0].astype(jnp.bfloat16)
    grad_win = weight_grad(normed, grad_gated)
    grad_inputs, grad_gain = norm_back(inputs, gain_row, input_back(grad_gated, w_in))
    return (grad_result + grad_inputs, grad_gain, grad_win, grad_wout)


def encoder_forward(inputs, weights):
    w_attn, w_extra, w_in, w_out, gain_rows = weights
    middle, first_kept = self_forward(inputs, gain_rows[0], w_attn, None)
    result, second_kept = ffn_forward(middle, gain_rows[1], w_in, w_out)
    normed = rms_norm(result, gain_rows[2]).astype(jnp.bfloat16)
    cross_kv = product(normed, w_extra).astype(jnp.bfloat16)
    return (result, cross_kv, (middle, first_kept, second_kept, normed))


def encoder_backward(inputs, weights, grad_result, grad_kv):
    w_attn, w_extra, w_in, w_out, gain_rows = weights
    result, _, kept_values = encoder_forward(inputs, weights)
    middle, first_kept, second_kept, normed = kept_values
    grad_extra = weight_grad(normed, grad_kv)
    grad_final, gain_final = norm_back(result, gain_rows[2], input_back(grad_kv, w_extra))
    grad_middle, gain_late, grad_win, grad_wout = ffn_backward(
        middle, gain_rows[1], w_in, w_out, second_kept, grad_result + grad_final
    )
    grad_inputs, gain_early, grad_attn = self_backward(
        inputs, gain_rows[0], w_attn, None, first_kept, grad_middle
    )
    return (
        grad_inputs,
        (
            grad_attn,
            grad_extra,
            grad_win,
            grad_wout,
            jnp.stack([gain_early, gain_late, gain_final]),
        ),
    )


def decoder_step(inputs, cross_kv, allowed, weights, grad_result):
    w_attn, w_extra, w_in, w_out, gain_rows = weights
    middle, first_kept = self_forward(inputs, gain_rows[0], w_attn, allowed)
    query_in = rms_norm(middle, gain_rows[2]).astype(jnp.bfloat16)
    queries = product(query_in, w_extra[:, :D]).astype(jnp.bfloat16)
    mixed_heads, log_total = attend_plain(queries, cross_kv[:, :D], cross_kv[:, D:], None)
    after_cross = middle + product(mixed_heads, w_extra[:, D:])
    result, second_kept = ffn_forward(after_cross, gain_rows[1], w_in, w_out)
    grad_after, gain_late, grad_win, grad_wout = ffn_backward(
        after_cross, gain_rows[1], w_in, w_out, second_kept, grad_result
    )
    grad_low = grad_after.astype(jnp.bfloat16)
    grad_cross_out = weight_grad(mixed_heads, grad_low)
    grad_mixed = input_back(grad_low, w_extra[:, D:]).astype(jnp.bfloat16)
    grad_queries, grad_keys, grad_values = attend_plain_back(
        queries, cross_kv[:, :D], cross_kv[:, D:], None, log_total, grad_mixed
    )
    grad_queries = grad_queries.astype(jnp.bfloat16)
    grad_cross_in = weight_grad(query_in, grad_queries)
    grad_normed, gain_cross = norm_back(
        middle, gain_rows[2], input_back(grad_queries, w_extra[:, :D])
    )
    grad_inputs, gain_early, grad_attn = self_backward(
        inputs, gain_rows[0], w_attn, allowed, first_kept, grad_after + grad_normed
    )
    grad_kv = jnp.concatenate([grad_keys, grad_values], axis=1).astype(jnp.bfloat16)
    gradients = (
        grad_attn,
        jnp.concatenate([grad_cross_in, grad_cross_out], axis=1),
        grad_win,
        grad_wout,
        jnp.stack([gain_early, gain_late, gain_cross]),
    )
    return (result, grad_inputs, grad_kv, gradients)


def general(acts, w_attn, w_extra, w_in, w_out, gains, segments, cotangent):
    gathered = (
        lax.all_gather(w_attn[0], "dp", axis=0, tiled=True),
        lax.all_gather(w_extra[0], "dp", axis=0, tiled=True),
        lax.all_gather(w_in[0], "dp", axis=0, tiled=True),
        lax.all_gather(w_out[0], "dp", axis=0, tiled=True),
        lax.all_gather(gains[0], "dp", axis=1, tiled=True),
    )
    weights = gathered[:4] + (gathered[4].astype(jnp.float32),)
    inputs = acts[0, :, 0]
    upstream = cotangent[0, :, 0]
    is_first = lax.axis_index("section") == 0
    positions = jnp.arange(SEQ)
    causal = positions[None, :] <= positions[:, None]
    zero_message = jnp.zeros((SEQ, 2 * D), jnp.bfloat16)
    zero_grads = tuple((jnp.zeros(weight.shape, jnp.float32) for weight in weights))
    carried = (jnp.zeros((MICRO, SEQ, D), jnp.float32), jnp.zeros((MICRO, SEQ, D), jnp.float32))
    received = zero_message
    returned = zero_message
    totals = zero_grads
    moments = MICRO + 2
    for moment in range(moments):

        def first_section(carried, received, returned):
            results, grad_inputs = carried
            message = zero_message
            fresh_grads = zero_grads
            if moment < MICRO:
                result, message, _ = encoder_forward(inputs[moment], weights)
                results = results.at[moment].set(result)
            if moment >= 2:
                grad_rows, fresh_grads = encoder_backward(
                    inputs[moment - 2], weights, upstream[moment - 2], returned
                )
                grad_inputs = grad_inputs.at[moment - 2].set(grad_rows)
            return ((results, grad_inputs), message, zero_message, fresh_grads)

        def second_section(carried, received, returned):
            results, grad_inputs = carried
            message = zero_message
            fresh_grads = zero_grads
            if 1 <= moment <= MICRO:
                segment_ids = segments[moment - 1, 0]
                allowed = (segment_ids[:, None] == segment_ids[None, :]) & causal
                result, grad_rows, message, fresh_grads = decoder_step(
                    inputs[moment - 1], received, allowed, weights, upstream[moment - 1]
                )
                results = results.at[moment - 1].set(result)
                grad_inputs = grad_inputs.at[moment - 1].set(grad_rows)
            return ((results, grad_inputs), zero_message, message, fresh_grads)

        carried, forward_message, back_message, fresh_grads = lax.cond(
            is_first, first_section, second_section, carried, received, returned
        )
        if moment < MICRO:
            received = from_behind(forward_message, "section", 1)
        if 1 <= moment <= MICRO:
            returned = from_behind(back_message, "section", -1)
        if moment >= 1:
            totals = tuple((jnp.add(*couple) for couple in zip(totals, fresh_grads)))
    results, grad_inputs = carried
    final = (
        lax.psum_scatter(totals[0], "dp", scatter_dimension=0, tiled=True),
        lax.psum_scatter(totals[1], "dp", scatter_dimension=0, tiled=True),
        lax.psum_scatter(totals[2], "dp", scatter_dimension=0, tiled=True),
        lax.psum_scatter(totals[3], "dp", scatter_dimension=0, tiled=True),
        lax.psum_scatter(totals[4], "dp", scatter_dimension=1, tiled=True),
    )
    return (
        results[None, :, None],
        grad_inputs[None, :, None],
        final[0][None],
        final[1][None],
        final[2][None],
        final[3][None],
        final[4][None],
    )


def step(acts, w_attn, w_extra, w_in, w_out, gains, segments, cotangent):
    me = lax.axis_index("dp")
    share = gains.shape[2]
    own_gain = lax.dynamic_update_slice(jnp.zeros((8, D), F32), gains[0].astype(F32), (0, me * share))
    anywhere = pl.BlockSpec(memory_space=pl.ANY)
    shape = lambda *s: jax.ShapeDtypeStruct(s, F32)
    scratch = scratch_list()
    results, input_grad, attn, extra, win, wout, gain = pl.pallas_call(
        whole_kernel,
        out_shape=(
            shape(ROWS, D), shape(ROWS, D), shape(48, 4 * D), shape(48, 2 * D), shape(48, 2 * FF), shape(128, D), shape(8, D),
        ),
        in_specs=[anywhere] * 7 + [pl.BlockSpec(memory_space=pltpu.VMEM)],
        out_specs=[anywhere] * 7,
        scratch_shapes=list(scratch.values()),
        compiler_params=pltpu.CompilerParams(
            collective_id=0, has_side_effects=True, vmem_limit_bytes=63 * 2**20
        ),
    )(
        acts.reshape(ROWS, D), cotangent.reshape(ROWS, D), w_attn[0], w_extra[0], w_in[0], w_out[0], own_gain,
        segments.reshape(MICRO, SEQ),
    )
    grad_gains = lax.dynamic_slice(gain, (0, me * share), (3, share))
    like = (1, MICRO, 1, SEQ, D)
    return (
        results.reshape(like), input_grad.reshape(like), attn[None], extra[None], win[None], wout[None], grad_gains[None],
    )


def solution(mesh):
    in_specs = (
        P("section", None, "dp", None, None),
        P("section", "dp", None),
        P("section", "dp", None),
        P("section", "dp", None),
        P("section", "dp", None),
        P("section", None, "dp"),
        P(None, "dp", None),
        P("section", None, "dp", None, None),
    )
    out_specs = (
        P("section", None, "dp", None, None),
        P("section", None, "dp", None, None),
        P("section", "dp", None),
        P("section", "dp", None),
        P("section", "dp", None),
        P("section", "dp", None),
        P("section", None, "dp"),
    )
    fits = mesh.shape["dp"] == 16
    return jax.shard_map(step if fits else general, mesh=mesh, in_specs=in_specs, out_specs=out_specs, check_vma=False)
```

```python
import jax
import jax.numpy as jnp
from jax import lax
from jax.experimental import pallas as pl
from jax.experimental.pallas import tpu as pltpu
from jax.sharding import PartitionSpec as P

D=768; HEADS=12; HDIM=64; FF=2048; SEQ=256; MICRO=2
ROWS=MICRO*SEQ
BF=jnp.bfloat16; F32=jnp.float32
QKV, OP, XA, XB, WIN, KV = 0, 3*D, 4*D, 5*D, 6*D, 6*D+2*FF
WIDE = KV + 2*D
NN=(((1,),(0,)),((),())); NT=(((1,),(1,)),((),()))

def mul(start, k): return pl.multiple_of(start, k)
def dot(a,b,dims=NN): return lax.dot_general(a,b,dims,preferred_element_type=F32)

def wide_cols(wa, start, size):
    return wa[:, :, :, :, pl.ds(start, size)].reshape(D, size)

def rms_rows(v):
    return lax.rsqrt(jnp.mean(v*v, axis=-1, keepdims=True) + 1e-6)

def norm_forward(v_ref, gain, n_ref, first=0, count=ROWS):
    @pl.loop(0, count//64)
    def _(i):
        rows=pl.ds(mul(first+i*64,64),64)
        v=v_ref[rows,:]
        n_ref[rows,:]=(v*rms_rows(v)*gain).astype(BF)

def norm_backward(v_ref, gain, dn_ref, g_ref, dgain_ref, slot, first=0, count=ROWS):
    def body(i, acc):
        rows=pl.ds(mul(first+i*64,64),64)
        v=v_ref[rows,:]; dn=dn_ref[rows,:]
        r=rms_rows(v)
        t=dn*gain
        vr=v*r
        g_ref[rows,:]+= r*(t - vr*jnp.mean(t*vr,axis=-1,keepdims=True))
        return acc+jnp.sum(dn*vr,axis=0,keepdims=True)
    acc=lax.fori_loop(0,count//64,body,jnp.zeros((1,D),F32))
    dgain_ref[slot:slot+1,:]+=acc

def transpose_to(src_ref, dst_ref, first=0, count=ROWS):
    cols=src_ref.shape[1]
    @pl.loop(0, cols//128)
    def _(j):
        cs=pl.ds(mul(j*128,128),128)
        dst_ref[cs, pl.ds(first,count)] = src_ref[pl.ds(first,count),cs].T

def project(n_ref, wa, wcol, out_ref, ocol, total, tile, first=0, count=ROWS):
    @pl.loop(0, total//tile)
    def _(j):
        w=wide_cols(wa, mul(wcol+j*tile,128), tile)
        out_ref[pl.ds(first,count), pl.ds(mul(ocol+j*tile,128),tile)] = dot(n_ref[pl.ds(first,count),:], w).astype(out_ref.dtype)

def project_add(a_ref, wa, wcol, base_ref, out_ref, tile, first=0, count=ROWS):
    rows=pl.ds(first,count)
    @pl.loop(0, D//tile)
    def _(j):
        w=wide_cols(wa, mul(wcol+j*tile,128), tile)
        cs=pl.ds(mul(j*tile,128),tile)
        out_ref[rows,cs] = base_ref[rows,cs]+dot(a_ref[rows,:], w)

def back_project(g_ref, gcol, wa, wcol, total, tile, acc_ref, first=0, count=ROWS, fresh=True):
    rows=pl.ds(first,count)
    def part(j):
        w=wide_cols(wa, mul(wcol+j*tile,128), tile)
        return dot(g_ref[rows, pl.ds(mul(gcol+j*tile,128),tile)], w, NT)
    if fresh:
        acc_ref[rows,:]=part(0)
    @pl.loop(1 if fresh else 0, total//tile)
    def _(j):
        acc_ref[rows,:]+=part(j)

def attend_forward(q_ref, qc, k_ref, kc, v_ref, vc, o_ref, oT_ref, mask_ref, start, stop):
    @pl.loop(start, stop)
    def _(i):
        img=i//6; p=i%6
        rows=pl.ds(mul(img*SEQ,SEQ),SEQ)
        def cols(base): return pl.ds(mul(base+p*128,128),128)
        q2=q_ref[rows,cols(qc)]*jnp.asarray(0.125,BF)
        k2=k_ref[rows,cols(kc)]
        vT=v_ref[rows,cols(vc)].T
        lane=lax.broadcasted_iota(jnp.int32,(SEQ,128),1)//64
        parts=[]
        for a in range(2):
            ka=jnp.where(lane==a,k2,jnp.zeros_like(k2))
            s=dot(ka,q2,NT)
            if mask_ref is not None:
                s=jnp.where(mask_ref[img].astype(F32)>0,s,-1e30)
            e=jnp.exp(s-jnp.max(s,axis=0,keepdims=True))
            w=(e*(1.0/jnp.sum(e,axis=0,keepdims=True))).astype(BF)
            parts.append(dot(vT[a*64:(a+1)*64],w))
        oT=jnp.concatenate(parts,axis=0).astype(BF)
        oT_ref[pl.ds(mul(p*128,128),128),rows]=oT
        o_ref[rows,cols(0)]=oT.T

def attend_backward(q_ref, qc, k_ref, kc, v_ref, vc, d_ref, mask_ref, dq_ref, dqc, dk_ref, dkc, dv_ref, dvc, start, stop):
    @pl.loop(start, stop)
    def _(i):
        img=i//6; p=i%6
        rows=pl.ds(mul(img*SEQ,SEQ),SEQ)
        def cols(base): return pl.ds(mul(base+p*128,128),128)
        q2=q_ref[rows,cols(qc)]
        qs=q2*jnp.asarray(0.125,BF)
        k2=k_ref[rows,cols(kc)]
        v2=v_ref[rows,cols(vc)]
        d2=d_ref[rows,cols(0)]
        kT=k2.T
        lane=lax.broadcasted_iota(jnp.int32,(SEQ,128),1)//64
        dqT=[]; dk=[]; dv=[]
        for a in range(2):
            mine=lane==a
            s=dot(jnp.where(mine,k2,jnp.zeros_like(k2)),qs,NT)
            if mask_ref is not None:
                s=jnp.where(mask_ref[img].astype(F32)>0,s,-1e30)
            e=jnp.exp(s-jnp.max(s,axis=0,keepdims=True))
            w=e*(1.0/jnp.sum(e,axis=0,keepdims=True))
            dw=dot(jnp.where(mine,v2,jnp.zeros_like(v2)),d2,NT)
            wd=w*dw
            ds=((wd-w*jnp.sum(wd,axis=0,keepdims=True))*0.125).astype(BF)
            dv.append(dot(w.astype(BF),d2))
            dk.append(dot(ds,q2))
            dqT.append(dot(kT[a*64:(a+1)*64],ds))
        dq_ref[rows,cols(dqc)]=jnp.concatenate(dqT,axis=0).astype(BF).T
        dk_ref[rows,cols(dkc)]=jnp.where(lane==0,dk[0],dk[1]).astype(BF)
        dv_ref[rows,cols(dvc)]=jnp.where(lane==0,dv[0],dv[1]).astype(BF)

C0=0.7978845608028654; C1=0.044715
def gated_forward(n_ref, wa, gu_ref, hid_ref, start, stop, first=0, count=ROWS, tile=256):
    rows=pl.ds(first,count)
    @pl.loop(start, stop)
    def _(j):
        lo=pl.ds(mul(j*tile,tile),tile); hi=pl.ds(mul(FF+j*tile,tile),tile)
        gate=dot(n_ref[rows,:], wide_cols(wa, mul(WIN+j*tile,128), tile))
        up=dot(n_ref[rows,:], wide_cols(wa, mul(WIN+FF+j*tile,128), tile))
        t=jnp.tanh(C0*(gate+C1*gate*gate*gate))
        hid_ref[rows,lo]=((0.5*gate*(1.0+t))*up).astype(BF)
        gu_ref[rows,lo]=gate.astype(BF)
        gu_ref[rows,hi]=up.astype(BF)

def down_forward(hid_ref, wo, base_ref, out_ref, first=0, count=ROWS):
    rows=pl.ds(first,count)
    def part(j):
        return dot(hid_ref[rows,pl.ds(mul(j*256,256),256)], wo[j//2,j%2].reshape(256,D))
    out_ref[rows,:]=base_ref[rows,:]+part(0)
    @pl.loop(1, FF//256)
    def _(j):
        out_ref[rows,:]+=part(j)

def gated_backward(gb_ref, wo, gu_ref, start, stop, first=0, count=ROWS, tile=256):
    rows=pl.ds(first,count)
    @pl.loop(start, stop)
    def _(j):
        lo=pl.ds(mul(j*tile,tile),tile); hi=pl.ds(mul(FF+j*tile,tile),tile)
        dh=dot(gb_ref[rows,:], wo[j//2,j%2].reshape(256,D), NT)
        gate=gu_ref[rows,lo].astype(F32); up=gu_ref[rows,hi].astype(F32)
        sq=gate*gate
        t=jnp.tanh(C0*(gate+C1*gate*sq))
        h=0.5*(1.0+t)
        slope=h+0.5*gate*(1.0-t*t)*(C0+(3*C0*C1)*sq)
        gu_ref[rows,lo]=(dh*up*slope).astype(BF)
        gu_ref[rows,hi]=(dh*(gate*h)).astype(BF)

def half_rows(nT_ref, c):
    return jnp.concatenate([nT_ref[pl.ds(mul((2*j+c)*48,16),48),:] for j in range(8)],axis=0)


MESH = pl.DeviceIdType.MESH
BIG = 1152

PARTS = {
    "q0": ("attn", 0, "wide", QKV, 1152), "q1": ("attn", 1152, "wide", QKV + 1152, 1152), "o": ("attn", 3 * D, "wide", OP, D),
    "g0": ("in", 0, "wide", WIN, 1024), "u0": ("in", FF, "wide", WIN + FF, 1024),
    "g1": ("in", 1024, "wide", WIN + 1024, 1024), "u1": ("in", FF + 1024, "wide", WIN + FF + 1024, 1024),
    "x0": ("extra", 0, "wide", XA, D), "x1": ("extra", D, "wide", XB, D),
    "k0": (None, 0, "wide", KV, D), "k1": (None, D, "wide", KV + D, D),
    "d0": ("out", 0, "tall", 0, 256), "d1": ("out", 256, "tall", 256, 256), "d2": ("out", 512, "tall", 512, 256),
}
PART_NAMES = tuple(PARTS)
ROUTES = (
    (("q0", "q1", "o", "g0", "u0", "g1", "u1", "d2"), {0: "d0", 2: "d1"}),
    (("q0", "q1", "o", "x0", "x1", "k0", "k1", "g0", "u0", "g1", "u1"), {0: "d0", 3: "d1", 6: "d2"}),
)
SUMS = {
    "out0": ("tall", 0, 384), "out1": ("tall", 384, 384),
    "in0": ("wide", WIN, 1024), "in1": ("wide", WIN + 1024, 1024),
    "in2": ("wide", WIN + FF, 1024), "in3": ("wide", WIN + FF + 1024, 1024),
    "x0": ("wide", XA, D), "x1": ("wide", XB, D),
    "k0": ("wide", KV, D), "k1": ("wide", KV + D, D),
    "o": ("wide", OP, D),
    "q0": ("wide", QKV, D), "q1": ("wide", QKV + D, D), "q2": ("wide", QKV + 2 * D, 384), "q3": ("wide", QKV + 2 * D + 384, 384),
}
SUM_NAMES = tuple(SUMS)
PAIRED = ()
OUT_OF = {
    "out0": ("out", 0), "out1": ("out", 384), "in0": ("in", 0), "in1": ("in", 1024), "in2": ("in", FF), "in3": ("in", FF + 1024),
    "x0": ("extra", 0), "x1": ("extra", D), "o": ("attn", 3 * D),
    "q0": ("attn", 0), "q1": ("attn", D), "q2": ("attn", 2 * D), "q3": ("attn", 2 * D + 384),
}
FREE = {"out": 0, "in": 1, "x": 2, "k": 3, "o": 4, "q": 5}


def scratch_list():
    V, DMA, REG = pltpu.VMEM, pltpu.SemaphoreType.DMA, pltpu.SemaphoreType.REGULAR
    n, s = len(PARTS), len(SUMS)
    return dict(
        wide=V((4, 2, 2, 48, WIDE), BF), tall=V((4, 2, 2, 128, D), BF),
        y_wide=V((4, 48, WIDE), BF), y_tall=V((4, 128, D), BF), pair_in=V((3, 2, 48, D), BF),
        stage=V((2, 4, 2, 48, 1024), BF), stage_tall=V((4, 2, 128, D), BF),
        fin=V((2, 48, 1024), F32), fin_tall=V((2, 128, 384), F32),
        x=V((ROWS, D), F32), mid=V((ROWS, D), F32), late=V((ROWS, D), F32), g=V((ROWS, D), F32), acc=V((ROWS, D), F32),
        n1=V((ROWS, D), BF), n2=V((ROWS, D), BF), n3=V((ROWS, D), BF), xin=V((ROWS, D), BF), nT=V((D, ROWS), BF),
        qkv=V((ROWS, 3 * D), BF), ao=V((ROWS, D), BF), aoT=V((D, ROWS), BF),
        xq=V((ROWS, D), BF), kv=V((ROWS, 2 * D), BF), cm=V((ROWS, D), BF), cmT=V((D, ROWS), BF),
        gu=V((ROWS, 2 * FF), BF), hid=V((ROWS, FF), BF), gb=V((ROWS, D), BF), gb2=V((ROWS, D), BF),
        mask=V((MICRO, SEQ, SEQ), BF), xsend=V((ROWS, D), BF),
        gz=V((4, 8, D), F32), gy=V((2, 8, D), F32), gc=V((2, 8, D), F32), gain=V((8, D), F32),
        dgain=V((8, D), F32), hz=V((4, 8, D), F32), hy=V((2, 8, D), F32), hc=V((2, 8, D), F32),
        s_in=DMA((3,)), s_own=DMA((n,)), s_kx=DMA, s_kr=DMA,
        s_rs=DMA((n, 3)), s_rr=DMA((n, 3)), s_ls=DMA((n, 3)), s_lr=DMA((n, 3)),
        s_ys=DMA((n, 4)), s_yr=DMA((n, 4)), s_cs=DMA((n,)), s_cr=DMA((n,)),
        s_ms=DMA((MICRO,)), s_mr=DMA((MICRO,)), s_gs=DMA((2, 5)), s_gr=DMA((2, 5)),
        t_cs=DMA((s,)), t_cr=DMA((s,)), t_ys=DMA((s,)), t_yr=DMA((s,)),
        t_rs=DMA((s,)), t_rr=DMA((s,)), t_ls=DMA((s,)), t_lr=DMA((s,)),
        t_xs=DMA((2,)), t_xr=DMA((2,)), t_out=DMA((s,)), s_out=DMA((3,)),
        free=REG((len(FREE),)), free_r=REG((s,)), free_l=REG((s,)),
    )


def whole_kernel(*refs):
    (acts_h, cot_h, attn_h, extra_h, in_h, out_h, gain_in, seg_in) = refs[:8]
    (res_o, grad_o, attn_o, extra_o, gin_o, gout_o, gain_o) = refs[8:15]
    R = type("Refs", (), {})()
    for name, ref in zip(scratch_list(), refs[15:]):
        setattr(R, name, ref)
    src = {"attn": attn_h, "extra": extra_h, "in": in_h, "out": out_h}
    dst = {"attn": attn_o, "extra": extra_o, "in": gin_o, "out": gout_o}
    buf = {"wide": R.wide, "tall": R.tall}
    ybuf = {"wide": R.y_wide, "tall": R.y_tall}

    section = lax.axis_index("section")
    me = lax.axis_index("dp")
    z, y, c = me // 4, (me // 2) % 2, me % 2
    first, second = section == 0, section == 1
    at = lambda zz, yy, cc: {"dp": zz * 4 + yy * 2 + cc}
    right, left = at(lax.rem(z + 1, 4), y, c), at(lax.rem(z + 3, 4), y, c)
    z_peer = [at(lax.rem(z + k, 4), y, c) for k in (1, 2, 3)]
    y_peer, c_peer, x_peer = at(z, 1 - y, c), at(z, y, 1 - c), {"section": 1 - section}

    def remote(a, b, ss, rs, dev):
        return pltpu.make_async_remote_copy(a, b, ss, rs, device_id=dev, device_id_type=MESH)

    def local(a, b, s):
        return pltpu.make_async_copy(a, b, s)

    def when(cond, fn):
        pl.when(cond)(fn)

    barrier = pltpu.get_barrier_semaphore()
    everyone = z_peer + [y_peer, c_peer, x_peer]
    for peer in everyone:
        pl.semaphore_signal(barrier, inc=1, device_id=peer, device_id_type=MESH)
    pl.semaphore_wait(barrier, len(everyone))

    def spot(name):
        arg, lo, b, col, size = PARTS[name]
        return PART_NAMES.index(name), buf[b], pl.ds(col, size)

    def in_place(name):
        i, b, cs = spot(name)
        return b.at[z, y, c, :, cs]

    def shard(name):
        arg, lo, _, _, size = PARTS[name]
        return in_place(name) if arg is None else src[arg].at[:, pl.ds(lo, size)]

    def own_copy(name):
        return local(shard(name), in_place(name), R.s_own.at[PART_NAMES.index(name)])

    def line_block(name, zz, pair):
        i, b, cs = spot(name)
        return b.at[zz, :, c, :, cs] if pair else b.at[zz, y, c, :, cs]

    def go_right(name, s, pair):
        i = PART_NAMES.index(name)
        d = line_block(name, z - s, pair)
        return remote(shard(name) if s == 0 and not pair else d, d, R.s_rs.at[i, s], R.s_rr.at[i, s], right)

    def go_left(name, s, pair):
        i = PART_NAMES.index(name)
        d = line_block(name, z + s, pair)
        return remote(shard(name) if s == 0 and not pair else d, d, R.s_ls.at[i, s], R.s_lr.at[i, s], left)

    def from_left(name, s, pair):
        i = PART_NAMES.index(name)
        d = line_block(name, z - s, pair)
        return remote(d, d, R.s_rs.at[i, s - 1], R.s_rr.at[i, s - 1], left)

    def from_right(name, s, pair):
        i = PART_NAMES.index(name)
        d = line_block(name, z + s, pair)
        return remote(d, d, R.s_ls.at[i, s - 1], R.s_lr.at[i, s - 1], right)

    def across(name, zz, own=False, pair=False):
        i, b, cs = spot(name)
        d = b.at[zz, y, c, :, cs]
        k = 0 if pair else zz
        return remote(shard(name) if own else d, d, R.s_ys.at[i, k], R.s_yr.at[i, k], y_peer)

    def across_in(name, zz, pair=False):
        i, b, cs = spot(name)
        d = b.at[zz, 1 - y, c, :, cs]
        k = 0 if pair else zz
        return remote(d, d, R.s_ys.at[i, k], R.s_yr.at[i, k], y_peer)

    def to_core(name):
        i, b, cs = spot(name)
        d = b.at[:, :, c, :, cs]
        return remote(d, d, R.s_cs.at[i], R.s_cr.at[i], c_peer)

    def core_in(name):
        i, b, cs = spot(name)
        d = b.at[:, :, 1 - c, :, cs]
        return remote(d, d, R.s_cs.at[i], R.s_cr.at[i], c_peer)

    def ends(s, go, cond=None):
        when((z >= s) & (z < 3), lambda: go(0))
        when((z + s <= 3) & (z > 0), lambda: go(1))

    def begin(name, pair):
        if PARTS[name][0] is not None:
            own_copy(name).start()
        if name == "k0":
            kv_shard.wait_recv()
        if not pair:
            when(z < 3, lambda: go_right(name, 0, False).start())
            when(z > 0, lambda: go_left(name, 0, False).start())
        across(name, z, True, pair).start()

    def pair_turn(name):
        own_copy(name).wait()
        across_in(name, z, True).wait_recv()
        when(z < 3, lambda: go_right(name, 0, True).start())
        when(z > 0, lambda: go_left(name, 0, True).start())

    def hop(name, s, pair):
        def lower():
            from_left(name, s, pair).wait_recv()
            if s < 3:
                when(z < 3, lambda: go_right(name, s, pair).start())
            if not pair:
                across(name, z - s).start()

        def upper():
            from_right(name, s, pair).wait_recv()
            if s < 3:
                when(z > 0, lambda: go_left(name, s, pair).start())
            if not pair:
                across(name, z + s).start()

        when(z >= s, lower)
        when(z + s <= 3, upper)

    def line_done(name, pair):
        if not pair:
            if PARTS[name][0] is not None:
                own_copy(name).wait()
            for zz in range(4):
                across_in(name, zz).wait_recv()
        to_core(name).start()

    def have(*names):
        for name in names:
            core_in(name).wait_recv()

    def sent(name, pair):
        for s in range(3):
            when((z >= s) & (z < 3), lambda: go_right(name, s, pair).wait_send())
            when((z + s <= 3) & (z > 0), lambda: go_left(name, s, pair).wait_send())
        for zz in range(1 if pair else 4):
            across(name, zz, False, pair).wait_send()
        to_core(name).wait_send()

    def all_sent(who):
        line, pairs = ROUTES[who]
        for name in line:
            sent(name, False)
        for name in pairs.values():
            sent(name, True)

    def section_tick(who, t):
        line, pairs = ROUTES[who]
        n = len(line)
        for start, name in pairs.items():
            if t == start:
                begin(name, True)
            if t == start + 1:
                pair_turn(name)
            for s in (1, 2, 3):
                if t == start + 1 + s:
                    hop(name, s, True)
            if t == start + 5:
                line_done(name, True)
        if t < n:
            begin(line[t], False)
        for s in (1, 2, 3):
            if 0 <= t - s < n:
                hop(line[t - s], s, False)
        if 0 <= t - 4 < n:
            line_done(line[t - 4], False)

    def tick(t):
        when(first, lambda: section_tick(0, t))
        when(second, lambda: section_tick(1, t))

    kv_block = R.wide.at[z, y, c, :, pl.ds(KV, 2 * D)]
    kv_shard = remote(extra_h, kv_block, R.s_kx, R.s_kr, x_peer)
    when(first, lambda: kv_shard.start())

    gain_own = local(gain_in, R.gz.at[z], R.s_in.at[0])
    gain_own.start()
    x_in = local(acts_h, R.x, R.s_in.at[1])
    x_in.start()
    g_in = local(cot_h, R.g, R.s_in.at[2])
    g_in.start()

    def small_z(own_ref, slots, row):
        return [remote(own_ref, slots.at[z], R.s_gs.at[row, k], R.s_gr.at[row, k], z_peer[k]) for k in range(3)]

    def small_pair(slots, row, k, dev):
        return remote(slots.at[0], slots.at[1], R.s_gs.at[row, k], R.s_gr.at[row, k], dev)

    gzc = small_z(gain_in, R.gz, 0)
    for q in gzc:
        q.start()
    tick(0)
    tick(1)
    gain_own.wait()
    for q in gzc:
        q.wait_recv()
    R.gy[0] = (R.gz[0] + R.gz[1]) + (R.gz[2] + R.gz[3])
    q = small_pair(R.gy, 0, 3, y_peer)
    q.start()
    tick(2)
    q.wait()
    R.gc[0] = R.gy[0] + R.gy[1]
    q = small_pair(R.gc, 0, 4, c_peer)
    q.start()
    tick(3)
    q.wait()
    R.gain[...] = R.gc[0] + R.gc[1]
    for q in gzc:
        q.wait_send()
    gain = lambda k: R.gain[k : k + 1, :]

    ones = jnp.where(first, 1.0, 0.0)
    for img in range(MICRO):
        row = jnp.broadcast_to(seg_in[img : img + 1, :].astype(F32), (SEQ, SEQ))
        key = lax.broadcasted_iota(jnp.int32, (SEQ, SEQ), 0)
        query = lax.broadcasted_iota(jnp.int32, (SEQ, SEQ), 1)
        allowed = jnp.where((row.T == row) & (key <= query), 1.0, ones)
        R.mask[img] = allowed.astype(BF)
    R.dgain[...] = jnp.zeros_like(R.dgain)

    x_in.wait()
    norm_forward(R.x, gain(0), R.n1)
    for t in range(4, 6):
        tick(t)
    have("q0", "q1")
    project(R.n1, R.wide, QKV, R.qkv, 0, 3 * D, 768)
    tick(6)

    def self_attention(a, b):
        attend_forward(R.qkv, 0, R.qkv, D, R.qkv, 2 * D, R.ao, R.aoT, R.mask, a, b)

    self_attention(0, 4)
    tick(7)
    self_attention(4, 8)
    tick(8)
    self_attention(8, 12)
    tick(9)
    have("o")
    project_add(R.ao, R.wide, OP, R.x, R.mid, 384)

    def message(img):
        rows = pl.ds(img * SEQ, SEQ)
        return remote(R.xsend.at[rows], R.xin.at[rows], R.s_ms.at[img], R.s_mr.at[img], x_peer)

    def down(base, out, cols):
        for lo in cols:
            cs = pl.ds(lo, 256)
            out[:, cs] = base[:, cs] + dot(R.hid[...], R.tall[:, :, :, :, cs].reshape(FF, 256))

    def enc_forward():
        norm_forward(R.mid, gain(1), R.n2)
        have("g0", "u0")
        gated_forward(R.n2, R.wide, R.gu, R.hid, 0, 2)
        section_tick(0, 10)
        gated_forward(R.n2, R.wide, R.gu, R.hid, 2, 4)
        have("g1", "u1")
        section_tick(0, 11)
        gated_forward(R.n2, R.wide, R.gu, R.hid, 4, 8)
        have("d0", "d1")
        down(R.mid, R.late, (0, 256))
        have("d2")
        down(R.mid, R.late, (512,))
        for img in range(MICRO):
            norm_forward(R.late, gain(2), R.xsend, img * SEQ, SEQ)
            message(img).start()
        all_sent(0)
        kv_shard.wait_send()

    def dec_forward():
        norm_forward(R.mid, gain(2), R.n3)
        section_tick(1, 10)
        have("x0")
        project(R.n3, R.wide, XA, R.xq, 0, D, 384)
        for t in (11, 12, 13, 14):
            section_tick(1, t)
        have("x1", "k0", "k1")
        all_sent(1)
        for img in range(MICRO):
            message(img).wait_recv()
            project(R.xin, R.wide, KV, R.kv, 0, 2 * D, 768, img * SEQ, SEQ)
            attend_forward(R.xq, 0, R.kv, 0, R.kv, D, R.cm, R.cmT, None, img * 6, img * 6 + 6)
        project_add(R.cm, R.wide, XB, R.mid, R.late, 384)
        norm_forward(R.late, gain(1), R.n2)
        have("g0", "u0", "g1", "u1")
        gated_forward(R.n2, R.wide, R.gu, R.hid, 0, 8)
        have("d0", "d1", "d2")


    def sum_spot(name):
        b, lo, size = SUMS[name]
        return SUM_NAMES.index(name), b, pl.ds(lo, size), size

    stage_of = {}

    def core_copy(name):
        k, b, cs, size = sum_spot(name)
        if b == "tall":
            s = R.stage_tall.at[:, :, :, cs]
        else:
            s = R.stage.at[stage_of[name], :, :, :, pl.ds(0, size)]
        return remote(s, buf[b].at[:, :, c, :, cs], R.t_cs.at[k], R.t_cr.at[k], c_peer)

    def paired(name):
        return name in PAIRED

    def y_copy(name):
        k, b, cs, size = sum_spot(name)
        if paired(name):
            return remote(buf[b].at[z, 1 - y, c, :, cs], ybuf[b].at[0, :, cs], R.t_ys.at[k], R.t_yr.at[k], y_peer)
        return remote(buf[b].at[:, 1 - y, c, :, cs], ybuf[b].at[:, :, cs], R.t_ys.at[k], R.t_yr.at[k], y_peer)

    def moving(name, a, e):
        _, b, cs, _ = sum_spot(name)
        return buf[b].at[a:e, :, c, :, cs] if paired(name) else buf[b].at[a:e, y, c, :, cs]

    def landing_left(name, a, e):
        _, b, cs, _ = sum_spot(name)
        return buf[b].at[a:e, :, 1 - c, :, cs] if paired(name) else buf[b].at[a:e, 0, 1 - c, :, cs]

    def landing_right(name, a, e):
        _, b, cs, size = sum_spot(name)
        if paired(name):
            return R.pair_in.at[a:e, :, :, pl.ds(SUMS[name][1] - XA, size)]
        return buf[b].at[a:e, 1, 1 - c, :, cs]

    def right_copy(name, zz):
        k = SUM_NAMES.index(name)
        return remote(moving(name, zz + 1, 4), landing_left(name, zz + 1, 4), R.t_rs.at[k], R.t_rr.at[k], right)

    def left_copy(name, zz):
        k = SUM_NAMES.index(name)
        return remote(moving(name, 0, zz), landing_right(name, 0, zz), R.t_ls.at[k], R.t_lr.at[k], left)

    def send_right(name, zz):
        pl.semaphore_wait(R.free_r.at[SUM_NAMES.index(name)], 1)
        right_copy(name, zz).start()

    def send_left(name, zz):
        pl.semaphore_wait(R.free_l.at[SUM_NAMES.index(name)], 1)
        left_copy(name, zz).start()

    def add_blocks(name, landed, a, e):
        mine = moving(name, a, e)

        @pl.loop(0, e - a)
        def _(j):
            mine[j] = (mine[j].astype(F32) + landed[j].astype(F32)).astype(BF)

    def add_left(name, zz):
        k = SUM_NAMES.index(name)
        d = landing_left(name, zz, 4)
        remote(d, d, R.t_rs.at[k], R.t_rr.at[k], left).wait_recv()
        add_blocks(name, d, zz, 4)

    def add_right(name, zz):
        k = SUM_NAMES.index(name)
        d = landing_right(name, 0, zz + 1)
        remote(d, d, R.t_ls.at[k], R.t_lr.at[k], right).wait_recv()
        add_blocks(name, d, 0, zz + 1)

    def open_line(name):
        k = SUM_NAMES.index(name)
        when(z > 0, lambda: pl.semaphore_signal(R.free_r.at[k], inc=1, device_id=left, device_id_type=MESH))
        when(z < 3, lambda: pl.semaphore_signal(R.free_l.at[k], inc=1, device_id=right, device_id_type=MESH))

    def line_a(name):
        when(z == 0, lambda: send_right(name, 0))
        when(z == 3, lambda: send_left(name, 3))

    def line_b(name):
        def one():
            add_left(name, 1)
            send_right(name, 1)

        def two():
            add_right(name, 2)
            send_left(name, 2)

        when(z == 1, one)
        when(z == 2, two)

    def line_c(name):
        def one():
            add_right(name, 1)
            send_left(name, 1)

        def two():
            add_left(name, 2)
            send_right(name, 2)

        when(z == 1, one)
        when(z == 2, two)

    def line_d(name):
        when(z == 0, lambda: add_right(name, 0))
        when(z == 3, lambda: add_left(name, 3))

    def line_sent(name):
        for zz in range(3):
            when(z == zz, lambda: right_copy(name, zz).wait_send())
            when(z == zz + 1, lambda: left_copy(name, zz + 1).wait_send())

    def release(name):
        pl.semaphore_signal(R.free.at[FREE[name]], inc=1, device_id=c_peer, device_id_type=MESH)

    def claim(name):
        pl.semaphore_wait(R.free.at[FREE[name]], 1)

    order = []

    def grad_wide(name, nT, g_ref, gcol, tile):
        k, b, cs, size = sum_spot(name)
        lo = SUMS[name][1]
        slot = len(order) % 2
        if len(order) >= 2:
            core_copy(order[-2]).wait_send()
        stage_of[name] = slot
        order.append(name)
        lhs = half_rows(nT, 1 - c)

        @pl.loop(0, size // tile)
        def _(j):
            w = dot(lhs, g_ref[:, pl.ds(mul(gcol + j * tile, 128), tile)]).astype(BF)
            R.stage[slot, :, :, :, pl.ds(mul(j * tile, 128), tile)] = w.reshape(4, 2, 48, tile)

        core_copy(name).start()
        mine = half_rows(nT, c)

        @pl.loop(0, size // tile)
        def _(j):
            w = dot(mine, g_ref[:, pl.ds(mul(gcol + j * tile, 128), tile)]).astype(BF)
            R.wide[:, :, c, :, pl.ds(mul(lo + j * tile, 128), tile)] = w.reshape(4, 2, 48, tile)

    def drain():
        for name in order[-2:]:
            core_copy(name).wait_send()
        order.clear()

    def grad_tall():
        def rows_of(j, cc):
            units = pl.ds(mul((2 * j + cc) * 128, 128), 128)
            return dot(R.hid[:, units].T, R.gb[...]).astype(BF)

        @pl.loop(0, 8)
        def _(j):
            R.stage_tall[j // 2, j % 2] = rows_of(j, 1 - c)

        core_copy("out0").start()
        core_copy("out1").start()

        @pl.loop(0, 8)
        def _(j):
            R.tall[j // 2, j % 2, c] = rows_of(j, c)

    ready, crossing, moving_on, finished = [], [], [], []

    def feed():
        while ready and len(crossing) < 2:
            name = ready.pop(0)
            y_copy(name).start()
            crossing.append(name)

    def core_stage(name, pass_on=True):
        k, b, cs, size = sum_spot(name)
        w = buf[b]
        landed = w.at[:, :, 1 - c, :, cs]
        remote(landed, landed, R.t_cs.at[k], R.t_cr.at[k], c_peer).wait_recv()

        @pl.loop(0, 8)
        def _(j):
            own = w[j // 2, j % 2, c, :, cs].astype(F32)
            w[j // 2, j % 2, c, :, cs] = (own + w[j // 2, j % 2, 1 - c, :, cs].astype(F32)).astype(BF)

        if pass_on:
            enter(name)

    def enter(name):
        open_line(name)
        if paired(name):
            line_a(name)
            moving_on.append([name, line_b, line_c, line_d, late_cross])
        else:
            ready.append(name)
            feed()

    def late_cross(name):
        y_copy(name).start()
        crossing.append(name)

    def y_stage(name):
        k, b, cs, size = sum_spot(name)
        w, r = buf[b], ybuf[b]
        if paired(name):
            d = r.at[0, :, cs]
            remote(d, d, R.t_ys.at[k], R.t_yr.at[k], y_peer).wait_recv()
            finish(name, w[z, y, c, :, cs].astype(F32) + r[0, :, cs].astype(F32))
            return
        y_copy(name).wait_recv()

        @pl.loop(0, 4)
        def _(j):
            w[j, y, c, :, cs] = (w[j, y, c, :, cs].astype(F32) + r[j, :, cs].astype(F32)).astype(BF)

        line_a(name)
        moving_on.append([name, line_b, line_c, line_d, last])

    def last(name):
        k, b, cs, size = sum_spot(name)
        finish(name, buf[b][z, y, c, :, cs].astype(F32))

    def turn():
        going = list(moving_on)
        if crossing:
            name = crossing.pop(0)
            y_stage(name)
            feed()
        for item in going:
            item.pop(1)(item[0])
            if len(item) == 1:
                moving_on.remove(item)

    def out_copy(name):
        k, b, cs, size = sum_spot(name)
        arg, lo = OUT_OF[name]
        kind = [f for f in finished if SUMS[f][0] == b]
        slot = kind.index(name) % 2
        f = R.fin_tall.at[slot] if b == "tall" else R.fin.at[slot, :, pl.ds(0, size)]
        return local(f, dst[arg].at[:, pl.ds(lo, size)], R.t_out.at[k])

    def finish(name, total):
        k, b, cs, size = sum_spot(name)
        kind = [f for f in finished if SUMS[f][0] == b]
        slot = len(kind) % 2
        if len(kind) >= 2:
            out_copy(kind[-2]).wait()
        finished.append(name)
        if b == "tall":
            R.fin_tall[slot] = total
        else:
            R.fin[slot, :, pl.ds(0, size)] = total
        out_copy(name).start()

    def over_copy(j):
        k, b, cs, size = sum_spot(("k0", "k1")[j])
        return remote(
            R.wide.at[:, :, c, :, cs], R.wide.at[:, :, c, :, pl.ds(XA + j * D, D)], R.t_xs.at[j], R.t_xr.at[j], x_peer
        )

    def round_g(to, first_row=0, count=ROWS):
        rows = pl.ds(first_row, count)
        to[rows, :] = R.g[rows, :].astype(BF)

    def project_back(g_ref, wcol, out_ref):
        out_ref[...] = dot(g_ref[...], wide_cols(R.wide, wcol, D), NT).astype(BF)

    def down_grads():
        release("out")
        claim("out")
        grad_tall()
        core_stage("out0")
        core_stage("out1")

    def in_grads():
        release("in")
        claim("in")
        grad_wide("in0", R.nT, R.gu, 0, 512)
        grad_wide("in1", R.nT, R.gu, 1024, 512)
        core_stage("in0")
        grad_wide("in2", R.nT, R.gu, FF, 512)
        core_stage("in1")
        grad_wide("in3", R.nT, R.gu, FF + 1024, 512)
        core_stage("in2")

    gains_own = lambda: small_pair(R.hc, 1, 4, c_peer)
    gains_row = lambda: small_pair(R.hy, 1, 3, y_peer)
    gains_line = lambda: small_z(R.gain, R.hz, 1)
    gain_copy = local(R.dgain, gain_o, R.s_out.at[2])
    grad_copy = local(R.g, grad_o, R.s_out.at[1])

    def gains_a():
        R.hc[0] = R.dgain[...]
        gains_own().start()

    def gains_b(_):
        gains_own().wait()
        R.hy[0] = R.hc[0] + R.hc[1]
        gains_row().start()

    def gains_c(_):
        gains_row().wait()
        R.gain[...] = R.hy[0] + R.hy[1]
        for q in gains_line():
            q.start()

    def gains_d(_):
        for q in gains_line():
            q.wait()
        R.hz[z] = R.gain[...]
        R.dgain[...] = (R.hz[0] + R.hz[1]) + (R.hz[2] + R.hz[3])
        gain_copy.start()

    g_in.wait()
    dec_res = local(R.acc, res_o, R.s_out.at[0])
    enc_res = local(R.late, res_o, R.s_out.at[0])

    def dec_middle():
        round_g(R.gb)
        gated_backward(R.gb, R.tall, R.gu, 0, 8)
        back_project(R.gu, 0, R.wide, WIN, 2 * FF, 512, R.acc)
        norm_backward(R.late, gain(1), R.acc, R.g, R.dgain, 1)
        round_g(R.gb2)
        project_back(R.gb2, XB, R.xsend)
        for img in range(MICRO):
            attend_backward(
                R.xq, 0, R.kv, 0, R.kv, D, R.xsend, None, R.xq, 0, R.kv, 0, R.kv, D, img * 6, img * 6 + 6
            )
            back_project(R.kv, 0, R.wide, KV, 2 * D, 768, R.acc, img * SEQ, SEQ)
            rows = pl.ds(img * SEQ, SEQ)
            R.xsend[rows, :] = R.acc[rows, :].astype(BF)
            message(img).start()
        down(R.late, R.acc, (0, 256, 512))
        dec_res.start()

    def dec_all():
        dec_forward()
        dec_middle()

    def enc_middle():
        enc_res.start()
        for img in range(MICRO):
            message(img).wait_send()
        for img in range(MICRO):
            lo = img * SEQ
            message(img).wait_recv()
            R.acc[pl.ds(lo, SEQ), :] = R.xin[pl.ds(lo, SEQ), :].astype(F32)
            norm_backward(R.late, gain(2), R.acc, R.g, R.dgain, 2, lo, SEQ)
            round_g(R.gb, lo, SEQ)
            gated_backward(R.gb, R.tall, R.gu, 0, 8, lo, SEQ)

    def enc_in():
        back_project(R.gu, 0, R.wide, WIN, 2 * FF, 512, R.acc)
        norm_backward(R.mid, gain(1), R.acc, R.g, R.dgain, 1)

    def dec_keys():
        release("k")
        transpose_to(R.xin, R.nT)
        claim("k")
        grad_wide("k0", R.nT, R.kv, 0, 384)
        grad_wide("k1", R.nT, R.kv, D, 384)
        core_stage("k0", False)
        over_copy(0).start()
        core_stage("k1", False)
        over_copy(1).start()
        drain()

    def dec_cross():
        dec_res.wait()
        back_project(R.xq, 0, R.wide, XA, D, 768, R.acc)
        release("x")
        transpose_to(R.n3, R.nT)
        claim("x")
        grad_wide("x0", R.nT, R.xq, 0, 384)
        grad_wide("x1", R.cmT, R.gb2, 0, 384)
        core_stage("x0", False)
        core_stage("x1", False)
        norm_backward(R.mid, gain(2), R.acc, R.g, R.dgain, 2)
        for img in range(MICRO):
            message(img).wait_send()
        drain()

    when(first, enc_forward)
    when(second, dec_all)
    when(first, enc_middle)
    down_grads()
    when(first, enc_in)
    when(second, dec_keys)
    transpose_to(R.n2, R.nT)
    in_grads()
    drain()
    core_stage("in3")
    when(second, dec_cross)

    round_g(R.gb2)
    project_back(R.gb2, OP, R.ao)
    release("o")
    claim("o")
    grad_wide("o", R.aoT, R.gb2, 0, 384)
    turn()
    attend_backward(R.qkv, 0, R.qkv, D, R.qkv, 2 * D, R.ao, R.mask, R.qkv, 0, R.qkv, D, R.qkv, 2 * D, 0, 6)
    core_stage("o")
    turn()
    attend_backward(R.qkv, 0, R.qkv, D, R.qkv, 2 * D, R.ao, R.mask, R.qkv, 0, R.qkv, D, R.qkv, 2 * D, 6, 12)
    turn()
    back_project(R.qkv, 0, R.wide, QKV, 3 * D, 768, R.acc)
    release("q")
    transpose_to(R.n1, R.nT)
    claim("q")
    for j in range(2):
        when(first, lambda: over_copy(j).wait_recv())
        enter(("x0", "x1")[j])
    grad_wide("q0", R.nT, R.qkv, 0, 384)
    grad_wide("q1", R.nT, R.qkv, D, 384)
    core_stage("q0")
    grad_wide("q2", R.nT, R.qkv, 2 * D, 384)
    core_stage("q1")
    grad_wide("q3", R.nT, R.qkv, 2 * D + 384, 384)
    core_stage("q2")
    core_stage("q3")
    turn()
    norm_backward(R.x, gain(0), R.acc, R.g, R.dgain, 0)
    grad_copy.start()
    gains_a()
    moving_on.append(["gains", gains_b, gains_c, gains_d])
    while ready or crossing or moving_on:
        turn()
    for name in ("out0", "out1"):
        core_copy(name).wait_send()
    drain()
    for name in finished:
        y_copy(name).wait_send()
        line_sent(name)
    for b in ("tall", "wide"):
        for name in [f for f in finished if SUMS[f][0] == b][-2:]:
            out_copy(name).wait()
    when(first, lambda: enc_res.wait())
    when(second, lambda: [over_copy(j).wait_send() for j in range(2)] and None)
    grad_copy.wait()
    gain_copy.wait()


def from_behind(block, axis, distance):
    devices = range(lax.axis_size(axis))
    route = [(i - distance, i) for i in devices if i - distance in devices]
    return lax.ppermute(block, axis, route)


def rms_norm(activations, gain_row):
    return (
        activations
        * lax.rsqrt(jnp.mean(activations * activations, axis=-1, keepdims=True) + 1e-06)
        * gain_row
    )


def product(left_side, right_side):
    return jnp.dot(left_side, right_side, preferred_element_type=jnp.float32)


def weight_grad(left_side, right_side):
    return jnp.einsum("sd,se->de", left_side, right_side, preferred_element_type=jnp.float32)


def input_back(gradient, weight):
    return jnp.einsum("se,de->sd", gradient, weight, preferred_element_type=jnp.float32)


def norm_back(activations, gain_row, gradient):
    _, pull_back = jax.vjp(rms_norm, activations, gain_row)
    return pull_back(gradient)


def heads_of(activations):
    return activations.reshape(activations.shape[0], HEADS, HDIM)


def logits_of(queries, keys_in, allowed):
    raw_logits = jnp.einsum(
        "qhd,khd->hqk", heads_of(queries), heads_of(keys_in), preferred_element_type=jnp.float32
    ) * HDIM ** (-0.5)
    if allowed is None:
        return raw_logits
    return jnp.where(allowed[None], raw_logits, -1e30)


def attend_plain(queries, keys_in, values, allowed):
    logits = logits_of(queries, keys_in, allowed)
    row_peak = jnp.max(logits, axis=-1, keepdims=True)
    weights = jnp.exp(logits - row_peak)
    row_total = jnp.sum(weights, axis=-1, keepdims=True)
    softmax_out = (weights / row_total).astype(jnp.bfloat16)
    mixed_heads = jnp.einsum(
        "hqk,khd->qhd", softmax_out, heads_of(values), preferred_element_type=jnp.float32
    )
    return (
        mixed_heads.reshape(queries.shape[0], D).astype(jnp.bfloat16),
        row_peak + jnp.log(row_total),
    )


def attend_plain_back(queries, keys_in, values, allowed, log_total, grad_mixed):
    softmax_out = jnp.exp(logits_of(queries, keys_in, allowed) - log_total)
    grad_heads = heads_of(grad_mixed)
    grad_softmax = jnp.einsum(
        "qhd,khd->hqk", grad_heads, heads_of(values), preferred_element_type=jnp.float32
    )
    grad_values = jnp.einsum(
        "hqk,qhd->khd",
        softmax_out.astype(jnp.bfloat16),
        grad_heads,
        preferred_element_type=jnp.float32,
    )
    inner_sum = jnp.sum(softmax_out * grad_softmax, axis=-1, keepdims=True)
    grad_logits = (softmax_out * (grad_softmax - inner_sum) * HDIM ** (-0.5)).astype(jnp.bfloat16)
    grad_queries = jnp.einsum(
        "hqk,khd->qhd", grad_logits, heads_of(keys_in), preferred_element_type=jnp.float32
    )
    grad_keys = jnp.einsum(
        "hqk,qhd->khd", grad_logits, heads_of(queries), preferred_element_type=jnp.float32
    )
    query_count = queries.shape[0]
    key_count = keys_in.shape[0]
    return (
        grad_queries.reshape(query_count, D),
        grad_keys.reshape(key_count, D),
        grad_values.reshape(key_count, D),
    )


def self_forward(inputs, gain_row, w_attn, allowed):
    normed = rms_norm(inputs, gain_row).astype(jnp.bfloat16)
    packed = product(normed, w_attn[:, : 3 * D]).astype(jnp.bfloat16)
    mixed_heads, log_total = attend_plain(
        packed[:, :D], packed[:, D : 2 * D], packed[:, 2 * D :], allowed
    )
    return (
        inputs + product(mixed_heads, w_attn[:, 3 * D :]),
        (normed, packed, mixed_heads, log_total),
    )


def self_backward(inputs, gain_row, w_attn, allowed, kept_values, grad_result):
    normed, packed, mixed_heads, log_total = kept_values
    grad_low = grad_result.astype(jnp.bfloat16)
    grad_proj = weight_grad(mixed_heads, grad_low)
    grad_mixed = input_back(grad_low, w_attn[:, 3 * D :]).astype(jnp.bfloat16)
    grad_queries, grad_keys, grad_values = attend_plain_back(
        packed[:, :D], packed[:, D : 2 * D], packed[:, 2 * D :], allowed, log_total, grad_mixed
    )
    grad_packed = jnp.concatenate([grad_queries, grad_keys, grad_values], axis=1).astype(
        jnp.bfloat16
    )
    grad_qkv = weight_grad(normed, grad_packed)
    grad_inputs, grad_gain = norm_back(
        inputs, gain_row, input_back(grad_packed, w_attn[:, : 3 * D])
    )
    return (grad_result + grad_inputs, grad_gain, jnp.concatenate([grad_qkv, grad_proj], axis=1))


def gated_unit(gated):
    return jax.nn.gelu(gated[:, :FF], approximate=True) * gated[:, FF:]


def ffn_forward(inputs, gain_row, w_in, w_out):
    normed = rms_norm(inputs, gain_row).astype(jnp.bfloat16)
    gated = product(normed, w_in)
    hidden = gated_unit(gated).astype(jnp.bfloat16)
    return (inputs + product(hidden, w_out), (normed, gated, hidden))


def ffn_backward(inputs, gain_row, w_in, w_out, kept_values, grad_result):
    normed, gated, hidden = kept_values
    grad_low = grad_result.astype(jnp.bfloat16)
    grad_wout = weight_grad(hidden, grad_low)
    _, pull_back = jax.vjp(gated_unit, gated)
    grad_gated = pull_back(input_back(grad_low, w_out))[0].astype(jnp.bfloat16)
    grad_win = weight_grad(normed, grad_gated)
    grad_inputs, grad_gain = norm_back(inputs, gain_row, input_back(grad_gated, w_in))
    return (grad_result + grad_inputs, grad_gain, grad_win, grad_wout)


def encoder_forward(inputs, weights):
    w_attn, w_extra, w_in, w_out, gain_rows = weights
    middle, first_kept = self_forward(inputs, gain_rows[0], w_attn, None)
    result, second_kept = ffn_forward(middle, gain_rows[1], w_in, w_out)
    normed = rms_norm(result, gain_rows[2]).astype(jnp.bfloat16)
    cross_kv = product(normed, w_extra).astype(jnp.bfloat16)
    return (result, cross_kv, (middle, first_kept, second_kept, normed))


def encoder_backward(inputs, weights, grad_result, grad_kv):
    w_attn, w_extra, w_in, w_out, gain_rows = weights
    result, _, kept_values = encoder_forward(inputs, weights)
    middle, first_kept, second_kept, normed = kept_values
    grad_extra = weight_grad(normed, grad_kv)
    grad_final, gain_final = norm_back(result, gain_rows[2], input_back(grad_kv, w_extra))
    grad_middle, gain_late, grad_win, grad_wout = ffn_backward(
        middle, gain_rows[1], w_in, w_out, second_kept, grad_result + grad_final
    )
    grad_inputs, gain_early, grad_attn = self_backward(
        inputs, gain_rows[0], w_attn, None, first_kept, grad_middle
    )
    return (
        grad_inputs,
        (
            grad_attn,
            grad_extra,
            grad_win,
            grad_wout,
            jnp.stack([gain_early, gain_late, gain_final]),
        ),
    )


def decoder_step(inputs, cross_kv, allowed, weights, grad_result):
    w_attn, w_extra, w_in, w_out, gain_rows = weights
    middle, first_kept = self_forward(inputs, gain_rows[0], w_attn, allowed)
    query_in = rms_norm(middle, gain_rows[2]).astype(jnp.bfloat16)
    queries = product(query_in, w_extra[:, :D]).astype(jnp.bfloat16)
    mixed_heads, log_total = attend_plain(queries, cross_kv[:, :D], cross_kv[:, D:], None)
    after_cross = middle + product(mixed_heads, w_extra[:, D:])
    result, second_kept = ffn_forward(after_cross, gain_rows[1], w_in, w_out)
    grad_after, gain_late, grad_win, grad_wout = ffn_backward(
        after_cross, gain_rows[1], w_in, w_out, second_kept, grad_result
    )
    grad_low = grad_after.astype(jnp.bfloat16)
    grad_cross_out = weight_grad(mixed_heads, grad_low)
    grad_mixed = input_back(grad_low, w_extra[:, D:]).astype(jnp.bfloat16)
    grad_queries, grad_keys, grad_values = attend_plain_back(
        queries, cross_kv[:, :D], cross_kv[:, D:], None, log_total, grad_mixed
    )
    grad_queries = grad_queries.astype(jnp.bfloat16)
    grad_cross_in = weight_grad(query_in, grad_queries)
    grad_normed, gain_cross = norm_back(
        middle, gain_rows[2], input_back(grad_queries, w_extra[:, :D])
    )
    grad_inputs, gain_early, grad_attn = self_backward(
        inputs, gain_rows[0], w_attn, allowed, first_kept, grad_after + grad_normed
    )
    grad_kv = jnp.concatenate([grad_keys, grad_values], axis=1).astype(jnp.bfloat16)
    gradients = (
        grad_attn,
        jnp.concatenate([grad_cross_in, grad_cross_out], axis=1),
        grad_win,
        grad_wout,
        jnp.stack([gain_early, gain_late, gain_cross]),
    )
    return (result, grad_inputs, grad_kv, gradients)


def general(acts, w_attn, w_extra, w_in, w_out, gains, segments, cotangent):
    gathered = (
        lax.all_gather(w_attn[0], "dp", axis=0, tiled=True),
        lax.all_gather(w_extra[0], "dp", axis=0, tiled=True),
        lax.all_gather(w_in[0], "dp", axis=0, tiled=True),
        lax.all_gather(w_out[0], "dp", axis=0, tiled=True),
        lax.all_gather(gains[0], "dp", axis=1, tiled=True),
    )
    weights = gathered[:4] + (gathered[4].astype(jnp.float32),)
    inputs = acts[0, :, 0]
    upstream = cotangent[0, :, 0]
    is_first = lax.axis_index("section") == 0
    positions = jnp.arange(SEQ)
    causal = positions[None, :] <= positions[:, None]
    zero_message = jnp.zeros((SEQ, 2 * D), jnp.bfloat16)
    zero_grads = tuple((jnp.zeros(weight.shape, jnp.float32) for weight in weights))
    carried = (jnp.zeros((MICRO, SEQ, D), jnp.float32), jnp.zeros((MICRO, SEQ, D), jnp.float32))
    received = zero_message
    returned = zero_message
    totals = zero_grads
    moments = MICRO + 2
    for moment in range(moments):

        def first_section(carried, received, returned):
            results, grad_inputs = carried
            message = zero_message
            fresh_grads = zero_grads
            if moment < MICRO:
                result, message, _ = encoder_forward(inputs[moment], weights)
                results = results.at[moment].set(result)
            if moment >= 2:
                grad_rows, fresh_grads = encoder_backward(
                    inputs[moment - 2], weights, upstream[moment - 2], returned
                )
                grad_inputs = grad_inputs.at[moment - 2].set(grad_rows)
            return ((results, grad_inputs), message, zero_message, fresh_grads)

        def second_section(carried, received, returned):
            results, grad_inputs = carried
            message = zero_message
            fresh_grads = zero_grads
            if 1 <= moment <= MICRO:
                segment_ids = segments[moment - 1, 0]
                allowed = (segment_ids[:, None] == segment_ids[None, :]) & causal
                result, grad_rows, message, fresh_grads = decoder_step(
                    inputs[moment - 1], received, allowed, weights, upstream[moment - 1]
                )
                results = results.at[moment - 1].set(result)
                grad_inputs = grad_inputs.at[moment - 1].set(grad_rows)
            return ((results, grad_inputs), zero_message, message, fresh_grads)

        carried, forward_message, back_message, fresh_grads = lax.cond(
            is_first, first_section, second_section, carried, received, returned
        )
        if moment < MICRO:
            received = from_behind(forward_message, "section", 1)
        if 1 <= moment <= MICRO:
            returned = from_behind(back_message, "section", -1)
        if moment >= 1:
            totals = tuple((jnp.add(*couple) for couple in zip(totals, fresh_grads)))
    results, grad_inputs = carried
    final = (
        lax.psum_scatter(totals[0], "dp", scatter_dimension=0, tiled=True),
        lax.psum_scatter(totals[1], "dp", scatter_dimension=0, tiled=True),
        lax.psum_scatter(totals[2], "dp", scatter_dimension=0, tiled=True),
        lax.psum_scatter(totals[3], "dp", scatter_dimension=0, tiled=True),
        lax.psum_scatter(totals[4], "dp", scatter_dimension=1, tiled=True),
    )
    return (
        results[None, :, None],
        grad_inputs[None, :, None],
        final[0][None],
        final[1][None],
        final[2][None],
        final[3][None],
        final[4][None],
    )


def step(acts, w_attn, w_extra, w_in, w_out, gains, segments, cotangent):
    me = lax.axis_index("dp")
    share = gains.shape[2]
    own_gain = lax.dynamic_update_slice(jnp.zeros((8, D), F32), gains[0].astype(F32), (0, me * share))
    anywhere = pl.BlockSpec(memory_space=pl.ANY)
    shape = lambda *s: jax.ShapeDtypeStruct(s, F32)
    scratch = scratch_list()
    results, input_grad, attn, extra, win, wout, gain = pl.pallas_call(
        whole_kernel,
        out_shape=(
            shape(ROWS, D), shape(ROWS, D), shape(48, 4 * D), shape(48, 2 * D), shape(48, 2 * FF), shape(128, D), shape(8, D),
        ),
        in_specs=[anywhere] * 7 + [pl.BlockSpec(memory_space=pltpu.VMEM)],
        out_specs=[anywhere] * 7,
        scratch_shapes=list(scratch.values()),
        compiler_params=pltpu.CompilerParams(
            collective_id=0, has_side_effects=True, vmem_limit_bytes=63 * 2**20
        ),
    )(
        acts.reshape(ROWS, D), cotangent.reshape(ROWS, D), w_attn[0], w_extra[0], w_in[0], w_out[0], own_gain,
        segments.reshape(MICRO, SEQ),
    )
    grad_gains = lax.dynamic_slice(gain, (0, me * share), (3, share))
    like = (1, MICRO, 1, SEQ, D)
    return (
        results.reshape(like), input_grad.reshape(like), attn[None], extra[None], win[None], wout[None], grad_gains[None],
    )


def solution(mesh):
    in_specs = (
        P("section", None, "dp", None, None),
        P("section", "dp", None),
        P("section", "dp", None),
        P("section", "dp", None),
        P("section", "dp", None),
        P("section", None, "dp"),
        P(None, "dp", None),
        P("section", None, "dp", None, None),
    )
    out_specs = (
        P("section", None, "dp", None, None),
        P("section", None, "dp", None, None),
        P("section", "dp", None),
        P("section", "dp", None),
        P("section", "dp", None),
        P("section", "dp", None),
        P("section", None, "dp"),
    )
    fits = mesh.shape["dp"] == 16
    return jax.shard_map(step if fits else general, mesh=mesh, in_specs=in_specs, out_specs=out_specs, check_vma=False)
```

```python
import jax
import jax.numpy as jnp
from jax import lax
from jax.experimental import pallas as pl
from jax.experimental.pallas import tpu as pltpu
from jax.sharding import PartitionSpec as P

D=768; HEADS=12; HDIM=64; FF=2048; SEQ=256; MICRO=2
ROWS=MICRO*SEQ
BF=jnp.bfloat16; F32=jnp.float32
QKV, OP, XA, XB, WIN, KV = 0, 3*D, 4*D, 5*D, 6*D, 6*D+2*FF
WIDE = KV + 2*D
NN=(((1,),(0,)),((),())); NT=(((1,),(1,)),((),()))

def mul(start, k): return pl.multiple_of(start, k)
def dot(a,b,dims=NN): return lax.dot_general(a,b,dims,preferred_element_type=F32)

def wide_cols(wa, start, size):
    return wa[:, :, :, :, pl.ds(start, size)].reshape(D, size)

def rms_rows(v):
    return lax.rsqrt(jnp.mean(v*v, axis=-1, keepdims=True) + 1e-6)

def norm_forward(v_ref, gain, n_ref, first=0, count=ROWS):
    @pl.loop(0, count//64)
    def _(i):
        rows=pl.ds(mul(first+i*64,64),64)
        v=v_ref[rows,:]
        n_ref[rows,:]=(v*rms_rows(v)*gain).astype(BF)

def norm_backward(v_ref, gain, dn_ref, g_ref, dgain_ref, slot, first=0, count=ROWS, low_ref=None):
    def body(i, acc):
        rows=pl.ds(mul(first+i*64,64),64)
        v=v_ref[rows,:]; dn=dn_ref[rows,:].astype(F32)
        r=rms_rows(v)
        t=dn*gain
        vr=v*r
        g=g_ref[rows,:]+r*(t-vr*jnp.mean(t*vr,axis=-1,keepdims=True))
        g_ref[rows,:]=g
        if low_ref is not None:
            low_ref[rows,:]=g.astype(BF)
        return acc+jnp.sum(dn*vr,axis=0,keepdims=True)
    acc=lax.fori_loop(0,count//64,body,jnp.zeros((1,D),F32))
    dgain_ref[slot:slot+1,:]+=acc

def transpose_to(src_ref, dst_ref, first=0, count=ROWS):
    cols=src_ref.shape[1]
    @pl.loop(0, cols//128)
    def _(j):
        cs=pl.ds(mul(j*128,128),128)
        dst_ref[cs, pl.ds(first,count)] = src_ref[pl.ds(first,count),cs].T

def project(n_ref, wa, wcol, out_ref, ocol, total, tile, first=0, count=ROWS):
    @pl.loop(0, total//tile)
    def _(j):
        w=wide_cols(wa, mul(wcol+j*tile,128), tile)
        out_ref[pl.ds(first,count), pl.ds(mul(ocol+j*tile,128),tile)] = dot(n_ref[pl.ds(first,count),:], w).astype(out_ref.dtype)

def project_add(a_ref, wa, wcol, base_ref, out_ref, tile, first=0, count=ROWS):
    rows=pl.ds(first,count)
    @pl.loop(0, D//tile)
    def _(j):
        w=wide_cols(wa, mul(wcol+j*tile,128), tile)
        cs=pl.ds(mul(j*tile,128),tile)
        out_ref[rows,cs] = base_ref[rows,cs]+dot(a_ref[rows,:], w)

def back_project(g_ref, gcol, wa, wcol, total, tile, acc_ref, first=0, count=ROWS, fresh=True):
    rows=pl.ds(first,count)
    def part(j):
        w=wide_cols(wa, mul(wcol+j*tile,128), tile)
        return dot(g_ref[rows, pl.ds(mul(gcol+j*tile,128),tile)], w, NT)
    if fresh:
        acc_ref[rows,:]=part(0)
    @pl.loop(1 if fresh else 0, total//tile)
    def _(j):
        acc_ref[rows,:]+=part(j)

def attend_forward(q_ref, qc, k_ref, kc, v_ref, vc, o_ref, oT_ref, mask_ref, start, stop, kept_ref=None):
    @pl.loop(start, stop)
    def _(i):
        img=i//6; p=i%6
        rows=pl.ds(mul(img*SEQ,SEQ),SEQ)
        def cols(base): return pl.ds(mul(base+p*128,128),128)
        q2=q_ref[rows,cols(qc)]*jnp.asarray(0.125,BF)
        k2=k_ref[rows,cols(kc)]
        vT=v_ref[rows,cols(vc)].T
        lane=lax.broadcasted_iota(jnp.int32,(SEQ,128),1)//64
        parts=[]
        for a in range(2):
            ka=jnp.where(lane==a,k2,jnp.zeros_like(k2))
            s=dot(ka,q2,NT)
            if mask_ref is not None:
                s=jnp.where(mask_ref[img].astype(F32)>0,s,-1e30)
            e=jnp.exp(s-jnp.max(s,axis=0,keepdims=True))
            w=(e*(1.0/jnp.sum(e,axis=0,keepdims=True))).astype(BF)
            if kept_ref is not None:
                kept_ref[i,a]=w
            parts.append(dot(vT[a*64:(a+1)*64],w))
        oT=jnp.concatenate(parts,axis=0).astype(BF)
        oT_ref[pl.ds(mul(p*128,128),128),rows]=oT
        o_ref[rows,cols(0)]=oT.T

def attend_backward(q_ref, qc, k_ref, kc, v_ref, vc, d_ref, mask_ref, dq_ref, dqc, dk_ref, dkc, dv_ref, dvc, start, stop, kept_ref=None):
    @pl.loop(start, stop)
    def _(i):
        img=i//6; p=i%6
        rows=pl.ds(mul(img*SEQ,SEQ),SEQ)
        def cols(base): return pl.ds(mul(base+p*128,128),128)
        q2=q_ref[rows,cols(qc)]
        qs=q2*jnp.asarray(0.125,BF)
        k2=k_ref[rows,cols(kc)]
        v2=v_ref[rows,cols(vc)]
        d2=d_ref[rows,cols(0)]
        kT=k2.T
        lane=lax.broadcasted_iota(jnp.int32,(SEQ,128),1)//64
        dqT=[]; dk=[]; dv=[]
        for a in range(2):
            mine=lane==a
            if kept_ref is not None:
                wb=kept_ref[i,a]
                w=wb.astype(F32)
            else:
                s=dot(jnp.where(mine,k2,jnp.zeros_like(k2)),qs,NT)
                if mask_ref is not None:
                    s=jnp.where(mask_ref[img].astype(F32)>0,s,-1e30)
                e=jnp.exp(s-jnp.max(s,axis=0,keepdims=True))
                w=e*(1.0/jnp.sum(e,axis=0,keepdims=True))
                wb=w.astype(BF)
            dw=dot(jnp.where(mine,v2,jnp.zeros_like(v2)),d2,NT)
            wd=w*dw
            ds=((wd-w*jnp.sum(wd,axis=0,keepdims=True))*0.125).astype(BF)
            dv.append(dot(wb,d2))
            dk.append(dot(ds,q2))
            dqT.append(dot(kT[a*64:(a+1)*64],ds))
        dq_ref[rows,cols(dqc)]=jnp.concatenate(dqT,axis=0).astype(BF).T
        dk_ref[rows,cols(dkc)]=jnp.where(lane==0,dk[0],dk[1]).astype(BF)
        dv_ref[rows,cols(dvc)]=jnp.where(lane==0,dv[0],dv[1]).astype(BF)

C0=0.7978845608028654; C1=0.044715
def gated_parts(n_ref, wa, j, rows, tile):
    gate=dot(n_ref[rows,:], wide_cols(wa, mul(WIN+j*tile,128), tile))
    up=dot(n_ref[rows,:], wide_cols(wa, mul(WIN+FF+j*tile,128), tile))
    sq=gate*gate
    t=jnp.tanh(gate*(C0+(C0*C1)*sq))
    h=0.5+0.5*t
    slope=h+(0.5*gate)*(1.0-t*t)*(C0+(3*C0*C1)*sq)
    return up, gate*h, slope

def gated_forward(n_ref, wa, gu_ref, hid_ref, start, stop, first=0, count=ROWS, tile=256):
    rows=pl.ds(first,count)
    @pl.loop(start, stop)
    def _(j):
        lo=pl.ds(mul(j*tile,tile),tile); hi=pl.ds(mul(FF+j*tile,tile),tile)
        up,act,slope=gated_parts(n_ref,wa,j,rows,tile)
        hid_ref[rows,lo]=(act*up).astype(BF)
        gu_ref[rows,lo]=(up*slope).astype(BF)
        gu_ref[rows,hi]=act.astype(BF)

def hidden_grad(gb_ref, wo, gu_ref, start, stop, tile=256):
    @pl.loop(start, stop)
    def _(j):
        gu_ref[:,pl.ds(mul(FF+j*tile,tile),tile)]=dot(gb_ref[...], wo[j//2,j%2].reshape(256,D), NT).astype(BF)

def gated_both(n_ref, wa, gu_ref, hid_ref, start, stop, tile=256):
    rows=pl.ds(0,ROWS)
    @pl.loop(start, stop)
    def _(j):
        lo=pl.ds(mul(j*tile,tile),tile); hi=pl.ds(mul(FF+j*tile,tile),tile)
        up,act,slope=gated_parts(n_ref,wa,j,rows,tile)
        hid_ref[rows,lo]=(act*up).astype(BF)
        dh=gu_ref[rows,hi].astype(F32)
        gu_ref[rows,lo]=(dh*up*slope).astype(BF)
        gu_ref[rows,hi]=(dh*act).astype(BF)

def gated_backward(gb_ref, wo, gu_ref, start, stop, first=0, count=ROWS, tile=256):
    rows=pl.ds(first,count)
    @pl.loop(start, stop)
    def _(j):
        lo=pl.ds(mul(j*tile,tile),tile); hi=pl.ds(mul(FF+j*tile,tile),tile)
        dh=dot(gb_ref[rows,:], wo[j//2,j%2].reshape(256,D), NT)
        gu_ref[rows,lo]=(dh*gu_ref[rows,lo].astype(F32)).astype(BF)
        gu_ref[rows,hi]=(dh*gu_ref[rows,hi].astype(F32)).astype(BF)

def half_rows(nT_ref, c):
    return jnp.concatenate([nT_ref[pl.ds(mul((2*j+c)*48,16),48),:] for j in range(8)],axis=0)


MESH = pl.DeviceIdType.MESH
BIG = 1152

PARTS = {
    "q0": ("attn", 0, "wide", QKV, 1152), "q1": ("attn", 1152, "wide", QKV + 1152, 1152), "o": ("attn", 3 * D, "wide", OP, D),
    "g0": ("in", 0, "wide", WIN, 1024), "u0": ("in", FF, "wide", WIN + FF, 1024),
    "g1": ("in", 1024, "wide", WIN + 1024, 1024), "u1": ("in", FF + 1024, "wide", WIN + FF + 1024, 1024),
    "x0": ("extra", 0, "wide", XA, D), "x1": ("extra", D, "wide", XB, D),
    "k0": (None, 0, "wide", KV, D), "k1": (None, D, "wide", KV + D, D),
    "d0": ("out", 0, "tall", 0, 256), "d1": ("out", 256, "tall", 256, 256), "d2": ("out", 512, "tall", 512, 256),
}
PART_NAMES = tuple(PARTS)
ROUTES = (
    (("q0", "q1", "o", "g0", "u0", "g1", "u1", "d2"), {0: "d0", 2: "d1"}),
    (("q0", "q1", "o", "x0", "x1", "k0", "k1", "g0", "u0", "g1", "u1"), {0: "d0", 3: "d1", 6: "d2"}),
)
SUMS = {
    "out0": ("tall", 0, 384), "out1": ("tall", 384, 384),
    "in0": ("wide", WIN, 1024), "in1": ("wide", WIN + 1024, 1024),
    "in2": ("wide", WIN + FF, 1024), "in3": ("wide", WIN + FF + 1024, 1024),
    "x0": ("wide", XA, D), "x1": ("wide", XB, D),
    "k0": ("wide", KV, D), "k1": ("wide", KV + D, D),
    "o": ("wide", OP, D),
    "q0": ("wide", QKV, D), "q1": ("wide", QKV + D, D), "q2": ("wide", QKV + 2 * D, 384), "q3": ("wide", QKV + 2 * D + 384, 384),
}
SUM_NAMES = tuple(SUMS)
PAIRED = ("out1",)
OUT_OF = {
    "out0": ("out", 0), "out1": ("out", 384), "in0": ("in", 0), "in1": ("in", 1024), "in2": ("in", FF), "in3": ("in", FF + 1024),
    "x0": ("extra", 0), "x1": ("extra", D), "o": ("attn", 3 * D),
    "q0": ("attn", 0), "q1": ("attn", D), "q2": ("attn", 2 * D), "q3": ("attn", 2 * D + 384),
}
FREE = {"out": 0, "in": 1, "x": 2, "k": 3, "o": 4, "q": 5}


def scratch_list():
    V, DMA, REG = pltpu.VMEM, pltpu.SemaphoreType.DMA, pltpu.SemaphoreType.REGULAR
    n, s = len(PARTS), len(SUMS)
    return dict(
        wide=V((4, 2, 2, 48, WIDE), BF), tall=V((4, 2, 2, 128, D), BF),
        y_wide=V((4, 48, WIDE), BF), y_tall=V((4, 128, D), BF), pair_in=V((1, 3, 2, 128, 384), BF),
        stage=V((2, 4, 2, 48, 1024), BF), stage_tall=V((4, 2, 128, D), BF),
        fin=V((2, 48, 1024), F32), fin_tall=V((2, 128, 384), F32),
        x=V((ROWS, D), F32), mid=V((ROWS, D), F32), late=V((ROWS, D), F32), g=V((ROWS, D), F32), acc=V((ROWS, D), F32),
        n1=V((ROWS, D), BF), n2=V((ROWS, D), BF), n3=V((ROWS, D), BF), xin=V((ROWS, D), BF), nT=V((D, ROWS), BF),
        qkv=V((ROWS, 3 * D), BF), ao=V((ROWS, D), BF), aoT=V((D, ROWS), BF),
        xq=V((ROWS, D), BF), kv=V((ROWS, 2 * D), BF), cm=V((ROWS, D), BF), cmT=V((D, ROWS), BF),
        gu=V((ROWS, 2 * FF), BF), hid=V((ROWS, FF), BF), hidT=V((FF, ROWS), BF), kept=V((12, 2, SEQ, SEQ), BF), gb=V((ROWS, D), BF), gb2=V((ROWS, D), BF),
        mask=V((MICRO, SEQ, SEQ), BF), xsend=V((ROWS, D), BF),
        gz=V((4, 8, D), F32), gy=V((2, 8, D), F32), gc=V((2, 8, D), F32), gain=V((8, D), F32),
        dgain=V((8, D), F32), hz=V((4, 8, D), F32), hy=V((2, 8, D), F32), hc=V((2, 8, D), F32),
        s_in=DMA((3,)), s_own=DMA((n,)), s_kx=DMA, s_kr=DMA,
        s_rs=DMA((n, 3)), s_rr=DMA((n, 3)), s_ls=DMA((n, 3)), s_lr=DMA((n, 3)),
        s_ys=DMA((n, 4)), s_yr=DMA((n, 4)), s_cs=DMA((n,)), s_cr=DMA((n,)),
        s_ms=DMA((MICRO,)), s_mr=DMA((MICRO,)), s_gs=DMA((2, 5)), s_gr=DMA((2, 5)),
        t_cs=DMA((s,)), t_cr=DMA((s,)), t_ys=DMA((s,)), t_yr=DMA((s,)),
        t_rs=DMA((s,)), t_rr=DMA((s,)), t_ls=DMA((s,)), t_lr=DMA((s,)),
        t_xs=DMA((2,)), t_xr=DMA((2,)), t_out=DMA((s,)), s_out=DMA((3,)),
        free=REG((len(FREE),)), free_r=REG((s,)), free_l=REG((s,)),
    )


def whole_kernel(*refs):
    (acts_h, cot_h, attn_h, extra_h, in_h, out_h, gain_in, seg_in) = refs[:8]
    (res_o, grad_o, attn_o, extra_o, gin_o, gout_o, gain_o) = refs[8:15]
    R = type("Refs", (), {})()
    for name, ref in zip(scratch_list(), refs[15:]):
        setattr(R, name, ref)
    src = {"attn": attn_h, "extra": extra_h, "in": in_h, "out": out_h}
    dst = {"attn": attn_o, "extra": extra_o, "in": gin_o, "out": gout_o}
    buf = {"wide": R.wide, "tall": R.tall}
    ybuf = {"wide": R.y_wide, "tall": R.y_tall}

    section = lax.axis_index("section")
    me = lax.axis_index("dp")
    z, y, c = me // 4, (me // 2) % 2, me % 2
    first, second = section == 0, section == 1
    at = lambda zz, yy, cc: {"dp": zz * 4 + yy * 2 + cc}
    right, left = at(lax.rem(z + 1, 4), y, c), at(lax.rem(z + 3, 4), y, c)
    z_peer = [at(lax.rem(z + k, 4), y, c) for k in (1, 2, 3)]
    y_peer, c_peer, x_peer = at(z, 1 - y, c), at(z, y, 1 - c), {"section": 1 - section}

    def remote(a, b, ss, rs, dev):
        return pltpu.make_async_remote_copy(a, b, ss, rs, device_id=dev, device_id_type=MESH)

    def local(a, b, s):
        return pltpu.make_async_copy(a, b, s)

    def when(cond, fn):
        pl.when(cond)(fn)

    barrier = pltpu.get_barrier_semaphore()
    everyone = z_peer + [y_peer, c_peer, x_peer]
    for peer in everyone:
        pl.semaphore_signal(barrier, inc=1, device_id=peer, device_id_type=MESH)
    pl.semaphore_wait(barrier, len(everyone))

    def spot(name):
        arg, lo, b, col, size = PARTS[name]
        return PART_NAMES.index(name), buf[b], pl.ds(col, size)

    def in_place(name):
        i, b, cs = spot(name)
        return b.at[z, y, c, :, cs]

    def shard(name):
        arg, lo, _, _, size = PARTS[name]
        return in_place(name) if arg is None else src[arg].at[:, pl.ds(lo, size)]

    def own_copy(name):
        return local(shard(name), in_place(name), R.s_own.at[PART_NAMES.index(name)])

    def line_block(name, zz, pair):
        i, b, cs = spot(name)
        return b.at[zz, :, c, :, cs] if pair else b.at[zz, y, c, :, cs]

    def go_right(name, s, pair):
        i = PART_NAMES.index(name)
        d = line_block(name, z - s, pair)
        return remote(shard(name) if s == 0 and not pair else d, d, R.s_rs.at[i, s], R.s_rr.at[i, s], right)

    def go_left(name, s, pair):
        i = PART_NAMES.index(name)
        d = line_block(name, z + s, pair)
        return remote(shard(name) if s == 0 and not pair else d, d, R.s_ls.at[i, s], R.s_lr.at[i, s], left)

    def from_left(name, s, pair):
        i = PART_NAMES.index(name)
        d = line_block(name, z - s, pair)
        return remote(d, d, R.s_rs.at[i, s - 1], R.s_rr.at[i, s - 1], left)

    def from_right(name, s, pair):
        i = PART_NAMES.index(name)
        d = line_block(name, z + s, pair)
        return remote(d, d, R.s_ls.at[i, s - 1], R.s_lr.at[i, s - 1], right)

    def across(name, zz, own=False, pair=False):
        i, b, cs = spot(name)
        d = b.at[zz, y, c, :, cs]
        k = 0 if pair else zz
        return remote(shard(name) if own else d, d, R.s_ys.at[i, k], R.s_yr.at[i, k], y_peer)

    def across_in(name, zz, pair=False):
        i, b, cs = spot(name)
        d = b.at[zz, 1 - y, c, :, cs]
        k = 0 if pair else zz
        return remote(d, d, R.s_ys.at[i, k], R.s_yr.at[i, k], y_peer)

    def to_core(name):
        i, b, cs = spot(name)
        d = b.at[:, :, c, :, cs]
        return remote(d, d, R.s_cs.at[i], R.s_cr.at[i], c_peer)

    def core_in(name):
        i, b, cs = spot(name)
        d = b.at[:, :, 1 - c, :, cs]
        return remote(d, d, R.s_cs.at[i], R.s_cr.at[i], c_peer)

    def ends(s, go, cond=None):
        when((z >= s) & (z < 3), lambda: go(0))
        when((z + s <= 3) & (z > 0), lambda: go(1))

    def begin(name, pair):
        if PARTS[name][0] is not None:
            own_copy(name).start()
        if name == "k0":
            kv_shard.wait_recv()
        if not pair:
            when(z < 3, lambda: go_right(name, 0, False).start())
            when(z > 0, lambda: go_left(name, 0, False).start())
        across(name, z, True, pair).start()

    def pair_turn(name):
        own_copy(name).wait()
        across_in(name, z, True).wait_recv()
        when(z < 3, lambda: go_right(name, 0, True).start())
        when(z > 0, lambda: go_left(name, 0, True).start())

    def hop(name, s, pair):
        def lower():
            from_left(name, s, pair).wait_recv()
            if s < 3:
                when(z < 3, lambda: go_right(name, s, pair).start())
            if not pair:
                across(name, z - s).start()

        def upper():
            from_right(name, s, pair).wait_recv()
            if s < 3:
                when(z > 0, lambda: go_left(name, s, pair).start())
            if not pair:
                across(name, z + s).start()

        when(z >= s, lower)
        when(z + s <= 3, upper)

    def line_done(name, pair):
        if not pair:
            if PARTS[name][0] is not None:
                own_copy(name).wait()
            for zz in range(4):
                across_in(name, zz).wait_recv()
        to_core(name).start()

    def have(*names):
        for name in names:
            core_in(name).wait_recv()

    def sent(name, pair):
        for s in range(3):
            when((z >= s) & (z < 3), lambda: go_right(name, s, pair).wait_send())
            when((z + s <= 3) & (z > 0), lambda: go_left(name, s, pair).wait_send())
        for zz in range(1 if pair else 4):
            across(name, zz, False, pair).wait_send()
        to_core(name).wait_send()

    def all_sent(who):
        line, pairs = ROUTES[who]
        for name in line:
            sent(name, False)
        for name in pairs.values():
            sent(name, True)

    def section_tick(who, t):
        line, pairs = ROUTES[who]
        n = len(line)
        for start, name in pairs.items():
            if t == start:
                begin(name, True)
            if t == start + 1:
                pair_turn(name)
            for s in (1, 2, 3):
                if t == start + 1 + s:
                    hop(name, s, True)
            if t == start + 5:
                line_done(name, True)
        if t < n:
            begin(line[t], False)
        for s in (1, 2, 3):
            if 0 <= t - s < n:
                hop(line[t - s], s, False)
        if 0 <= t - 4 < n:
            line_done(line[t - 4], False)

    def tick(t):
        when(first, lambda: section_tick(0, t))
        when(second, lambda: section_tick(1, t))

    kv_block = R.wide.at[z, y, c, :, pl.ds(KV, 2 * D)]
    kv_shard = remote(extra_h, kv_block, R.s_kx, R.s_kr, x_peer)
    when(first, lambda: kv_shard.start())

    gain_own = local(gain_in, R.gz.at[z], R.s_in.at[0])
    gain_own.start()
    x_in = local(acts_h, R.x, R.s_in.at[1])
    x_in.start()
    g_in = local(cot_h, R.g, R.s_in.at[2])
    g_in.start()

    def small_z(own_ref, slots, row):
        return [remote(own_ref, slots.at[z], R.s_gs.at[row, k], R.s_gr.at[row, k], z_peer[k]) for k in range(3)]

    def small_pair(slots, row, k, dev):
        return remote(slots.at[0], slots.at[1], R.s_gs.at[row, k], R.s_gr.at[row, k], dev)

    gzc = small_z(gain_in, R.gz, 0)
    for q in gzc:
        q.start()
    tick(0)
    tick(1)
    gain_own.wait()
    for q in gzc:
        q.wait_recv()
    R.gy[0] = (R.gz[0] + R.gz[1]) + (R.gz[2] + R.gz[3])
    q = small_pair(R.gy, 0, 3, y_peer)
    q.start()
    tick(2)
    q.wait()
    R.gc[0] = R.gy[0] + R.gy[1]
    q = small_pair(R.gc, 0, 4, c_peer)
    q.start()
    tick(3)
    q.wait()
    R.gain[...] = R.gc[0] + R.gc[1]
    for q in gzc:
        q.wait_send()
    gain = lambda k: R.gain[k : k + 1, :]

    ones = jnp.where(first, 1.0, 0.0)
    for img in range(MICRO):
        row = jnp.broadcast_to(seg_in[img : img + 1, :].astype(F32), (SEQ, SEQ))
        key = lax.broadcasted_iota(jnp.int32, (SEQ, SEQ), 0)
        query = lax.broadcasted_iota(jnp.int32, (SEQ, SEQ), 1)
        allowed = jnp.where((row.T == row) & (key <= query), 1.0, ones)
        R.mask[img] = allowed.astype(BF)
    R.dgain[...] = jnp.zeros_like(R.dgain)

    x_in.wait()
    norm_forward(R.x, gain(0), R.n1)
    for t in range(4, 6):
        tick(t)
    have("q0", "q1")
    project(R.n1, R.wide, QKV, R.qkv, 0, 3 * D, 768)
    tick(6)

    def self_attention(a, b):
        attend_forward(R.qkv, 0, R.qkv, D, R.qkv, 2 * D, R.ao, R.aoT, R.mask, a, b)

    self_attention(0, 4)
    tick(7)
    self_attention(4, 8)
    tick(8)
    self_attention(8, 12)
    tick(9)
    have("o")
    project_add(R.ao, R.wide, OP, R.x, R.mid, 384)

    def message(img):
        rows = pl.ds(img * SEQ, SEQ)
        return remote(R.xsend.at[rows], R.xin.at[rows], R.s_ms.at[img], R.s_mr.at[img], x_peer)

    def down(base, out, cols):
        for lo in cols:
            cs = pl.ds(lo, 256)
            out[:, cs] = base[:, cs] + dot(R.hid[...], R.tall[:, :, :, :, cs].reshape(FF, 256))

    def round_g(to, first_row=0, count=ROWS):
        rows = pl.ds(first_row, count)
        to[rows, :] = R.g[rows, :].astype(BF)

    def enc_forward():
        norm_forward(R.mid, gain(1), R.n2)
        have("g0", "u0")
        gated_forward(R.n2, R.wide, R.gu, R.hid, 0, 2)
        section_tick(0, 10)
        gated_forward(R.n2, R.wide, R.gu, R.hid, 2, 4)
        have("g1", "u1")
        section_tick(0, 11)
        gated_forward(R.n2, R.wide, R.gu, R.hid, 4, 8)
        have("d0", "d1")
        down(R.mid, R.late, (0, 256))
        have("d2")
        down(R.mid, R.late, (512,))
        for img in range(MICRO):
            norm_forward(R.late, gain(2), R.xsend, img * SEQ, SEQ)
            message(img).start()
        all_sent(0)
        kv_shard.wait_send()

    def dec_forward():
        norm_forward(R.mid, gain(2), R.n3)
        section_tick(1, 10)
        have("x0")
        project(R.n3, R.wide, XA, R.xq, 0, D, 384)
        section_tick(1, 11)
        section_tick(1, 12)
        have("d0", "d1", "d2")
        g_in.wait()
        round_g(R.gb)
        hidden_grad(R.gb, R.tall, R.gu, 0, 8)
        section_tick(1, 13)
        have("x1", "k0", "k1")

        def cross(img):
            message(img).wait_recv()
            project(R.xin, R.wide, KV, R.kv, 0, 2 * D, 768, img * SEQ, SEQ)
            attend_forward(R.xq, 0, R.kv, 0, R.kv, D, R.cm, R.cmT, None, img * 6, img * 6 + 6, R.kept)

        cross(0)
        section_tick(1, 14)
        cross(1)
        project_add(R.cm, R.wide, XB, R.mid, R.late, 384)
        norm_forward(R.late, gain(1), R.n2)
        have("g0", "u0", "g1", "u1")
        gated_both(R.n2, R.wide, R.gu, R.hid, 0, 8)
        all_sent(1)

    def sum_spot(name):
        b, lo, size = SUMS[name]
        return SUM_NAMES.index(name), b, pl.ds(lo, size), size

    stage_of = {}

    def core_copy(name):
        k, b, cs, size = sum_spot(name)
        if b == "tall":
            s = R.stage_tall.at[:, :, :, cs]
        else:
            s = R.stage.at[stage_of[name], :, :, :, pl.ds(0, size)]
        return remote(s, buf[b].at[:, :, c, :, cs], R.t_cs.at[k], R.t_cr.at[k], c_peer)

    def paired(name):
        return name in PAIRED

    def y_copy(name):
        k, b, cs, size = sum_spot(name)
        if paired(name):
            return remote(buf[b].at[z, 1 - y, c, :, cs], ybuf[b].at[0, :, cs], R.t_ys.at[k], R.t_yr.at[k], y_peer)
        return remote(buf[b].at[:, 1 - y, c, :, cs], ybuf[b].at[:, :, cs], R.t_ys.at[k], R.t_yr.at[k], y_peer)

    def moving(name, a, e):
        _, b, cs, _ = sum_spot(name)
        return buf[b].at[a:e, :, c, :, cs] if paired(name) else buf[b].at[a:e, y, c, :, cs]

    def landing_left(name, a, e):
        _, b, cs, _ = sum_spot(name)
        return buf[b].at[a:e, :, 1 - c, :, cs] if paired(name) else buf[b].at[a:e, 0, 1 - c, :, cs]

    def landing_right(name, a, e):
        _, b, cs, size = sum_spot(name)
        if paired(name):
            return R.pair_in.at[PAIRED.index(name), a:e]
        return buf[b].at[a:e, 1, 1 - c, :, cs]

    def right_copy(name, zz):
        k = SUM_NAMES.index(name)
        return remote(moving(name, zz + 1, 4), landing_left(name, zz + 1, 4), R.t_rs.at[k], R.t_rr.at[k], right)

    def left_copy(name, zz):
        k = SUM_NAMES.index(name)
        return remote(moving(name, 0, zz), landing_right(name, 0, zz), R.t_ls.at[k], R.t_lr.at[k], left)

    def send_right(name, zz):
        pl.semaphore_wait(R.free_r.at[SUM_NAMES.index(name)], 1)
        right_copy(name, zz).start()

    def send_left(name, zz):
        pl.semaphore_wait(R.free_l.at[SUM_NAMES.index(name)], 1)
        left_copy(name, zz).start()

    def add_blocks(name, landed, a, e):
        mine = moving(name, a, e)

        @pl.loop(0, e - a)
        def _(j):
            mine[j] = (mine[j].astype(F32) + landed[j].astype(F32)).astype(BF)

    def add_left(name, zz):
        k = SUM_NAMES.index(name)
        d = landing_left(name, zz, 4)
        remote(d, d, R.t_rs.at[k], R.t_rr.at[k], left).wait_recv()
        add_blocks(name, d, zz, 4)

    def add_right(name, zz):
        k = SUM_NAMES.index(name)
        d = landing_right(name, 0, zz + 1)
        remote(d, d, R.t_ls.at[k], R.t_lr.at[k], right).wait_recv()
        add_blocks(name, d, 0, zz + 1)

    def open_line(name):
        k = SUM_NAMES.index(name)
        when(z > 0, lambda: pl.semaphore_signal(R.free_r.at[k], inc=1, device_id=left, device_id_type=MESH))
        when(z < 3, lambda: pl.semaphore_signal(R.free_l.at[k], inc=1, device_id=right, device_id_type=MESH))

    def line_a(name):
        when(z == 0, lambda: send_right(name, 0))
        when(z == 3, lambda: send_left(name, 3))

    def line_b(name):
        def one():
            add_left(name, 1)
            send_right(name, 1)

        def two():
            add_right(name, 2)
            send_left(name, 2)

        when(z == 1, one)
        when(z == 2, two)

    def line_c(name):
        def one():
            add_right(name, 1)
            send_left(name, 1)

        def two():
            add_left(name, 2)
            send_right(name, 2)

        when(z == 1, one)
        when(z == 2, two)

    def line_d(name):
        when(z == 0, lambda: add_right(name, 0))
        when(z == 3, lambda: add_left(name, 3))

    def line_sent(name):
        for zz in range(3):
            when(z == zz, lambda: right_copy(name, zz).wait_send())
            when(z == zz + 1, lambda: left_copy(name, zz + 1).wait_send())

    def release(name):
        pl.semaphore_signal(R.free.at[FREE[name]], inc=1, device_id=c_peer, device_id_type=MESH)

    def claim(name):
        pl.semaphore_wait(R.free.at[FREE[name]], 1)

    order = []

    def grad_wide(name, nT, g_ref, gcol, tile):
        k, b, cs, size = sum_spot(name)
        lo = SUMS[name][1]
        slot = len(order) % 2
        if len(order) >= 2:
            core_copy(order[-2]).wait_send()
        stage_of[name] = slot
        order.append(name)
        lhs = half_rows(nT, 1 - c)

        @pl.loop(0, size // tile)
        def _(j):
            w = dot(lhs, g_ref[:, pl.ds(mul(gcol + j * tile, 128), tile)]).astype(BF)
            R.stage[slot, :, :, :, pl.ds(mul(j * tile, 128), tile)] = w.reshape(4, 2, 48, tile)

        core_copy(name).start()
        mine = half_rows(nT, c)

        @pl.loop(0, size // tile)
        def _(j):
            w = dot(mine, g_ref[:, pl.ds(mul(gcol + j * tile, 128), tile)]).astype(BF)
            R.wide[:, :, c, :, pl.ds(mul(lo + j * tile, 128), tile)] = w.reshape(4, 2, 48, tile)

    def drain():
        for name in order[-2:]:
            core_copy(name).wait_send()
        order.clear()

    def grad_tall():
        def rows_of(j, cc):
            return dot(R.hidT[pl.ds(mul((2 * j + cc) * 128, 128), 128), :], R.gb[...]).astype(BF)

        @pl.loop(0, 8)
        def _(j):
            R.stage_tall[j // 2, j % 2] = rows_of(j, 1 - c)

        core_copy("out0").start()
        core_copy("out1").start()

        @pl.loop(0, 8)
        def _(j):
            R.tall[j // 2, j % 2, c] = rows_of(j, c)

    ready, crossing, moving_on, finished = [], [], [], []

    def feed():
        while ready and len(crossing) < 3:
            name = ready.pop(0)
            y_copy(name).start()
            crossing.append(name)

    def core_stage(name, pass_on=True):
        k, b, cs, size = sum_spot(name)
        w = buf[b]
        landed = w.at[:, :, 1 - c, :, cs]
        remote(landed, landed, R.t_cs.at[k], R.t_cr.at[k], c_peer).wait_recv()

        @pl.loop(0, 8)
        def _(j):
            own = w[j // 2, j % 2, c, :, cs].astype(F32)
            w[j // 2, j % 2, c, :, cs] = (own + w[j // 2, j % 2, 1 - c, :, cs].astype(F32)).astype(BF)

        if pass_on:
            enter(name)

    def enter(name):
        open_line(name)
        if paired(name):
            line_a(name)
            moving_on.append([name, later, line_b, later, line_c, later, line_d, late_cross])
        else:
            ready.append(name)
            feed()

    def later(name):
        pass

    def late_cross(name):
        y_copy(name).start()
        crossing.append(name)

    def y_stage(name):
        k, b, cs, size = sum_spot(name)
        w, r = buf[b], ybuf[b]
        if paired(name):
            d = r.at[0, :, cs]
            remote(d, d, R.t_ys.at[k], R.t_yr.at[k], y_peer).wait_recv()
            finish(name, w[z, y, c, :, cs].astype(F32) + r[0, :, cs].astype(F32))
            return
        y_copy(name).wait_recv()

        @pl.loop(0, 4)
        def _(j):
            w[j, y, c, :, cs] = (w[j, y, c, :, cs].astype(F32) + r[j, :, cs].astype(F32)).astype(BF)

        line_a(name)
        moving_on.append([name, later, line_b, later, line_c, later, line_d, last])

    def last(name):
        k, b, cs, size = sum_spot(name)
        finish(name, buf[b][z, y, c, :, cs].astype(F32))

    def turn():
        going = list(moving_on)
        if crossing:
            name = crossing.pop(0)
            y_stage(name)
            feed()
        for item in going:
            item.pop(1)(item[0])
            if len(item) == 1:
                moving_on.remove(item)

    def out_copy(name):
        k, b, cs, size = sum_spot(name)
        arg, lo = OUT_OF[name]
        kind = [f for f in finished if SUMS[f][0] == b]
        slot = kind.index(name) % 2
        f = R.fin_tall.at[slot] if b == "tall" else R.fin.at[slot, :, pl.ds(0, size)]
        return local(f, dst[arg].at[:, pl.ds(lo, size)], R.t_out.at[k])

    def finish(name, total):
        k, b, cs, size = sum_spot(name)
        kind = [f for f in finished if SUMS[f][0] == b]
        slot = len(kind) % 2
        if len(kind) >= 2:
            out_copy(kind[-2]).wait()
        finished.append(name)
        if b == "tall":
            R.fin_tall[slot] = total
        else:
            R.fin[slot, :, pl.ds(0, size)] = total
        out_copy(name).start()

    def over_copy(j):
        k, b, cs, size = sum_spot(("k0", "k1")[j])
        return remote(
            R.wide.at[:, :, c, :, cs], R.wide.at[:, :, c, :, pl.ds(XA + j * D, D)], R.t_xs.at[j], R.t_xr.at[j], x_peer
        )

    def project_back(g_ref, wcol, out_ref):
        out_ref[...] = dot(g_ref[...], wide_cols(R.wide, wcol, D), NT).astype(BF)

    def down_grads():
        release("out")
        claim("out")
        grad_tall()
        core_stage("out0")
        core_stage("out1")

    def in_grads():
        release("in")
        claim("in")
        grad_wide("in0", R.nT, R.gu, 0, 512)
        grad_wide("in1", R.nT, R.gu, 1024, 512)
        core_stage("in0")
        grad_wide("in2", R.nT, R.gu, FF, 512)
        core_stage("in1")
        grad_wide("in3", R.nT, R.gu, FF + 1024, 512)
        core_stage("in2")

    gains_own = lambda: small_pair(R.hc, 1, 4, c_peer)
    gains_row = lambda: small_pair(R.hy, 1, 3, y_peer)
    gains_line = lambda: small_z(R.gain, R.hz, 1)
    gain_copy = local(R.dgain, gain_o, R.s_out.at[2])
    grad_copy = local(R.g, grad_o, R.s_out.at[1])

    def gains_a():
        R.hc[0] = R.dgain[...]
        gains_own().start()

    def gains_b(_):
        gains_own().wait()
        R.hy[0] = R.hc[0] + R.hc[1]
        gains_row().start()

    def gains_c(_):
        gains_row().wait()
        R.gain[...] = R.hy[0] + R.hy[1]
        for q in gains_line():
            q.start()

    def gains_d(_):
        for q in gains_line():
            q.wait()
        R.hz[z] = R.gain[...]
        R.dgain[...] = (R.hz[0] + R.hz[1]) + (R.hz[2] + R.hz[3])
        gain_copy.start()

    dec_res = local(R.acc, res_o, R.s_out.at[0])
    enc_res = local(R.late, res_o, R.s_out.at[0])

    def dec_middle():
        back_project(R.gu, 0, R.wide, WIN, 2 * FF, 1024, R.acc)
        norm_backward(R.late, gain(1), R.acc, R.g, R.dgain, 1, low_ref=R.gb2)
        project_back(R.gb2, XB, R.xsend)
        for img in range(MICRO):
            attend_backward(
                R.xq, 0, R.kv, 0, R.kv, D, R.xsend, None, R.xq, 0, R.kv, 0, R.kv, D, img * 6, img * 6 + 6, R.kept
            )
            back_project(R.kv, 0, R.wide, KV, 2 * D, 768, R.acc, img * SEQ, SEQ)
            rows = pl.ds(img * SEQ, SEQ)
            R.xsend[rows, :] = R.acc[rows, :].astype(BF)
            message(img).start()
        down(R.late, R.acc, (0, 256, 512))
        dec_res.start()
        transpose_to(R.hid, R.hidT)

    def dec_all():
        dec_forward()
        dec_middle()

    def enc_middle():
        enc_res.start()
        transpose_to(R.hid, R.hidT)
        transpose_to(R.n2, R.nT)
        g_in.wait()
        for img in range(MICRO):
            message(img).wait_send()
        for img in range(MICRO):
            lo = img * SEQ
            message(img).wait_recv()
            norm_backward(R.late, gain(2), R.xin, R.g, R.dgain, 2, lo, SEQ, R.gb)
            gated_backward(R.gb, R.tall, R.gu, 0, 8, lo, SEQ)

    def enc_in():
        back_project(R.gu, 0, R.wide, WIN, 2 * FF, 1024, R.acc)
        norm_backward(R.mid, gain(1), R.acc, R.g, R.dgain, 1, low_ref=R.gb2)

    def dec_keys():
        release("k")
        transpose_to(R.xin, R.nT)
        claim("k")
        grad_wide("k0", R.nT, R.kv, 0, 384)
        grad_wide("k1", R.nT, R.kv, D, 384)
        core_stage("k0", False)
        over_copy(0).start()
        core_stage("k1", False)
        over_copy(1).start()
        drain()
        transpose_to(R.n2, R.nT)

    def dec_cross():
        dec_res.wait()
        back_project(R.xq, 0, R.wide, XA, D, 768, R.acc)
        release("x")
        transpose_to(R.n3, R.nT)
        claim("x")
        grad_wide("x0", R.nT, R.xq, 0, 384)
        grad_wide("x1", R.cmT, R.gb2, 0, 384)
        core_stage("x0", False)
        core_stage("x1", False)
        norm_backward(R.mid, gain(2), R.acc, R.g, R.dgain, 2, low_ref=R.gb2)
        for img in range(MICRO):
            message(img).wait_send()
        drain()

    when(first, enc_forward)
    when(second, dec_all)
    when(first, enc_middle)
    down_grads()
    when(first, enc_in)
    when(second, dec_keys)
    in_grads()
    drain()
    core_stage("in3")
    when(second, dec_cross)

    project_back(R.gb2, OP, R.ao)
    release("o")
    claim("o")
    grad_wide("o", R.aoT, R.gb2, 0, 384)
    turn()
    attend_backward(R.qkv, 0, R.qkv, D, R.qkv, 2 * D, R.ao, R.mask, R.qkv, 0, R.qkv, D, R.qkv, 2 * D, 0, 6)
    core_stage("o")
    turn()
    attend_backward(R.qkv, 0, R.qkv, D, R.qkv, 2 * D, R.ao, R.mask, R.qkv, 0, R.qkv, D, R.qkv, 2 * D, 6, 12)
    turn()
    back_project(R.qkv, 0, R.wide, QKV, 3 * D, 768, R.acc)
    release("q")
    transpose_to(R.n1, R.nT)
    claim("q")
    for j in range(2):
        when(first, lambda: over_copy(j).wait_recv())
        enter(("x0", "x1")[j])
    grad_wide("q0", R.nT, R.qkv, 0, 384)
    grad_wide("q1", R.nT, R.qkv, D, 384)
    core_stage("q0")
    grad_wide("q2", R.nT, R.qkv, 2 * D, 384)
    core_stage("q1")
    grad_wide("q3", R.nT, R.qkv, 2 * D + 384, 384)
    core_stage("q2")
    core_stage("q3")
    turn()
    norm_backward(R.x, gain(0), R.acc, R.g, R.dgain, 0)
    grad_copy.start()
    gains_a()
    moving_on.append(["gains", gains_b, later, later, later, gains_c, later, later, gains_d])
    while ready or crossing or moving_on:
        turn()
    for name in ("out0", "out1"):
        core_copy(name).wait_send()
    drain()
    for name in finished:
        y_copy(name).wait_send()
        line_sent(name)
    for b in ("tall", "wide"):
        for name in [f for f in finished if SUMS[f][0] == b][-2:]:
            out_copy(name).wait()
    when(first, lambda: enc_res.wait())
    when(second, lambda: [over_copy(j).wait_send() for j in range(2)] and None)
    grad_copy.wait()
    gain_copy.wait()


def from_behind(block, axis, distance):
    devices = range(lax.axis_size(axis))
    route = [(i - distance, i) for i in devices if i - distance in devices]
    return lax.ppermute(block, axis, route)


def rms_norm(activations, gain_row):
    return (
        activations
        * lax.rsqrt(jnp.mean(activations * activations, axis=-1, keepdims=True) + 1e-06)
        * gain_row
    )


def product(left_side, right_side):
    return jnp.dot(left_side, right_side, preferred_element_type=jnp.float32)


def weight_grad(left_side, right_side):
    return jnp.einsum("sd,se->de", left_side, right_side, preferred_element_type=jnp.float32)


def input_back(gradient, weight):
    return jnp.einsum("se,de->sd", gradient, weight, preferred_element_type=jnp.float32)


def norm_back(activations, gain_row, gradient):
    _, pull_back = jax.vjp(rms_norm, activations, gain_row)
    return pull_back(gradient)


def heads_of(activations):
    return activations.reshape(activations.shape[0], HEADS, HDIM)


def logits_of(queries, keys_in, allowed):
    raw_logits = jnp.einsum(
        "qhd,khd->hqk", heads_of(queries), heads_of(keys_in), preferred_element_type=jnp.float32
    ) * HDIM ** (-0.5)
    if allowed is None:
        return raw_logits
    return jnp.where(allowed[None], raw_logits, -1e30)


def attend_plain(queries, keys_in, values, allowed):
    logits = logits_of(queries, keys_in, allowed)
    row_peak = jnp.max(logits, axis=-1, keepdims=True)
    weights = jnp.exp(logits - row_peak)
    row_total = jnp.sum(weights, axis=-1, keepdims=True)
    softmax_out = (weights / row_total).astype(jnp.bfloat16)
    mixed_heads = jnp.einsum(
        "hqk,khd->qhd", softmax_out, heads_of(values), preferred_element_type=jnp.float32
    )
    return (
        mixed_heads.reshape(queries.shape[0], D).astype(jnp.bfloat16),
        row_peak + jnp.log(row_total),
    )


def attend_plain_back(queries, keys_in, values, allowed, log_total, grad_mixed):
    softmax_out = jnp.exp(logits_of(queries, keys_in, allowed) - log_total)
    grad_heads = heads_of(grad_mixed)
    grad_softmax = jnp.einsum(
        "qhd,khd->hqk", grad_heads, heads_of(values), preferred_element_type=jnp.float32
    )
    grad_values = jnp.einsum(
        "hqk,qhd->khd",
        softmax_out.astype(jnp.bfloat16),
        grad_heads,
        preferred_element_type=jnp.float32,
    )
    inner_sum = jnp.sum(softmax_out * grad_softmax, axis=-1, keepdims=True)
    grad_logits = (softmax_out * (grad_softmax - inner_sum) * HDIM ** (-0.5)).astype(jnp.bfloat16)
    grad_queries = jnp.einsum(
        "hqk,khd->qhd", grad_logits, heads_of(keys_in), preferred_element_type=jnp.float32
    )
    grad_keys = jnp.einsum(
        "hqk,qhd->khd", grad_logits, heads_of(queries), preferred_element_type=jnp.float32
    )
    query_count = queries.shape[0]
    key_count = keys_in.shape[0]
    return (
        grad_queries.reshape(query_count, D),
        grad_keys.reshape(key_count, D),
        grad_values.reshape(key_count, D),
    )


def self_forward(inputs, gain_row, w_attn, allowed):
    normed = rms_norm(inputs, gain_row).astype(jnp.bfloat16)
    packed = product(normed, w_attn[:, : 3 * D]).astype(jnp.bfloat16)
    mixed_heads, log_total = attend_plain(
        packed[:, :D], packed[:, D : 2 * D], packed[:, 2 * D :], allowed
    )
    return (
        inputs + product(mixed_heads, w_attn[:, 3 * D :]),
        (normed, packed, mixed_heads, log_total),
    )


def self_backward(inputs, gain_row, w_attn, allowed, kept_values, grad_result):
    normed, packed, mixed_heads, log_total = kept_values
    grad_low = grad_result.astype(jnp.bfloat16)
    grad_proj = weight_grad(mixed_heads, grad_low)
    grad_mixed = input_back(grad_low, w_attn[:, 3 * D :]).astype(jnp.bfloat16)
    grad_queries, grad_keys, grad_values = attend_plain_back(
        packed[:, :D], packed[:, D : 2 * D], packed[:, 2 * D :], allowed, log_total, grad_mixed
    )
    grad_packed = jnp.concatenate([grad_queries, grad_keys, grad_values], axis=1).astype(
        jnp.bfloat16
    )
    grad_qkv = weight_grad(normed, grad_packed)
    grad_inputs, grad_gain = norm_back(
        inputs, gain_row, input_back(grad_packed, w_attn[:, : 3 * D])
    )
    return (grad_result + grad_inputs, grad_gain, jnp.concatenate([grad_qkv, grad_proj], axis=1))


def gated_unit(gated):
    return jax.nn.gelu(gated[:, :FF], approximate=True) * gated[:, FF:]


def ffn_forward(inputs, gain_row, w_in, w_out):
    normed = rms_norm(inputs, gain_row).astype(jnp.bfloat16)
    gated = product(normed, w_in)
    hidden = gated_unit(gated).astype(jnp.bfloat16)
    return (inputs + product(hidden, w_out), (normed, gated, hidden))


def ffn_backward(inputs, gain_row, w_in, w_out, kept_values, grad_result):
    normed, gated, hidden = kept_values
    grad_low = grad_result.astype(jnp.bfloat16)
    grad_wout = weight_grad(hidden, grad_low)
    _, pull_back = jax.vjp(gated_unit, gated)
    grad_gated = pull_back(input_back(grad_low, w_out))[0].astype(jnp.bfloat16)
    grad_win = weight_grad(normed, grad_gated)
    grad_inputs, grad_gain = norm_back(inputs, gain_row, input_back(grad_gated, w_in))
    return (grad_result + grad_inputs, grad_gain, grad_win, grad_wout)


def encoder_forward(inputs, weights):
    w_attn, w_extra, w_in, w_out, gain_rows = weights
    middle, first_kept = self_forward(inputs, gain_rows[0], w_attn, None)
    result, second_kept = ffn_forward(middle, gain_rows[1], w_in, w_out)
    normed = rms_norm(result, gain_rows[2]).astype(jnp.bfloat16)
    cross_kv = product(normed, w_extra).astype(jnp.bfloat16)
    return (result, cross_kv, (middle, first_kept, second_kept, normed))


def encoder_backward(inputs, weights, grad_result, grad_kv):
    w_attn, w_extra, w_in, w_out, gain_rows = weights
    result, _, kept_values = encoder_forward(inputs, weights)
    middle, first_kept, second_kept, normed = kept_values
    grad_extra = weight_grad(normed, grad_kv)
    grad_final, gain_final = norm_back(result, gain_rows[2], input_back(grad_kv, w_extra))
    grad_middle, gain_late, grad_win, grad_wout = ffn_backward(
        middle, gain_rows[1], w_in, w_out, second_kept, grad_result + grad_final
    )
    grad_inputs, gain_early, grad_attn = self_backward(
        inputs, gain_rows[0], w_attn, None, first_kept, grad_middle
    )
    return (
        grad_inputs,
        (
            grad_attn,
            grad_extra,
            grad_win,
            grad_wout,
            jnp.stack([gain_early, gain_late, gain_final]),
        ),
    )


def decoder_step(inputs, cross_kv, allowed, weights, grad_result):
    w_attn, w_extra, w_in, w_out, gain_rows = weights
    middle, first_kept = self_forward(inputs, gain_rows[0], w_attn, allowed)
    query_in = rms_norm(middle, gain_rows[2]).astype(jnp.bfloat16)
    queries = product(query_in, w_extra[:, :D]).astype(jnp.bfloat16)
    mixed_heads, log_total = attend_plain(queries, cross_kv[:, :D], cross_kv[:, D:], None)
    after_cross = middle + product(mixed_heads, w_extra[:, D:])
    result, second_kept = ffn_forward(after_cross, gain_rows[1], w_in, w_out)
    grad_after, gain_late, grad_win, grad_wout = ffn_backward(
        after_cross, gain_rows[1], w_in, w_out, second_kept, grad_result
    )
    grad_low = grad_after.astype(jnp.bfloat16)
    grad_cross_out = weight_grad(mixed_heads, grad_low)
    grad_mixed = input_back(grad_low, w_extra[:, D:]).astype(jnp.bfloat16)
    grad_queries, grad_keys, grad_values = attend_plain_back(
        queries, cross_kv[:, :D], cross_kv[:, D:], None, log_total, grad_mixed
    )
    grad_queries = grad_queries.astype(jnp.bfloat16)
    grad_cross_in = weight_grad(query_in, grad_queries)
    grad_normed, gain_cross = norm_back(
        middle, gain_rows[2], input_back(grad_queries, w_extra[:, :D])
    )
    grad_inputs, gain_early, grad_attn = self_backward(
        inputs, gain_rows[0], w_attn, allowed, first_kept, grad_after + grad_normed
    )
    grad_kv = jnp.concatenate([grad_keys, grad_values], axis=1).astype(jnp.bfloat16)
    gradients = (
        grad_attn,
        jnp.concatenate([grad_cross_in, grad_cross_out], axis=1),
        grad_win,
        grad_wout,
        jnp.stack([gain_early, gain_late, gain_cross]),
    )
    return (result, grad_inputs, grad_kv, gradients)


def general(acts, w_attn, w_extra, w_in, w_out, gains, segments, cotangent):
    gathered = (
        lax.all_gather(w_attn[0], "dp", axis=0, tiled=True),
        lax.all_gather(w_extra[0], "dp", axis=0, tiled=True),
        lax.all_gather(w_in[0], "dp", axis=0, tiled=True),
        lax.all_gather(w_out[0], "dp", axis=0, tiled=True),
        lax.all_gather(gains[0], "dp", axis=1, tiled=True),
    )
    weights = gathered[:4] + (gathered[4].astype(jnp.float32),)
    inputs = acts[0, :, 0]
    upstream = cotangent[0, :, 0]
    is_first = lax.axis_index("section") == 0
    positions = jnp.arange(SEQ)
    causal = positions[None, :] <= positions[:, None]
    zero_message = jnp.zeros((SEQ, 2 * D), jnp.bfloat16)
    zero_grads = tuple((jnp.zeros(weight.shape, jnp.float32) for weight in weights))
    carried = (jnp.zeros((MICRO, SEQ, D), jnp.float32), jnp.zeros((MICRO, SEQ, D), jnp.float32))
    received = zero_message
    returned = zero_message
    totals = zero_grads
    moments = MICRO + 2
    for moment in range(moments):

        def first_section(carried, received, returned):
            results, grad_inputs = carried
            message = zero_message
            fresh_grads = zero_grads
            if moment < MICRO:
                result, message, _ = encoder_forward(inputs[moment], weights)
                results = results.at[moment].set(result)
            if moment >= 2:
                grad_rows, fresh_grads = encoder_backward(
                    inputs[moment - 2], weights, upstream[moment - 2], returned
                )
                grad_inputs = grad_inputs.at[moment - 2].set(grad_rows)
            return ((results, grad_inputs), message, zero_message, fresh_grads)

        def second_section(carried, received, returned):
            results, grad_inputs = carried
            message = zero_message
            fresh_grads = zero_grads
            if 1 <= moment <= MICRO:
                segment_ids = segments[moment - 1, 0]
                allowed = (segment_ids[:, None] == segment_ids[None, :]) & causal
                result, grad_rows, message, fresh_grads = decoder_step(
                    inputs[moment - 1], received, allowed, weights, upstream[moment - 1]
                )
                results = results.at[moment - 1].set(result)
                grad_inputs = grad_inputs.at[moment - 1].set(grad_rows)
            return ((results, grad_inputs), zero_message, message, fresh_grads)

        carried, forward_message, back_message, fresh_grads = lax.cond(
            is_first, first_section, second_section, carried, received, returned
        )
        if moment < MICRO:
            received = from_behind(forward_message, "section", 1)
        if 1 <= moment <= MICRO:
            returned = from_behind(back_message, "section", -1)
        if moment >= 1:
            totals = tuple((jnp.add(*couple) for couple in zip(totals, fresh_grads)))
    results, grad_inputs = carried
    final = (
        lax.psum_scatter(totals[0], "dp", scatter_dimension=0, tiled=True),
        lax.psum_scatter(totals[1], "dp", scatter_dimension=0, tiled=True),
        lax.psum_scatter(totals[2], "dp", scatter_dimension=0, tiled=True),
        lax.psum_scatter(totals[3], "dp", scatter_dimension=0, tiled=True),
        lax.psum_scatter(totals[4], "dp", scatter_dimension=1, tiled=True),
    )
    return (
        results[None, :, None],
        grad_inputs[None, :, None],
        final[0][None],
        final[1][None],
        final[2][None],
        final[3][None],
        final[4][None],
    )


def step(acts, w_attn, w_extra, w_in, w_out, gains, segments, cotangent):
    me = lax.axis_index("dp")
    share = gains.shape[2]
    own_gain = lax.dynamic_update_slice(jnp.zeros((8, D), F32), gains[0].astype(F32), (0, me * share))
    anywhere = pl.BlockSpec(memory_space=pl.ANY)
    shape = lambda *s: jax.ShapeDtypeStruct(s, F32)
    scratch = scratch_list()
    results, input_grad, attn, extra, win, wout, gain = pl.pallas_call(
        whole_kernel,
        out_shape=(
            shape(ROWS, D), shape(ROWS, D), shape(48, 4 * D), shape(48, 2 * D), shape(48, 2 * FF), shape(128, D), shape(8, D),
        ),
        in_specs=[anywhere] * 7 + [pl.BlockSpec(memory_space=pltpu.VMEM)],
        out_specs=[anywhere] * 7,
        scratch_shapes=list(scratch.values()),
        compiler_params=pltpu.CompilerParams(
            collective_id=0, has_side_effects=True, vmem_limit_bytes=63 * 2**20
        ),
    )(
        acts.reshape(ROWS, D), cotangent.reshape(ROWS, D), w_attn[0], w_extra[0], w_in[0], w_out[0], own_gain,
        segments.reshape(MICRO, SEQ),
    )
    grad_gains = lax.dynamic_slice(gain, (0, me * share), (3, share))
    like = (1, MICRO, 1, SEQ, D)
    return (
        results.reshape(like), input_grad.reshape(like), attn[None], extra[None], win[None], wout[None], grad_gains[None],
    )


def solution(mesh):
    in_specs = (
        P("section", None, "dp", None, None),
        P("section", "dp", None),
        P("section", "dp", None),
        P("section", "dp", None),
        P("section", "dp", None),
        P("section", None, "dp"),
        P(None, "dp", None),
        P("section", None, "dp", None, None),
    )
    out_specs = (
        P("section", None, "dp", None, None),
        P("section", None, "dp", None, None),
        P("section", "dp", None),
        P("section", "dp", None),
        P("section", "dp", None),
        P("section", "dp", None),
        P("section", None, "dp"),
    )
    fits = mesh.shape["dp"] == 16
    return jax.shard_map(step if fits else general, mesh=mesh, in_specs=in_specs, out_specs=out_specs, check_vma=False)
```

```python
import jax
import jax.numpy as jnp
from jax import lax
from jax.experimental import pallas as pl
from jax.experimental.pallas import tpu as pltpu
from jax.sharding import PartitionSpec as P

D=768; HEADS=12; HDIM=64; FF=2048; SEQ=256; MICRO=2
ROWS=MICRO*SEQ
BF=jnp.bfloat16; F32=jnp.float32
QKV, OP, XA, XB, WIN, KV = 0, 3*D, 4*D, 5*D, 6*D, 6*D+2*FF
WIDE = KV + 2*D
NN=(((1,),(0,)),((),())); NT=(((1,),(1,)),((),()))

def mul(start, k): return pl.multiple_of(start, k)
def dot(a,b,dims=NN): return lax.dot_general(a,b,dims,preferred_element_type=F32)

def wide_cols(wa, start, size):
    return wa[:, :, :, :, pl.ds(start, size)].reshape(D, size)

def rms_rows(v):
    return lax.rsqrt(jnp.mean(v*v, axis=-1, keepdims=True) + 1e-6)

def norm_forward(v_ref, gain, n_ref, first=0, count=ROWS):
    @pl.loop(0, count//64)
    def _(i):
        rows=pl.ds(mul(first+i*64,64),64)
        v=v_ref[rows,:]
        n_ref[rows,:]=(v*rms_rows(v)*gain).astype(BF)

def norm_backward(v_ref, gain, dn_ref, g_ref, dgain_ref, slot, first=0, count=ROWS, low_ref=None):
    def body(i, acc):
        rows=pl.ds(mul(first+i*64,64),64)
        v=v_ref[rows,:]; dn=dn_ref[rows,:].astype(F32)
        r=rms_rows(v)
        t=dn*gain
        vr=v*r
        g=g_ref[rows,:]+r*(t-vr*jnp.mean(t*vr,axis=-1,keepdims=True))
        g_ref[rows,:]=g
        if low_ref is not None:
            low_ref[rows,:]=g.astype(BF)
        return acc+jnp.sum(dn*vr,axis=0,keepdims=True)
    acc=lax.fori_loop(0,count//64,body,jnp.zeros((1,D),F32))
    dgain_ref[slot:slot+1,:]+=acc

def transpose_to(src_ref, dst_ref, first=0, count=ROWS):
    cols=src_ref.shape[1]
    @pl.loop(0, cols//128)
    def _(j):
        cs=pl.ds(mul(j*128,128),128)
        dst_ref[cs, pl.ds(first,count)] = src_ref[pl.ds(first,count),cs].T

def project(n_ref, wa, wcol, out_ref, ocol, total, tile, first=0, count=ROWS):
    @pl.loop(0, total//tile)
    def _(j):
        w=wide_cols(wa, mul(wcol+j*tile,128), tile)
        out_ref[pl.ds(first,count), pl.ds(mul(ocol+j*tile,128),tile)] = dot(n_ref[pl.ds(first,count),:], w).astype(out_ref.dtype)

def project_add(a_ref, wa, wcol, base_ref, out_ref, tile, first=0, count=ROWS):
    rows=pl.ds(first,count)
    @pl.loop(0, D//tile)
    def _(j):
        w=wide_cols(wa, mul(wcol+j*tile,128), tile)
        cs=pl.ds(mul(j*tile,128),tile)
        out_ref[rows,cs] = base_ref[rows,cs]+dot(a_ref[rows,:], w)

def back_project(g_ref, gcol, wa, wcol, total, tile, acc_ref, first=0, count=ROWS, fresh=True):
    rows=pl.ds(first,count)
    def part(j):
        w=wide_cols(wa, mul(wcol+j*tile,128), tile)
        return dot(g_ref[rows, pl.ds(mul(gcol+j*tile,128),tile)], w, NT)
    if fresh:
        acc_ref[rows,:]=part(0)
    @pl.loop(1 if fresh else 0, total//tile)
    def _(j):
        acc_ref[rows,:]+=part(j)

def attend_forward(q_ref, qc, k_ref, kc, v_ref, vc, o_ref, oT_ref, mask_ref, start, stop, kept_ref=None, unroll=1):
    @pl.loop(start, stop, unroll=unroll)
    def _(i):
        img=i//6; p=i%6
        rows=pl.ds(mul(img*SEQ,SEQ),SEQ)
        def cols(base): return pl.ds(mul(base+p*128,128),128)
        q2=q_ref[rows,cols(qc)]*jnp.asarray(0.125,BF)
        k2=k_ref[rows,cols(kc)]
        vT=v_ref[rows,cols(vc)].T
        lane=lax.broadcasted_iota(jnp.int32,(SEQ,128),1)//64
        parts=[]
        for a in range(2):
            ka=jnp.where(lane==a,k2,jnp.zeros_like(k2))
            s=dot(ka,q2,NT)
            if mask_ref is not None:
                s=jnp.where(mask_ref[img].astype(F32)>0,s,-1e30)
            e=jnp.exp(s-jnp.max(s,axis=0,keepdims=True))
            w=(e*(1.0/jnp.sum(e,axis=0,keepdims=True))).astype(BF)
            if kept_ref is not None:
                kept_ref[pl.ds(mul(i*SEQ,SEQ),SEQ),a*SEQ:(a+1)*SEQ]=w
            parts.append(dot(vT[a*64:(a+1)*64],w))
        oT=jnp.concatenate(parts,axis=0).astype(BF)
        oT_ref[pl.ds(mul(p*128,128),128),rows]=oT
        o_ref[rows,cols(0)]=oT.T

def attend_backward(q_ref, qc, k_ref, kc, v_ref, vc, d_ref, mask_ref, dq_ref, dqc, dk_ref, dkc, dv_ref, dvc, start, stop, kept_ref=None):
    @pl.loop(start, stop)
    def _(i):
        img=i//6; p=i%6
        rows=pl.ds(mul(img*SEQ,SEQ),SEQ)
        def cols(base): return pl.ds(mul(base+p*128,128),128)
        q2=q_ref[rows,cols(qc)]
        qs=q2*jnp.asarray(0.125,BF)
        k2=k_ref[rows,cols(kc)]
        v2=v_ref[rows,cols(vc)]
        d2=d_ref[rows,cols(0)]
        kT=k2.T
        lane=lax.broadcasted_iota(jnp.int32,(SEQ,128),1)//64
        dqT=[]; dk=[]; dv=[]
        for a in range(2):
            mine=lane==a
            if kept_ref is not None:
                wb=kept_ref[pl.ds(mul(i*SEQ,SEQ),SEQ),a*SEQ:(a+1)*SEQ]
                w=wb.astype(F32)
            else:
                s=dot(jnp.where(mine,k2,jnp.zeros_like(k2)),qs,NT)
                if mask_ref is not None:
                    s=jnp.where(mask_ref[img].astype(F32)>0,s,-1e30)
                e=jnp.exp(s-jnp.max(s,axis=0,keepdims=True))
                w=e*(1.0/jnp.sum(e,axis=0,keepdims=True))
                wb=w.astype(BF)
            dw=dot(jnp.where(mine,v2,jnp.zeros_like(v2)),d2,NT)
            wd=w*dw
            ds=((wd-w*jnp.sum(wd,axis=0,keepdims=True))*0.125).astype(BF)
            dv.append(dot(wb,d2))
            dk.append(dot(ds,q2))
            dqT.append(dot(kT[a*64:(a+1)*64],ds))
        dq_ref[rows,cols(dqc)]=jnp.concatenate(dqT,axis=0).astype(BF).T
        dk_ref[rows,cols(dkc)]=jnp.where(lane==0,dk[0],dk[1]).astype(BF)
        dv_ref[rows,cols(dvc)]=jnp.where(lane==0,dv[0],dv[1]).astype(BF)

C0=0.7978845608028654; C1=0.044715
def gated_parts(n_ref, wa, j, rows, tile):
    gate=dot(n_ref[rows,:], wide_cols(wa, mul(WIN+j*tile,128), tile))
    up=dot(n_ref[rows,:], wide_cols(wa, mul(WIN+FF+j*tile,128), tile))
    sq=gate*gate
    t=jnp.tanh(gate*(C0+(C0*C1)*sq))
    h=0.5+0.5*t
    slope=h+(0.5*gate)*(1.0-t*t)*(C0+(3*C0*C1)*sq)
    return up, gate*h, slope

def gated_forward(n_ref, wa, gu_ref, hid_ref, start, stop, first=0, count=ROWS, tile=256):
    rows=pl.ds(first,count)
    @pl.loop(start, stop)
    def _(j):
        lo=pl.ds(mul(j*tile,tile),tile); hi=pl.ds(mul(FF+j*tile,tile),tile)
        up,act,slope=gated_parts(n_ref,wa,j,rows,tile)
        hid_ref[rows,lo]=(act*up).astype(BF)
        gu_ref[rows,lo]=(up*slope).astype(BF)
        gu_ref[rows,hi]=act.astype(BF)

def hidden_grad(gb_ref, wo, gu_ref):
    @pl.loop(0, 4, unroll=2)
    def _(j):
        gu_ref[:,pl.ds(mul(FF+j*512,512),512)]=dot(gb_ref[...], wo[j].reshape(512,D), NT).astype(BF)

def gated_both(n_ref, wa, gu_ref, hid_ref, start, stop, tile=256):
    rows=pl.ds(0,ROWS)
    @pl.loop(start, stop)
    def _(j):
        lo=pl.ds(mul(j*tile,tile),tile); hi=pl.ds(mul(FF+j*tile,tile),tile)
        up,act,slope=gated_parts(n_ref,wa,j,rows,tile)
        hid_ref[rows,lo]=(act*up).astype(BF)
        dh=gu_ref[rows,hi].astype(F32)
        gu_ref[rows,lo]=(dh*up*slope).astype(BF)
        gu_ref[rows,hi]=(dh*act).astype(BF)

def gated_backward(gb_ref, wo, gu_ref, first=0, count=ROWS):
    rows=pl.ds(first,count)
    @pl.loop(0, 4, unroll=4)
    def _(j):
        lo=pl.ds(mul(j*512,512),512); hi=pl.ds(mul(FF+j*512,512),512)
        dh=dot(gb_ref[rows,:], wo[j].reshape(512,D), NT)
        gu_ref[rows,lo]=(dh*gu_ref[rows,lo].astype(F32)).astype(BF)
        gu_ref[rows,hi]=(dh*gu_ref[rows,hi].astype(F32)).astype(BF)

def half_rows(nT_ref, c):
    return jnp.concatenate([nT_ref[pl.ds(mul((2*j+c)*48,16),48),:] for j in range(8)],axis=0)


MESH = pl.DeviceIdType.MESH
BIG = 1152

PARTS = {
    "q0": ("attn", 0, "wide", QKV, 1152), "q1": ("attn", 1152, "wide", QKV + 1152, 1152), "o": ("attn", 3 * D, "wide", OP, D),
    "g0": ("in", 0, "wide", WIN, 1024), "u0": ("in", FF, "wide", WIN + FF, 1024),
    "g1": ("in", 1024, "wide", WIN + 1024, 1024), "u1": ("in", FF + 1024, "wide", WIN + FF + 1024, 1024),
    "x0": ("extra", 0, "wide", XA, D), "x1": ("extra", D, "wide", XB, D),
    "k0": (None, 0, "wide", KV, D), "k1": (None, D, "wide", KV + D, D),
    "d0": ("out", 0, "tall", 0, 256), "d1": ("out", 256, "tall", 256, 256), "d2": ("out", 512, "tall", 512, 256),
}
PART_NAMES = tuple(PARTS)
ROUTES = (
    (("q0", "q1", "o", "g0", "u0", "g1", "u1", "d2"), {3: "d0", 5: "d1"}),
    (("q0", "q1", "o", "x0", "x1", "k0", "k1", "g0", "u0", "g1", "u1"), {2: "d0", 4: "d1", 7: "d2"}),
)
SUMS = {
    "out0": ("tall", 0, 384), "out1": ("tall", 384, 384),
    "in0": ("wide", WIN, 1024), "in1": ("wide", WIN + 1024, 1024),
    "in2": ("wide", WIN + FF, 1024), "in3": ("wide", WIN + FF + 1024, 1024),
    "x0": ("wide", XA, D), "x1": ("wide", XB, D),
    "k0": ("wide", KV, D), "k1": ("wide", KV + D, D),
    "o": ("wide", OP, D),
    "q0": ("wide", QKV, D), "q1": ("wide", QKV + D, D), "q2": ("wide", QKV + 2 * D, 384), "q3": ("wide", QKV + 2 * D + 384, 384),
}
SUM_NAMES = tuple(SUMS)
PAIRED = ("out1",)
DIRECT = ("q1", "q2", "q3")
OUT_OF = {
    "out0": ("out", 0), "out1": ("out", 384), "in0": ("in", 0), "in1": ("in", 1024), "in2": ("in", FF), "in3": ("in", FF + 1024),
    "x0": ("extra", 0), "x1": ("extra", D), "o": ("attn", 3 * D),
    "q0": ("attn", 0), "q1": ("attn", D), "q2": ("attn", 2 * D), "q3": ("attn", 2 * D + 384),
}
FREE = {"out": 0, "in": 1, "x": 2, "k": 3, "o": 4, "q": 5}


def scratch_list():
    V, DMA, REG = pltpu.VMEM, pltpu.SemaphoreType.DMA, pltpu.SemaphoreType.REGULAR
    n, s = len(PARTS), len(SUMS)
    return dict(
        wide=V((4, 2, 2, 48, WIDE), BF), tall=V((4, 2, 2, 128, D), BF),
        y_wide=V((4, 48, WIDE), BF), y_tall=V((4, 128, D), BF), pair_in=V((1, 3, 2, 128, 384), BF),
        stage=V((2, 4, 2, 48, 1024), BF), stage_tall=V((4, 2, 128, D), BF),
        fin=V((2, 48, 1024), F32), fin_tall=V((2, 128, 384), F32),
        x=V((ROWS, D), F32), mid=V((ROWS, D), F32), late=V((ROWS, D), F32), g=V((ROWS, D), F32),
        n1=V((ROWS, D), BF), n2=V((ROWS, D), BF), n3=V((ROWS, D), BF), xin=V((ROWS, D), BF), nT=V((D, ROWS), BF),
        qkv=V((ROWS, 3 * D), BF), ao=V((ROWS, D), BF), aoT=V((D, ROWS), BF),
        xq=V((ROWS, D), BF), kv=V((ROWS, 2 * D), BF), cmT=V((D, ROWS), BF),
        gu=V((ROWS, 2 * FF), BF), hid=V((ROWS, FF), BF), kept=V((12 * SEQ, 2 * SEQ), BF), gb=V((ROWS, D), BF), gb2=V((ROWS, D), BF),
        mask=V((MICRO, SEQ, SEQ), BF), xsend=V((ROWS, D), BF),
        gz=V((4, 8, D), F32), gy=V((2, 8, D), F32), gc=V((2, 8, D), F32), gain=V((8, D), F32),
        dgain=V((8, D), F32), gout=V((3, 48), F32), hz=V((4, 8, D), F32), hy=V((2, 8, D), F32), hc=V((2, 8, D), F32),
        s_in=DMA((3,)), s_own=DMA((n,)), s_kx=DMA, s_kr=DMA,
        s_rs=DMA((n, 3)), s_rr=DMA((n, 3)), s_ls=DMA((n, 3)), s_lr=DMA((n, 3)),
        s_ys=DMA((n, 4)), s_yr=DMA((n, 4)), s_cs=DMA((n,)), s_cr=DMA((n,)),
        s_ms=DMA((MICRO,)), s_mr=DMA((MICRO,)), s_gs=DMA((2, 5)), s_gr=DMA((2, 5)),
        t_cs=DMA((s,)), t_cr=DMA((s,)), t_ys=DMA((s,)), t_yr=DMA((s,)),
        t_rs=DMA((s,)), t_rr=DMA((s,)), t_ls=DMA((s,)), t_lr=DMA((s,)),
        t_ds=DMA((len(DIRECT), 3)), t_dr=DMA((len(DIRECT), 3)), t_xs=DMA((2,)), t_xr=DMA((2,)), t_out=DMA((s,)), s_out=DMA((3,)),
        free=REG((len(FREE),)), free_r=REG((s,)), free_l=REG((s,)),
    )


def whole_kernel(*refs):
    (acts_h, cot_h, attn_h, extra_h, in_h, out_h, gain_in, seg_in) = refs[:8]
    (res_o, grad_o, attn_o, extra_o, gin_o, gout_o, gain_o) = refs[8:15]
    R = type("Refs", (), {})()
    for name, ref in zip(scratch_list(), refs[15:]):
        setattr(R, name, ref)
    src = {"attn": attn_h, "extra": extra_h, "in": in_h, "out": out_h}
    dst = {"attn": attn_o, "extra": extra_o, "in": gin_o, "out": gout_o}
    buf = {"wide": R.wide, "tall": R.tall}
    ybuf = {"wide": R.y_wide, "tall": R.y_tall}

    R.acc = R.x
    hidT = R.kept.at[pl.ds(0, FF)]

    section = lax.axis_index("section")
    me = lax.axis_index("dp")
    z, y, c = me // 4, (me // 2) % 2, me % 2
    first, second = section == 0, section == 1
    at = lambda zz, yy, cc: {"dp": zz * 4 + yy * 2 + cc}
    right, left = at(lax.rem(z + 1, 4), y, c), at(lax.rem(z + 3, 4), y, c)
    z_peer = [at(lax.rem(z + k, 4), y, c) for k in (1, 2, 3)]
    y_peer, c_peer, x_peer = at(z, 1 - y, c), at(z, y, 1 - c), {"section": 1 - section}

    def remote(a, b, ss, rs, dev):
        return pltpu.make_async_remote_copy(a, b, ss, rs, device_id=dev, device_id_type=MESH)

    def local(a, b, s):
        return pltpu.make_async_copy(a, b, s)

    def when(cond, fn):
        pl.when(cond)(fn)

    barrier = pltpu.get_barrier_semaphore()
    everyone = z_peer + [y_peer, c_peer, x_peer]
    for peer in everyone:
        pl.semaphore_signal(barrier, inc=1, device_id=peer, device_id_type=MESH)
    pl.semaphore_wait(barrier, len(everyone))

    def spot(name):
        arg, lo, b, col, size = PARTS[name]
        return PART_NAMES.index(name), buf[b], pl.ds(col, size)

    def in_place(name):
        i, b, cs = spot(name)
        return b.at[z, y, c, :, cs]

    def shard(name):
        arg, lo, _, _, size = PARTS[name]
        return in_place(name) if arg is None else src[arg].at[:, pl.ds(lo, size)]

    def own_copy(name):
        return local(shard(name), in_place(name), R.s_own.at[PART_NAMES.index(name)])

    def line_block(name, zz, pair):
        i, b, cs = spot(name)
        return b.at[zz, :, c, :, cs] if pair else b.at[zz, y, c, :, cs]

    def go_right(name, s, pair):
        i = PART_NAMES.index(name)
        d = line_block(name, z - s, pair)
        return remote(shard(name) if s == 0 and not pair else d, d, R.s_rs.at[i, s], R.s_rr.at[i, s], right)

    def go_left(name, s, pair):
        i = PART_NAMES.index(name)
        d = line_block(name, z + s, pair)
        return remote(shard(name) if s == 0 and not pair else d, d, R.s_ls.at[i, s], R.s_lr.at[i, s], left)

    def from_left(name, s, pair):
        i = PART_NAMES.index(name)
        d = line_block(name, z - s, pair)
        return remote(d, d, R.s_rs.at[i, s - 1], R.s_rr.at[i, s - 1], left)

    def from_right(name, s, pair):
        i = PART_NAMES.index(name)
        d = line_block(name, z + s, pair)
        return remote(d, d, R.s_ls.at[i, s - 1], R.s_lr.at[i, s - 1], right)

    def across(name, zz, own=False, pair=False):
        i, b, cs = spot(name)
        d = b.at[zz, y, c, :, cs]
        k = 0 if pair else zz
        return remote(shard(name) if own else d, d, R.s_ys.at[i, k], R.s_yr.at[i, k], y_peer)

    def across_in(name, zz, pair=False):
        i, b, cs = spot(name)
        d = b.at[zz, 1 - y, c, :, cs]
        k = 0 if pair else zz
        return remote(d, d, R.s_ys.at[i, k], R.s_yr.at[i, k], y_peer)

    def to_core(name):
        i, b, cs = spot(name)
        d = b.at[:, :, c, :, cs]
        return remote(d, d, R.s_cs.at[i], R.s_cr.at[i], c_peer)

    def core_in(name):
        i, b, cs = spot(name)
        d = b.at[:, :, 1 - c, :, cs]
        return remote(d, d, R.s_cs.at[i], R.s_cr.at[i], c_peer)

    def ends(s, go, cond=None):
        when((z >= s) & (z < 3), lambda: go(0))
        when((z + s <= 3) & (z > 0), lambda: go(1))

    def begin(name, pair):
        if PARTS[name][0] is not None:
            own_copy(name).start()
        if name == "k0":
            kv_shard.wait_recv()
        if not pair:
            when(z < 3, lambda: go_right(name, 0, False).start())
            when(z > 0, lambda: go_left(name, 0, False).start())
        across(name, z, True, pair).start()

    def pair_turn(name):
        own_copy(name).wait()
        across_in(name, z, True).wait_recv()
        when(z < 3, lambda: go_right(name, 0, True).start())
        when(z > 0, lambda: go_left(name, 0, True).start())

    def hop(name, s, pair):
        def lower():
            from_left(name, s, pair).wait_recv()
            if s < 3:
                when(z < 3, lambda: go_right(name, s, pair).start())
            if not pair:
                across(name, z - s).start()

        def upper():
            from_right(name, s, pair).wait_recv()
            if s < 3:
                when(z > 0, lambda: go_left(name, s, pair).start())
            if not pair:
                across(name, z + s).start()

        when(z >= s, lower)
        when(z + s <= 3, upper)

    def line_done(name, pair):
        if not pair:
            if PARTS[name][0] is not None:
                own_copy(name).wait()
            for zz in range(4):
                across_in(name, zz).wait_recv()
        to_core(name).start()

    def have(*names):
        for name in names:
            core_in(name).wait_recv()

    def sent(name, pair):
        for s in range(3):
            when((z >= s) & (z < 3), lambda: go_right(name, s, pair).wait_send())
            when((z + s <= 3) & (z > 0), lambda: go_left(name, s, pair).wait_send())
        for zz in range(1 if pair else 4):
            across(name, zz, False, pair).wait_send()
        to_core(name).wait_send()

    def all_sent(who):
        line, pairs = ROUTES[who]
        for name in line:
            sent(name, False)
        for name in pairs.values():
            sent(name, True)

    def section_tick(who, t):
        line, pairs = ROUTES[who]
        n = len(line)
        for start, name in pairs.items():
            if t == start:
                begin(name, True)
            if t == start + 1:
                pair_turn(name)
            for s in (1, 2, 3):
                if t == start + 1 + s:
                    hop(name, s, True)
            if t == start + 5:
                line_done(name, True)
        if t < n:
            begin(line[t], False)
        for s in (1, 2, 3):
            if 0 <= t - s < n:
                hop(line[t - s], s, False)
        if 0 <= t - 4 < n:
            line_done(line[t - 4], False)

    def tick(t):
        when(first, lambda: section_tick(0, t))
        when(second, lambda: section_tick(1, t))

    kv_block = R.wide.at[z, y, c, :, pl.ds(KV, 2 * D)]
    kv_shard = remote(extra_h, kv_block, R.s_kx, R.s_kr, x_peer)
    when(first, lambda: kv_shard.start())

    share = gain_in.shape[1]
    spread = (
        lax.broadcasted_iota(jnp.int32, (share, D), 1) - me * share == lax.broadcasted_iota(jnp.int32, (share, D), 0)
    ).astype(F32)
    R.gz[z] = jnp.zeros((8, D), F32)
    R.gz[z, 0:3, :] = dot(gain_in[...], spread.astype(BF))
    x_in = local(acts_h, R.x, R.s_in.at[1])
    x_in.start()
    g_in = local(cot_h, R.g, R.s_in.at[2])
    g_in.start()

    def small_z(own_ref, slots, row):
        return [remote(own_ref, slots.at[z], R.s_gs.at[row, k], R.s_gr.at[row, k], z_peer[k]) for k in range(3)]

    def small_pair(slots, row, k, dev):
        return remote(slots.at[0], slots.at[1], R.s_gs.at[row, k], R.s_gr.at[row, k], dev)

    gzc = small_z(R.gz.at[z], R.gz, 0)
    for q in gzc:
        q.start()
    tick(0)
    tick(1)
    for q in gzc:
        q.wait_recv()
    R.gy[0] = (R.gz[0] + R.gz[1]) + (R.gz[2] + R.gz[3])
    q = small_pair(R.gy, 0, 3, y_peer)
    q.start()
    tick(2)
    q.wait()
    R.gc[0] = R.gy[0] + R.gy[1]
    q = small_pair(R.gc, 0, 4, c_peer)
    q.start()
    tick(3)
    q.wait()
    R.gain[...] = R.gc[0] + R.gc[1]
    for q in gzc:
        q.wait_send()
    gain = lambda k: R.gain[k : k + 1, :]

    ones = jnp.where(first, 1.0, 0.0)
    for img in range(MICRO):
        row = jnp.broadcast_to(seg_in[img : img + 1, :].astype(F32), (SEQ, SEQ))
        key = lax.broadcasted_iota(jnp.int32, (SEQ, SEQ), 0)
        query = lax.broadcasted_iota(jnp.int32, (SEQ, SEQ), 1)
        allowed = jnp.where((row.T == row) & (key <= query), 1.0, ones)
        R.mask[img] = allowed.astype(BF)
    R.dgain[...] = jnp.zeros_like(R.dgain)

    x_in.wait()
    norm_forward(R.x, gain(0), R.n1)
    for t in range(4, 6):
        tick(t)
    have("q0", "q1")
    project(R.n1, R.wide, QKV, R.qkv, 0, 3 * D, 768)
    tick(6)

    def self_attention(a, b):
        attend_forward(R.qkv, 0, R.qkv, D, R.qkv, 2 * D, R.ao, R.aoT, R.mask, a, b)

    self_attention(0, 4)
    tick(7)
    self_attention(4, 8)
    tick(8)
    self_attention(8, 12)
    tick(9)
    have("o")
    project_add(R.ao, R.wide, OP, R.x, R.mid, 384)

    def message(img):
        rows = pl.ds(img * SEQ, SEQ)
        return remote(R.xsend.at[rows], R.xin.at[rows], R.s_ms.at[img], R.s_mr.at[img], x_peer)

    def down(base, out, cols, first_row=0, count=ROWS):
        rows = pl.ds(first_row, count)
        for lo in cols:
            cs = pl.ds(lo, 256)
            out[rows, cs] = base[rows, cs] + dot(R.hid[rows, :], R.tall[:, :, :, :, cs].reshape(FF, 256))

    def round_g(to, first_row=0, count=ROWS):
        rows = pl.ds(first_row, count)
        to[rows, :] = R.g[rows, :].astype(BF)

    def enc_forward():
        norm_forward(R.mid, gain(1), R.n2)
        have("g0", "u0")
        gated_forward(R.n2, R.wide, R.gu, R.hid, 0, 1, tile=512)
        section_tick(0, 10)
        gated_forward(R.n2, R.wide, R.gu, R.hid, 1, 2, tile=512)
        have("g1", "u1")
        gated_forward(R.n2, R.wide, R.gu, R.hid, 1, 2, tile=1024)
        section_tick(0, 11)
        have("d0", "d1")
        down(R.mid, R.late, (0, 256))
        have("d2")
        for img in range(MICRO):
            down(R.mid, R.late, (512,), img * SEQ, SEQ)
            norm_forward(R.late, gain(2), R.xsend, img * SEQ, SEQ)
            message(img).start()
        all_sent(0)
        kv_shard.wait_send()

    def dec_forward():
        norm_forward(R.mid, gain(2), R.n3)
        section_tick(1, 10)
        have("x0")
        project(R.n3, R.wide, XA, R.xq, 0, D, 384)
        section_tick(1, 11)
        section_tick(1, 12)
        have("d0", "d1", "d2")
        g_in.wait()
        round_g(R.gb)
        hidden_grad(R.gb, R.tall, R.gu)
        section_tick(1, 13)
        have("x1", "k0", "k1")

        def cross(img):
            message(img).wait_recv()
            project(R.xin, R.wide, KV, R.kv, 0, 2 * D, 768, img * SEQ, SEQ)
            attend_forward(R.xq, 0, R.kv, 0, R.kv, D, R.ao, R.cmT, None, img * 6, img * 6 + 6, R.kept, 3)

        cross(0)
        section_tick(1, 14)
        cross(1)
        project_add(R.ao, R.wide, XB, R.mid, R.late, 384)
        norm_forward(R.late, gain(1), R.n2)
        have("g0", "u0", "g1", "u1")
        gated_both(R.n2, R.wide, R.gu, R.hid, 0, 2, 1024)
        all_sent(1)

    def sum_spot(name):
        b, lo, size = SUMS[name]
        return SUM_NAMES.index(name), b, pl.ds(lo, size), size

    stage_of = {}

    def core_copy(name):
        k, b, cs, size = sum_spot(name)
        if b == "tall":
            s = R.stage_tall.at[:, :, :, cs]
        else:
            s = R.stage.at[stage_of[name], :, :, :, pl.ds(0, size)]
        return remote(s, buf[b].at[:, :, c, :, cs], R.t_cs.at[k], R.t_cr.at[k], c_peer)

    def paired(name):
        return name in PAIRED

    def y_copy(name):
        k, b, cs, size = sum_spot(name)
        if paired(name):
            return remote(buf[b].at[z, 1 - y, c, :, cs], ybuf[b].at[0, :, cs], R.t_ys.at[k], R.t_yr.at[k], y_peer)
        return remote(buf[b].at[:, 1 - y, c, :, cs], ybuf[b].at[:, :, cs], R.t_ys.at[k], R.t_yr.at[k], y_peer)

    def moving(name, a, e):
        _, b, cs, _ = sum_spot(name)
        return buf[b].at[a:e, :, c, :, cs] if paired(name) else buf[b].at[a:e, y, c, :, cs]

    def landing_left(name, a, e):
        _, b, cs, _ = sum_spot(name)
        return buf[b].at[a:e, :, 1 - c, :, cs] if paired(name) else buf[b].at[a:e, 0, 1 - c, :, cs]

    def landing_right(name, a, e):
        _, b, cs, size = sum_spot(name)
        if paired(name):
            return R.pair_in.at[PAIRED.index(name), a:e]
        return buf[b].at[a:e, 1, 1 - c, :, cs]

    def right_copy(name, zz):
        k = SUM_NAMES.index(name)
        return remote(moving(name, zz + 1, 4), landing_left(name, zz + 1, 4), R.t_rs.at[k], R.t_rr.at[k], right)

    def left_copy(name, zz):
        k = SUM_NAMES.index(name)
        return remote(moving(name, 0, zz), landing_right(name, 0, zz), R.t_ls.at[k], R.t_lr.at[k], left)

    def send_right(name, zz):
        pl.semaphore_wait(R.free_r.at[SUM_NAMES.index(name)], 1)
        right_copy(name, zz).start()

    def send_left(name, zz):
        pl.semaphore_wait(R.free_l.at[SUM_NAMES.index(name)], 1)
        left_copy(name, zz).start()

    def add_blocks(name, landed, a, e):
        mine = moving(name, a, e)

        @pl.loop(0, e - a)
        def _(j):
            mine[j] = (mine[j].astype(F32) + landed[j].astype(F32)).astype(BF)

    def add_left(name, zz):
        k = SUM_NAMES.index(name)
        d = landing_left(name, zz, 4)
        remote(d, d, R.t_rs.at[k], R.t_rr.at[k], left).wait_recv()
        add_blocks(name, d, zz, 4)

    def add_right(name, zz):
        k = SUM_NAMES.index(name)
        d = landing_right(name, 0, zz + 1)
        remote(d, d, R.t_ls.at[k], R.t_lr.at[k], right).wait_recv()
        add_blocks(name, d, 0, zz + 1)

    def open_line(name):
        k = SUM_NAMES.index(name)
        if name in DIRECT:
            for peer in z_peer:
                pl.semaphore_signal(R.free_r.at[k], inc=1, device_id=peer, device_id_type=MESH)
            return
        when(z > 0, lambda: pl.semaphore_signal(R.free_r.at[k], inc=1, device_id=left, device_id_type=MESH))
        when(z < 3, lambda: pl.semaphore_signal(R.free_l.at[k], inc=1, device_id=right, device_id_type=MESH))

    def straight(name):
        k, b, cs, size = sum_spot(name)
        d, w = DIRECT.index(name), buf[b]
        return [
            remote(
                w.at[lax.rem(z + j + 1, 4), y, c, :, cs], w.at[z, 0, 1 - c, :, cs], R.t_ds.at[d, j], R.t_dr.at[d, j], z_peer[j]
            )
            for j in range(3)
        ]

    def collect(name):
        k, b, cs, size = sum_spot(name)
        d, w = DIRECT.index(name), buf[b]
        total = w[z, y, c, :, cs].astype(F32)
        for j in range(3):
            landed = w.at[lax.rem(z + 3 - j, 4), 0, 1 - c, :, cs]
            remote(landed, landed, R.t_ds.at[d, j], R.t_dr.at[d, j], z_peer[2 - j]).wait_recv()
            total = total + landed[...].astype(F32)
        finish(name, total)

    def line_a(name):
        when(z == 0, lambda: send_right(name, 0))
        when(z == 3, lambda: send_left(name, 3))

    def line_b(name):
        def one():
            add_left(name, 1)
            send_right(name, 1)

        def two():
            add_right(name, 2)
            send_left(name, 2)

        when(z == 1, one)
        when(z == 2, two)

    def line_c(name):
        def one():
            add_right(name, 1)
            send_left(name, 1)

        def two():
            add_left(name, 2)
            send_right(name, 2)

        when(z == 1, one)
        when(z == 2, two)

    def line_d(name):
        when(z == 0, lambda: add_right(name, 0))
        when(z == 3, lambda: add_left(name, 3))

    def line_sent(name):
        if name in DIRECT:
            for q in straight(name):
                q.wait_send()
            return
        for zz in range(3):
            when(z == zz, lambda: right_copy(name, zz).wait_send())
            when(z == zz + 1, lambda: left_copy(name, zz + 1).wait_send())

    def release(name):
        pl.semaphore_signal(R.free.at[FREE[name]], inc=1, device_id=c_peer, device_id_type=MESH)

    def claim(name):
        pl.semaphore_wait(R.free.at[FREE[name]], 1)

    order = []

    def grad_wide(name, nT, g_ref, gcol, tile):
        k, b, cs, size = sum_spot(name)
        lo = SUMS[name][1]
        slot = len(order) % 2
        if len(order) >= 2:
            core_copy(order[-2]).wait_send()
        stage_of[name] = slot
        order.append(name)
        lhs = half_rows(nT, 1 - c)

        @pl.loop(0, size // tile)
        def _(j):
            w = dot(lhs, g_ref[:, pl.ds(mul(gcol + j * tile, 128), tile)]).astype(BF)
            R.stage[slot, :, :, :, pl.ds(mul(j * tile, 128), tile)] = w.reshape(4, 2, 48, tile)

        core_copy(name).start()
        mine = half_rows(nT, c)

        @pl.loop(0, size // tile)
        def _(j):
            w = dot(mine, g_ref[:, pl.ds(mul(gcol + j * tile, 128), tile)]).astype(BF)
            R.wide[:, :, c, :, pl.ds(mul(lo + j * tile, 128), tile)] = w.reshape(4, 2, 48, tile)

    def drain():
        for name in order[-2:]:
            core_copy(name).wait_send()
        order.clear()

    def grad_tall(name):
        k, b, cs, size = sum_spot(name)

        def rows_of(j, cc):
            units = [hidT[pl.ds(mul((8 * j + 2 * i + cc) * 128, 128), 128), :] for i in range(4)]
            return dot(jnp.concatenate(units, axis=0), R.gb[:, cs]).astype(BF).reshape(2, 2, 128, size)

        @pl.loop(0, 2)
        def _(j):
            R.stage_tall[pl.ds(2 * j, 2), :, :, cs] = rows_of(j, 1 - c)

        core_copy(name).start()

        @pl.loop(0, 2)
        def _(j):
            R.tall[pl.ds(2 * j, 2), :, c, :, cs] = rows_of(j, c)

    ready, crossing, moving_on, finished = [], [], [], []

    def feed():
        while ready and len(crossing) < 3:
            name = ready.pop(0)
            y_copy(name).start()
            crossing.append(name)

    def core_stage(name, pass_on=True):
        k, b, cs, size = sum_spot(name)
        w = buf[b]
        landed = w.at[:, :, 1 - c, :, cs]
        remote(landed, landed, R.t_cs.at[k], R.t_cr.at[k], c_peer).wait_recv()

        @pl.loop(0, 8)
        def _(j):
            own = w[j // 2, j % 2, c, :, cs].astype(F32)
            w[j // 2, j % 2, c, :, cs] = (own + w[j // 2, j % 2, 1 - c, :, cs].astype(F32)).astype(BF)

        if pass_on:
            enter(name)

    def enter(name):
        open_line(name)
        if paired(name):
            line_a(name)
            moving_on.append([name, later, line_b, later, line_c, later, line_d, late_cross])
        else:
            ready.append(name)
            feed()

    def later(name):
        pass

    def late_cross(name):
        y_copy(name).start()
        crossing.append(name)

    def y_stage(name):
        k, b, cs, size = sum_spot(name)
        w, r = buf[b], ybuf[b]
        if paired(name):
            d = r.at[0, :, cs]
            remote(d, d, R.t_ys.at[k], R.t_yr.at[k], y_peer).wait_recv()
            finish(name, w[z, y, c, :, cs].astype(F32) + r[0, :, cs].astype(F32))
            return
        y_copy(name).wait_recv()

        @pl.loop(0, 4)
        def _(j):
            w[j, y, c, :, cs] = (w[j, y, c, :, cs].astype(F32) + r[j, :, cs].astype(F32)).astype(BF)

        if name in DIRECT:
            pl.semaphore_wait(R.free_r.at[k], 3)
            for q in straight(name):
                q.start()
            moving_on.append([name, later, collect])
            return
        line_a(name)
        moving_on.append([name, later, line_b, later, line_c, later, line_d, last])

    def last(name):
        k, b, cs, size = sum_spot(name)
        finish(name, buf[b][z, y, c, :, cs].astype(F32))

    def turn():
        going = list(moving_on)
        if crossing:
            name = crossing.pop(0)
            y_stage(name)
            feed()
        for item in going:
            item.pop(1)(item[0])
            if len(item) == 1:
                moving_on.remove(item)

    def out_copy(name):
        k, b, cs, size = sum_spot(name)
        arg, lo = OUT_OF[name]
        kind = [f for f in finished if SUMS[f][0] == b]
        slot = kind.index(name) % 2
        f = R.fin_tall.at[slot] if b == "tall" else R.fin.at[slot, :, pl.ds(0, size)]
        return local(f, dst[arg].at[:, pl.ds(lo, size)], R.t_out.at[k])

    def finish(name, total):
        k, b, cs, size = sum_spot(name)
        kind = [f for f in finished if SUMS[f][0] == b]
        slot = len(kind) % 2
        if len(kind) >= 2:
            out_copy(kind[-2]).wait()
        finished.append(name)
        if b == "tall":
            R.fin_tall[slot] = total
        else:
            R.fin[slot, :, pl.ds(0, size)] = total
        out_copy(name).start()

    def over_copy(j):
        k, b, cs, size = sum_spot(("k0", "k1")[j])
        return remote(
            R.wide.at[:, :, c, :, cs], R.wide.at[:, :, c, :, pl.ds(XA + j * D, D)], R.t_xs.at[j], R.t_xr.at[j], x_peer
        )

    def project_back(g_ref, wcol, out_ref):
        out_ref[...] = dot(g_ref[...], wide_cols(R.wide, wcol, D), NT).astype(BF)

    def down_grads():
        release("out")
        claim("out")
        grad_tall("out0")
        core_stage("out0")
        grad_tall("out1")
        core_stage("out1")

    def in_grads():
        release("in")
        claim("in")
        grad_wide("in0", R.nT, R.gu, 0, 512)
        grad_wide("in1", R.nT, R.gu, 1024, 512)
        core_stage("in0")
        grad_wide("in2", R.nT, R.gu, FF, 512)
        core_stage("in1")
        grad_wide("in3", R.nT, R.gu, FF + 1024, 512)
        core_stage("in2")

    gains_own = lambda: small_pair(R.hc, 1, 4, c_peer)
    gains_row = lambda: small_pair(R.hy, 1, 3, y_peer)
    gains_line = lambda: small_z(R.gain, R.hz, 1)
    gain_copy = local(R.gout, gain_o, R.s_out.at[2])
    grad_copy = local(R.g, grad_o, R.s_out.at[1])

    def gains_a():
        R.hc[0] = R.dgain[...]
        gains_own().start()

    def gains_b(_):
        gains_own().wait()
        R.hy[0] = R.hc[0] + R.hc[1]
        gains_row().start()

    def gains_c(_):
        gains_row().wait()
        R.gain[...] = R.hy[0] + R.hy[1]
        for q in gains_line():
            q.start()

    def gains_d(_):
        for q in gains_line():
            q.wait()
        R.hz[z] = R.gain[...]
        whole = (R.hz[0] + R.hz[1]) + (R.hz[2] + R.hz[3])
        own = lax.dot_general(whole, spread, NT, precision=lax.Precision.HIGHEST, preferred_element_type=F32)
        R.gout[...] = own[0:3]
        gain_copy.start()

    dec_res = local(R.acc, res_o, R.s_out.at[0])
    enc_res = local(R.late, res_o, R.s_out.at[0])

    def dec_middle():
        back_project(R.gu, 0, R.wide, WIN, 2 * FF, 2048, R.acc)
        norm_backward(R.late, gain(1), R.acc, R.g, R.dgain, 1, low_ref=R.gb2)
        project_back(R.gb2, XB, R.xsend)
        for img in range(MICRO):
            attend_backward(
                R.xq, 0, R.kv, 0, R.kv, D, R.xsend, None, R.xq, 0, R.kv, 0, R.kv, D, img * 6, img * 6 + 6, R.kept
            )
            back_project(R.kv, 0, R.wide, KV, 2 * D, 768, R.acc, img * SEQ, SEQ)
            rows = pl.ds(img * SEQ, SEQ)
            R.xsend[rows, :] = R.acc[rows, :].astype(BF)
            message(img).start()
        down(R.late, R.acc, (0, 256, 512))
        dec_res.start()
        transpose_to(R.hid, hidT)

    def dec_all():
        dec_forward()
        dec_middle()

    def enc_middle():
        enc_res.start()
        transpose_to(R.hid, hidT)
        transpose_to(R.n2, R.nT)
        g_in.wait()
        for img in range(MICRO):
            message(img).wait_send()
        for img in range(MICRO):
            lo = img * SEQ
            message(img).wait_recv()
            norm_backward(R.late, gain(2), R.xin, R.g, R.dgain, 2, lo, SEQ, R.gb)
            gated_backward(R.gb, R.tall, R.gu, lo, SEQ)

    def enc_in():
        back_project(R.gu, 0, R.wide, WIN, 2 * FF, 2048, R.acc)
        norm_backward(R.mid, gain(1), R.acc, R.g, R.dgain, 1, low_ref=R.gb2)

    def dec_keys():
        release("k")
        transpose_to(R.xin, R.nT)
        claim("k")
        grad_wide("k0", R.nT, R.kv, 0, 384)
        grad_wide("k1", R.nT, R.kv, D, 384)
        core_stage("k0", False)
        over_copy(0).start()
        core_stage("k1", False)
        over_copy(1).start()
        drain()
        transpose_to(R.n2, R.nT)

    def dec_cross():
        dec_res.wait()
        back_project(R.xq, 0, R.wide, XA, D, 768, R.acc)
        release("x")
        transpose_to(R.n3, R.nT)
        claim("x")
        grad_wide("x0", R.nT, R.xq, 0, 384)
        grad_wide("x1", R.cmT, R.gb2, 0, 384)
        core_stage("x0", False)
        core_stage("x1", False)
        norm_backward(R.mid, gain(2), R.acc, R.g, R.dgain, 2, low_ref=R.gb2)
        for img in range(MICRO):
            message(img).wait_send()
        drain()

    when(first, enc_forward)
    when(second, dec_all)
    when(first, enc_middle)
    down_grads()
    when(first, enc_in)
    when(second, dec_keys)
    in_grads()
    drain()
    core_stage("in3")
    when(second, dec_cross)

    when(first, lambda: enc_res.wait())
    x_again = local(acts_h, R.late, R.s_in.at[1])
    x_again.start()
    project_back(R.gb2, OP, R.ao)
    release("o")
    claim("o")
    grad_wide("o", R.aoT, R.gb2, 0, 384)
    turn()
    attend_backward(R.qkv, 0, R.qkv, D, R.qkv, 2 * D, R.ao, R.mask, R.qkv, 0, R.qkv, D, R.qkv, 2 * D, 0, 6)
    core_stage("o")
    turn()
    attend_backward(R.qkv, 0, R.qkv, D, R.qkv, 2 * D, R.ao, R.mask, R.qkv, 0, R.qkv, D, R.qkv, 2 * D, 6, 12)
    turn()
    back_project(R.qkv, 0, R.wide, QKV, 3 * D, 768, R.acc)
    release("q")
    transpose_to(R.n1, R.nT)
    claim("q")
    for j in range(2):
        when(first, lambda: over_copy(j).wait_recv())
        enter(("x0", "x1")[j])
    grad_wide("q0", R.nT, R.qkv, 0, 384)
    grad_wide("q1", R.nT, R.qkv, D, 384)
    core_stage("q0")
    grad_wide("q2", R.nT, R.qkv, 2 * D, 384)
    core_stage("q1")
    grad_wide("q3", R.nT, R.qkv, 2 * D + 384, 384)
    core_stage("q2")
    core_stage("q3")
    turn()
    x_again.wait()
    norm_backward(R.late, gain(0), R.acc, R.g, R.dgain, 0)
    grad_copy.start()
    gains_a()
    moving_on.append(["gains", gains_b, later, later, later, gains_c, later, later, gains_d])
    while ready or crossing or moving_on:
        turn()
    for name in ("out0", "out1"):
        core_copy(name).wait_send()
    drain()
    for name in finished:
        y_copy(name).wait_send()
        line_sent(name)
    for b in ("tall", "wide"):
        for name in [f for f in finished if SUMS[f][0] == b][-2:]:
            out_copy(name).wait()
    when(second, lambda: [over_copy(j).wait_send() for j in range(2)] and None)
    grad_copy.wait()
    gain_copy.wait()


def from_behind(block, axis, distance):
    devices = range(lax.axis_size(axis))
    route = [(i - distance, i) for i in devices if i - distance in devices]
    return lax.ppermute(block, axis, route)


def rms_norm(activations, gain_row):
    return (
        activations
        * lax.rsqrt(jnp.mean(activations * activations, axis=-1, keepdims=True) + 1e-06)
        * gain_row
    )


def product(left_side, right_side):
    return jnp.dot(left_side, right_side, preferred_element_type=jnp.float32)


def weight_grad(left_side, right_side):
    return jnp.einsum("sd,se->de", left_side, right_side, preferred_element_type=jnp.float32)


def input_back(gradient, weight):
    return jnp.einsum("se,de->sd", gradient, weight, preferred_element_type=jnp.float32)


def norm_back(activations, gain_row, gradient):
    _, pull_back = jax.vjp(rms_norm, activations, gain_row)
    return pull_back(gradient)


def heads_of(activations):
    return activations.reshape(activations.shape[0], HEADS, HDIM)


def logits_of(queries, keys_in, allowed):
    raw_logits = jnp.einsum(
        "qhd,khd->hqk", heads_of(queries), heads_of(keys_in), preferred_element_type=jnp.float32
    ) * HDIM ** (-0.5)
    if allowed is None:
        return raw_logits
    return jnp.where(allowed[None], raw_logits, -1e30)


def attend_plain(queries, keys_in, values, allowed):
    logits = logits_of(queries, keys_in, allowed)
    row_peak = jnp.max(logits, axis=-1, keepdims=True)
    weights = jnp.exp(logits - row_peak)
    row_total = jnp.sum(weights, axis=-1, keepdims=True)
    softmax_out = (weights / row_total).astype(jnp.bfloat16)
    mixed_heads = jnp.einsum(
        "hqk,khd->qhd", softmax_out, heads_of(values), preferred_element_type=jnp.float32
    )
    return (
        mixed_heads.reshape(queries.shape[0], D).astype(jnp.bfloat16),
        row_peak + jnp.log(row_total),
    )


def attend_plain_back(queries, keys_in, values, allowed, log_total, grad_mixed):
    softmax_out = jnp.exp(logits_of(queries, keys_in, allowed) - log_total)
    grad_heads = heads_of(grad_mixed)
    grad_softmax = jnp.einsum(
        "qhd,khd->hqk", grad_heads, heads_of(values), preferred_element_type=jnp.float32
    )
    grad_values = jnp.einsum(
        "hqk,qhd->khd",
        softmax_out.astype(jnp.bfloat16),
        grad_heads,
        preferred_element_type=jnp.float32,
    )
    inner_sum = jnp.sum(softmax_out * grad_softmax, axis=-1, keepdims=True)
    grad_logits = (softmax_out * (grad_softmax - inner_sum) * HDIM ** (-0.5)).astype(jnp.bfloat16)
    grad_queries = jnp.einsum(
        "hqk,khd->qhd", grad_logits, heads_of(keys_in), preferred_element_type=jnp.float32
    )
    grad_keys = jnp.einsum(
        "hqk,qhd->khd", grad_logits, heads_of(queries), preferred_element_type=jnp.float32
    )
    query_count = queries.shape[0]
    key_count = keys_in.shape[0]
    return (
        grad_queries.reshape(query_count, D),
        grad_keys.reshape(key_count, D),
        grad_values.reshape(key_count, D),
    )


def self_forward(inputs, gain_row, w_attn, allowed):
    normed = rms_norm(inputs, gain_row).astype(jnp.bfloat16)
    packed = product(normed, w_attn[:, : 3 * D]).astype(jnp.bfloat16)
    mixed_heads, log_total = attend_plain(
        packed[:, :D], packed[:, D : 2 * D], packed[:, 2 * D :], allowed
    )
    return (
        inputs + product(mixed_heads, w_attn[:, 3 * D :]),
        (normed, packed, mixed_heads, log_total),
    )


def self_backward(inputs, gain_row, w_attn, allowed, kept_values, grad_result):
    normed, packed, mixed_heads, log_total = kept_values
    grad_low = grad_result.astype(jnp.bfloat16)
    grad_proj = weight_grad(mixed_heads, grad_low)
    grad_mixed = input_back(grad_low, w_attn[:, 3 * D :]).astype(jnp.bfloat16)
    grad_queries, grad_keys, grad_values = attend_plain_back(
        packed[:, :D], packed[:, D : 2 * D], packed[:, 2 * D :], allowed, log_total, grad_mixed
    )
    grad_packed = jnp.concatenate([grad_queries, grad_keys, grad_values], axis=1).astype(
        jnp.bfloat16
    )
    grad_qkv = weight_grad(normed, grad_packed)
    grad_inputs, grad_gain = norm_back(
        inputs, gain_row, input_back(grad_packed, w_attn[:, : 3 * D])
    )
    return (grad_result + grad_inputs, grad_gain, jnp.concatenate([grad_qkv, grad_proj], axis=1))


def gated_unit(gated):
    return jax.nn.gelu(gated[:, :FF], approximate=True) * gated[:, FF:]


def ffn_forward(inputs, gain_row, w_in, w_out):
    normed = rms_norm(inputs, gain_row).astype(jnp.bfloat16)
    gated = product(normed, w_in)
    hidden = gated_unit(gated).astype(jnp.bfloat16)
    return (inputs + product(hidden, w_out), (normed, gated, hidden))


def ffn_backward(inputs, gain_row, w_in, w_out, kept_values, grad_result):
    normed, gated, hidden = kept_values
    grad_low = grad_result.astype(jnp.bfloat16)
    grad_wout = weight_grad(hidden, grad_low)
    _, pull_back = jax.vjp(gated_unit, gated)
    grad_gated = pull_back(input_back(grad_low, w_out))[0].astype(jnp.bfloat16)
    grad_win = weight_grad(normed, grad_gated)
    grad_inputs, grad_gain = norm_back(inputs, gain_row, input_back(grad_gated, w_in))
    return (grad_result + grad_inputs, grad_gain, grad_win, grad_wout)


def encoder_forward(inputs, weights):
    w_attn, w_extra, w_in, w_out, gain_rows = weights
    middle, first_kept = self_forward(inputs, gain_rows[0], w_attn, None)
    result, second_kept = ffn_forward(middle, gain_rows[1], w_in, w_out)
    normed = rms_norm(result, gain_rows[2]).astype(jnp.bfloat16)
    cross_kv = product(normed, w_extra).astype(jnp.bfloat16)
    return (result, cross_kv, (middle, first_kept, second_kept, normed))


def encoder_backward(inputs, weights, grad_result, grad_kv):
    w_attn, w_extra, w_in, w_out, gain_rows = weights
    result, _, kept_values = encoder_forward(inputs, weights)
    middle, first_kept, second_kept, normed = kept_values
    grad_extra = weight_grad(normed, grad_kv)
    grad_final, gain_final = norm_back(result, gain_rows[2], input_back(grad_kv, w_extra))
    grad_middle, gain_late, grad_win, grad_wout = ffn_backward(
        middle, gain_rows[1], w_in, w_out, second_kept, grad_result + grad_final
    )
    grad_inputs, gain_early, grad_attn = self_backward(
        inputs, gain_rows[0], w_attn, None, first_kept, grad_middle
    )
    return (
        grad_inputs,
        (
            grad_attn,
            grad_extra,
            grad_win,
            grad_wout,
            jnp.stack([gain_early, gain_late, gain_final]),
        ),
    )


def decoder_step(inputs, cross_kv, allowed, weights, grad_result):
    w_attn, w_extra, w_in, w_out, gain_rows = weights
    middle, first_kept = self_forward(inputs, gain_rows[0], w_attn, allowed)
    query_in = rms_norm(middle, gain_rows[2]).astype(jnp.bfloat16)
    queries = product(query_in, w_extra[:, :D]).astype(jnp.bfloat16)
    mixed_heads, log_total = attend_plain(queries, cross_kv[:, :D], cross_kv[:, D:], None)
    after_cross = middle + product(mixed_heads, w_extra[:, D:])
    result, second_kept = ffn_forward(after_cross, gain_rows[1], w_in, w_out)
    grad_after, gain_late, grad_win, grad_wout = ffn_backward(
        after_cross, gain_rows[1], w_in, w_out, second_kept, grad_result
    )
    grad_low = grad_after.astype(jnp.bfloat16)
    grad_cross_out = weight_grad(mixed_heads, grad_low)
    grad_mixed = input_back(grad_low, w_extra[:, D:]).astype(jnp.bfloat16)
    grad_queries, grad_keys, grad_values = attend_plain_back(
        queries, cross_kv[:, :D], cross_kv[:, D:], None, log_total, grad_mixed
    )
    grad_queries = grad_queries.astype(jnp.bfloat16)
    grad_cross_in = weight_grad(query_in, grad_queries)
    grad_normed, gain_cross = norm_back(
        middle, gain_rows[2], input_back(grad_queries, w_extra[:, :D])
    )
    grad_inputs, gain_early, grad_attn = self_backward(
        inputs, gain_rows[0], w_attn, allowed, first_kept, grad_after + grad_normed
    )
    grad_kv = jnp.concatenate([grad_keys, grad_values], axis=1).astype(jnp.bfloat16)
    gradients = (
        grad_attn,
        jnp.concatenate([grad_cross_in, grad_cross_out], axis=1),
        grad_win,
        grad_wout,
        jnp.stack([gain_early, gain_late, gain_cross]),
    )
    return (result, grad_inputs, grad_kv, gradients)


def general(acts, w_attn, w_extra, w_in, w_out, gains, segments, cotangent):
    gathered = (
        lax.all_gather(w_attn[0], "dp", axis=0, tiled=True),
        lax.all_gather(w_extra[0], "dp", axis=0, tiled=True),
        lax.all_gather(w_in[0], "dp", axis=0, tiled=True),
        lax.all_gather(w_out[0], "dp", axis=0, tiled=True),
        lax.all_gather(gains[0], "dp", axis=1, tiled=True),
    )
    weights = gathered[:4] + (gathered[4].astype(jnp.float32),)
    inputs = acts[0, :, 0]
    upstream = cotangent[0, :, 0]
    is_first = lax.axis_index("section") == 0
    positions = jnp.arange(SEQ)
    causal = positions[None, :] <= positions[:, None]
    zero_message = jnp.zeros((SEQ, 2 * D), jnp.bfloat16)
    zero_grads = tuple((jnp.zeros(weight.shape, jnp.float32) for weight in weights))
    carried = (jnp.zeros((MICRO, SEQ, D), jnp.float32), jnp.zeros((MICRO, SEQ, D), jnp.float32))
    received = zero_message
    returned = zero_message
    totals = zero_grads
    moments = MICRO + 2
    for moment in range(moments):

        def first_section(carried, received, returned):
            results, grad_inputs = carried
            message = zero_message
            fresh_grads = zero_grads
            if moment < MICRO:
                result, message, _ = encoder_forward(inputs[moment], weights)
                results = results.at[moment].set(result)
            if moment >= 2:
                grad_rows, fresh_grads = encoder_backward(
                    inputs[moment - 2], weights, upstream[moment - 2], returned
                )
                grad_inputs = grad_inputs.at[moment - 2].set(grad_rows)
            return ((results, grad_inputs), message, zero_message, fresh_grads)

        def second_section(carried, received, returned):
            results, grad_inputs = carried
            message = zero_message
            fresh_grads = zero_grads
            if 1 <= moment <= MICRO:
                segment_ids = segments[moment - 1, 0]
                allowed = (segment_ids[:, None] == segment_ids[None, :]) & causal
                result, grad_rows, message, fresh_grads = decoder_step(
                    inputs[moment - 1], received, allowed, weights, upstream[moment - 1]
                )
                results = results.at[moment - 1].set(result)
                grad_inputs = grad_inputs.at[moment - 1].set(grad_rows)
            return ((results, grad_inputs), zero_message, message, fresh_grads)

        carried, forward_message, back_message, fresh_grads = lax.cond(
            is_first, first_section, second_section, carried, received, returned
        )
        if moment < MICRO:
            received = from_behind(forward_message, "section", 1)
        if 1 <= moment <= MICRO:
            returned = from_behind(back_message, "section", -1)
        if moment >= 1:
            totals = tuple((jnp.add(*couple) for couple in zip(totals, fresh_grads)))
    results, grad_inputs = carried
    final = (
        lax.psum_scatter(totals[0], "dp", scatter_dimension=0, tiled=True),
        lax.psum_scatter(totals[1], "dp", scatter_dimension=0, tiled=True),
        lax.psum_scatter(totals[2], "dp", scatter_dimension=0, tiled=True),
        lax.psum_scatter(totals[3], "dp", scatter_dimension=0, tiled=True),
        lax.psum_scatter(totals[4], "dp", scatter_dimension=1, tiled=True),
    )
    return (
        results[None, :, None],
        grad_inputs[None, :, None],
        final[0][None],
        final[1][None],
        final[2][None],
        final[3][None],
        final[4][None],
    )


def step(acts, w_attn, w_extra, w_in, w_out, gains, segments, cotangent):
    anywhere = pl.BlockSpec(memory_space=pl.ANY)
    shape = lambda *s: jax.ShapeDtypeStruct(s, F32)
    scratch = scratch_list()
    held = pl.pallas_call(
        whole_kernel,
        out_shape=(
            shape(ROWS, D), shape(ROWS, D), shape(48, 4 * D), shape(48, 2 * D), shape(48, 2 * FF), shape(128, D), shape(3, 48),
        ),
        in_specs=[anywhere] * 6 + [pl.BlockSpec(memory_space=pltpu.VMEM)] * 2,
        out_specs=[anywhere] * 7,
        scratch_shapes=list(scratch.values()),
        compiler_params=pltpu.CompilerParams(
            collective_id=0, has_side_effects=True, vmem_limit_bytes=63 * 2**20
        ),
    )(
        acts.reshape(ROWS, D), cotangent.reshape(ROWS, D), w_attn[0], w_extra[0], w_in[0], w_out[0], gains[0],
        segments.reshape(MICRO, SEQ),
    )
    results, input_grad, attn, extra, win, wout, grad_gains = held
    like = (1, MICRO, 1, SEQ, D)
    return (
        results.reshape(like), input_grad.reshape(like), attn[None], extra[None], win[None], wout[None], grad_gains[None],
    )


def solution(mesh):
    in_specs = (
        P("section", None, "dp", None, None),
        P("section", "dp", None),
        P("section", "dp", None),
        P("section", "dp", None),
        P("section", "dp", None),
        P("section", None, "dp"),
        P(None, "dp", None),
        P("section", None, "dp", None, None),
    )
    out_specs = (
        P("section", None, "dp", None, None),
        P("section", None, "dp", None, None),
        P("section", "dp", None),
        P("section", "dp", None),
        P("section", "dp", None),
        P("section", "dp", None),
        P("section", None, "dp"),
    )
    fits = mesh.shape["dp"] == 16
    return jax.shard_map(step if fits else general, mesh=mesh, in_specs=in_specs, out_specs=out_specs, check_vma=False)
```

```python
import jax
import jax.numpy as jnp
from jax import lax
from jax.experimental import pallas as pl
from jax.experimental.pallas import tpu as pltpu
from jax.sharding import PartitionSpec as P

D=768; HEADS=12; HDIM=64; FF=2048; SEQ=256; MICRO=2
ROWS=MICRO*SEQ
BF=jnp.bfloat16; F32=jnp.float32
QKV, OP, XA, XB, WIN, KV = 0, 3*D, 4*D, 5*D, 6*D, 6*D+2*FF
WIDE = KV + 2*D
NN=(((1,),(0,)),((),())); NT=(((1,),(1,)),((),()))

def mul(start, k): return pl.multiple_of(start, k)
def dot(a,b,dims=NN): return lax.dot_general(a,b,dims,preferred_element_type=F32)

def wide_cols(wa, start, size):
    return wa[:, :, :, :, pl.ds(start, size)].reshape(D, size)

def rms_rows(v):
    return lax.rsqrt(jnp.mean(v*v, axis=-1, keepdims=True) + 1e-6)

def norm_forward(v_ref, gain, n_ref, first=0, count=ROWS):
    @pl.loop(0, count//64)
    def _(i):
        rows=pl.ds(mul(first+i*64,64),64)
        v=v_ref[rows,:]
        n_ref[rows,:]=(v*rms_rows(v)*gain).astype(BF)

def norm_backward(v_ref, gain, dn_ref, g_ref, dgain_ref, slot, first=0, count=ROWS, low_ref=None):
    def body(i, acc):
        rows=pl.ds(mul(first+i*64,64),64)
        v=v_ref[rows,:]; dn=dn_ref[rows,:].astype(F32)
        r=rms_rows(v)
        t=dn*gain
        vr=v*r
        g=g_ref[rows,:]+r*(t-vr*jnp.mean(t*vr,axis=-1,keepdims=True))
        g_ref[rows,:]=g
        if low_ref is not None:
            low_ref[rows,:]=g.astype(BF)
        return acc+jnp.sum(dn*vr,axis=0,keepdims=True)
    acc=lax.fori_loop(0,count//64,body,jnp.zeros((1,D),F32))
    dgain_ref[slot:slot+1,:]+=acc

def transpose_to(src_ref, dst_ref, first=0, count=ROWS):
    cols=src_ref.shape[1]
    @pl.loop(0, cols//128)
    def _(j):
        cs=pl.ds(mul(j*128,128),128)
        dst_ref[cs, pl.ds(first,count)] = src_ref[pl.ds(first,count),cs].T

def project(n_ref, wa, wcol, out_ref, ocol, total, tile, first=0, count=ROWS):
    @pl.loop(0, total//tile)
    def _(j):
        w=wide_cols(wa, mul(wcol+j*tile,128), tile)
        out_ref[pl.ds(first,count), pl.ds(mul(ocol+j*tile,128),tile)] = dot(n_ref[pl.ds(first,count),:], w).astype(out_ref.dtype)

def project_add(a_ref, wa, wcol, base_ref, out_ref, tile, first=0, count=ROWS):
    rows=pl.ds(first,count)
    @pl.loop(0, D//tile)
    def _(j):
        w=wide_cols(wa, mul(wcol+j*tile,128), tile)
        cs=pl.ds(mul(j*tile,128),tile)
        out_ref[rows,cs] = base_ref[rows,cs]+dot(a_ref[rows,:], w)

def back_project(g_ref, gcol, wa, wcol, total, tile, acc_ref, first=0, count=ROWS, fresh=True):
    rows=pl.ds(first,count)
    def part(j):
        w=wide_cols(wa, mul(wcol+j*tile,128), tile)
        return dot(g_ref[rows, pl.ds(mul(gcol+j*tile,128),tile)], w, NT)
    if fresh:
        acc_ref[rows,:]=part(0)
    @pl.loop(1 if fresh else 0, total//tile)
    def _(j):
        acc_ref[rows,:]+=part(j)

def attend_forward(q_ref, qc, k_ref, kc, v_ref, vc, o_ref, oT_ref, mask_ref, start, stop, kept_ref=None, unroll=1):
    @pl.loop(start, stop, unroll=unroll)
    def _(i):
        img=i//6; p=i%6
        rows=pl.ds(mul(img*SEQ,SEQ),SEQ)
        def cols(base): return pl.ds(mul(base+p*128,128),128)
        q2=q_ref[rows,cols(qc)]*jnp.asarray(0.125,BF)
        k2=k_ref[rows,cols(kc)]
        vT=v_ref[rows,cols(vc)].T
        lane=lax.broadcasted_iota(jnp.int32,(SEQ,128),1)//64
        parts=[]
        for a in range(2):
            ka=jnp.where(lane==a,k2,jnp.zeros_like(k2))
            s=dot(ka,q2,NT)
            if mask_ref is not None:
                s=jnp.where(mask_ref[img].astype(F32)>0,s,-1e30)
            e=jnp.exp(s-jnp.max(s,axis=0,keepdims=True))
            w=(e*(1.0/jnp.sum(e,axis=0,keepdims=True))).astype(BF)
            if kept_ref is not None:
                kept_ref[pl.ds(mul(i*SEQ,SEQ),SEQ),a*SEQ:(a+1)*SEQ]=w
            parts.append(dot(vT[a*64:(a+1)*64],w))
        oT=jnp.concatenate(parts,axis=0).astype(BF)
        oT_ref[pl.ds(mul(p*128,128),128),rows]=oT
        o_ref[rows,cols(0)]=oT.T

def attend_backward(q_ref, qc, k_ref, kc, v_ref, vc, d_ref, mask_ref, dq_ref, dqc, dk_ref, dkc, dv_ref, dvc, start, stop, kept_ref=None):
    @pl.loop(start, stop)
    def _(i):
        img=i//6; p=i%6
        rows=pl.ds(mul(img*SEQ,SEQ),SEQ)
        def cols(base): return pl.ds(mul(base+p*128,128),128)
        q2=q_ref[rows,cols(qc)]
        qs=q2*jnp.asarray(0.125,BF)
        k2=k_ref[rows,cols(kc)]
        v2=v_ref[rows,cols(vc)]
        d2=d_ref[rows,cols(0)]
        kT=k2.T
        lane=lax.broadcasted_iota(jnp.int32,(SEQ,128),1)//64
        dqT=[]; dk=[]; dv=[]
        for a in range(2):
            mine=lane==a
            if kept_ref is not None:
                wb=kept_ref[pl.ds(mul(i*SEQ,SEQ),SEQ),a*SEQ:(a+1)*SEQ]
                w=wb.astype(F32)
            else:
                s=dot(jnp.where(mine,k2,jnp.zeros_like(k2)),qs,NT)
                if mask_ref is not None:
                    s=jnp.where(mask_ref[img].astype(F32)>0,s,-1e30)
                e=jnp.exp(s-jnp.max(s,axis=0,keepdims=True))
                w=e*(1.0/jnp.sum(e,axis=0,keepdims=True))
                wb=w.astype(BF)
            dw=dot(jnp.where(mine,v2,jnp.zeros_like(v2)),d2,NT)
            wd=w*dw
            ds=((wd-w*jnp.sum(wd,axis=0,keepdims=True))*0.125).astype(BF)
            dv.append(dot(wb,d2))
            dk.append(dot(ds,q2))
            dqT.append(dot(kT[a*64:(a+1)*64],ds))
        dq_ref[rows,cols(dqc)]=jnp.concatenate(dqT,axis=0).astype(BF).T
        dk_ref[rows,cols(dkc)]=jnp.where(lane==0,dk[0],dk[1]).astype(BF)
        dv_ref[rows,cols(dvc)]=jnp.where(lane==0,dv[0],dv[1]).astype(BF)

C0=0.7978845608028654; C1=0.044715
def gated_parts(n_ref, wa, j, rows, tile):
    gate=dot(n_ref[rows,:], wide_cols(wa, mul(WIN+j*tile,128), tile))
    up=dot(n_ref[rows,:], wide_cols(wa, mul(WIN+FF+j*tile,128), tile))
    sq=gate*gate
    t=jnp.tanh(gate*(C0+(C0*C1)*sq))
    h=0.5+0.5*t
    slope=h+(0.5*gate)*(1.0-t*t)*(C0+(3*C0*C1)*sq)
    return up, gate*h, slope

def gated_forward(n_ref, wa, gu_ref, hid_ref, start, stop, first=0, count=ROWS, tile=256):
    rows=pl.ds(first,count)
    @pl.loop(start, stop)
    def _(j):
        lo=pl.ds(mul(j*tile,tile),tile); hi=pl.ds(mul(FF+j*tile,tile),tile)
        up,act,slope=gated_parts(n_ref,wa,j,rows,tile)
        hid_ref[rows,lo]=(act*up).astype(BF)
        gu_ref[rows,lo]=(up*slope).astype(BF)
        gu_ref[rows,hi]=act.astype(BF)

def hidden_grad(gb_ref, wo, gu_ref):
    @pl.loop(0, 4, unroll=2)
    def _(j):
        gu_ref[:,pl.ds(mul(FF+j*512,512),512)]=dot(gb_ref[...], wo[j].reshape(512,D), NT).astype(BF)

def gated_both(n_ref, wa, gu_ref, hid_ref, start, stop, tile=256):
    rows=pl.ds(0,ROWS)
    @pl.loop(start, stop)
    def _(j):
        lo=pl.ds(mul(j*tile,tile),tile); hi=pl.ds(mul(FF+j*tile,tile),tile)
        up,act,slope=gated_parts(n_ref,wa,j,rows,tile)
        hid_ref[rows,lo]=(act*up).astype(BF)
        dh=gu_ref[rows,hi].astype(F32)
        gu_ref[rows,lo]=(dh*up*slope).astype(BF)
        gu_ref[rows,hi]=(dh*act).astype(BF)

def gated_backward(gb_ref, wo, gu_ref, first=0, count=ROWS):
    rows=pl.ds(first,count)
    @pl.loop(0, 4, unroll=4)
    def _(j):
        lo=pl.ds(mul(j*512,512),512); hi=pl.ds(mul(FF+j*512,512),512)
        dh=dot(gb_ref[rows,:], wo[j].reshape(512,D), NT)
        gu_ref[rows,lo]=(dh*gu_ref[rows,lo].astype(F32)).astype(BF)
        gu_ref[rows,hi]=(dh*gu_ref[rows,hi].astype(F32)).astype(BF)

def half_rows(nT_ref, c):
    return jnp.concatenate([nT_ref[pl.ds(mul((2*j+c)*48,16),48),:] for j in range(8)],axis=0)


MESH = pl.DeviceIdType.MESH
BIG = 1152

PARTS = {
    "q0": ("attn", 0, "wide", QKV, 1152), "q1": ("attn", 1152, "wide", QKV + 1152, 1152), "o": ("attn", 3 * D, "wide", OP, D),
    "g0": ("in", 0, "wide", WIN, 1024), "u0": ("in", FF, "wide", WIN + FF, 1024),
    "g1": ("in", 1024, "wide", WIN + 1024, 1024), "u1": ("in", FF + 1024, "wide", WIN + FF + 1024, 1024),
    "x0": ("extra", 0, "wide", XA, D), "x1": ("extra", D, "wide", XB, D),
    "k0": (None, 0, "wide", KV, D), "k1": (None, D, "wide", KV + D, D),
    "d0": ("out", 0, "tall", 0, 256), "d1": ("out", 256, "tall", 256, 256), "d2": ("out", 512, "tall", 512, 256),
}
PART_NAMES = tuple(PARTS)
ROUTES = (
    (("q0", "q1", "o", "g0", "u0", "g1", "u1", "d2"), {3: "d0", 5: "d1"}),
    (("q0", "q1", "o", "x0", "x1", "k0", "k1", "g0", "u0", "g1", "u1"), {2: "d0", 4: "d1", 7: "d2"}),
)
SUMS = {
    "out0": ("tall", 0, 384), "out1": ("tall", 384, 384),
    "in0": ("wide", WIN, 1024), "in1": ("wide", WIN + 1024, 1024),
    "in2": ("wide", WIN + FF, 1024), "in3": ("wide", WIN + FF + 1024, 1024),
    "x0": ("wide", XA, D), "x1": ("wide", XB, D),
    "k0": ("wide", KV, D), "k1": ("wide", KV + D, D),
    "o": ("wide", OP, D),
    "q0": ("wide", QKV, D), "q1": ("wide", QKV + D, D), "q2": ("wide", QKV + 2 * D, 384), "q3": ("wide", QKV + 2 * D + 384, 384),
}
SUM_NAMES = tuple(SUMS)
PAIRED = ("out1",)
SECOND_ONLY = ("x1", "k1")
DIRECT = ("q2", "q3")
OUT_OF = {
    "out0": ("out", 0), "out1": ("out", 384), "in0": ("in", 0), "in1": ("in", 1024), "in2": ("in", FF), "in3": ("in", FF + 1024),
    "x0": ("extra", 0), "x1": ("extra", D), "o": ("attn", 3 * D),
    "q0": ("attn", 0), "q1": ("attn", D), "q2": ("attn", 2 * D), "q3": ("attn", 2 * D + 384),
}
FREE = {"out": 0, "in": 1, "x": 2, "k": 3, "o": 4, "q": 5}


def scratch_list():
    V, DMA, REG = pltpu.VMEM, pltpu.SemaphoreType.DMA, pltpu.SemaphoreType.REGULAR
    n, s = len(PARTS), len(SUMS)
    return dict(
        wide=V((4, 2, 2, 48, WIDE), BF), tall=V((4, 2, 2, 128, D), BF),
        y_wide=V((4, 48, WIDE), BF), y_tall=V((4, 128, D), BF), pair_in=V((1, 3, 2, 128, 384), BF),
        stage=V((2, 4, 2, 48, 1024), BF), stage_tall=V((4, 2, 128, D), BF),
        fin=V((2, 48, 1024), F32), fin_tall=V((2, 128, 384), F32), fin_x=V((48, D), F32), fin_k=V((48, D), F32),
        x=V((ROWS, D), F32), mid=V((ROWS, D), F32), late=V((ROWS, D), F32), g=V((ROWS, D), F32),
        n1=V((ROWS, D), BF), n2=V((ROWS, D), BF), n3=V((ROWS, D), BF), xin=V((ROWS, D), BF), nT=V((D, ROWS), BF),
        qkv=V((ROWS, 3 * D), BF), ao=V((ROWS, D), BF), aoT=V((D, ROWS), BF),
        xq=V((ROWS, D), BF), kv=V((ROWS, 2 * D), BF), cmT=V((D, ROWS), BF),
        gu=V((ROWS, 2 * FF), BF), hid=V((ROWS, FF), BF), kept=V((12 * SEQ, 2 * SEQ), BF), gb=V((ROWS, D), BF), gb2=V((ROWS, D), BF),
        mask=V((MICRO, SEQ, SEQ), BF), xsend=V((ROWS, D), BF),
        gz=V((4, 8, D), F32), gy=V((2, 8, D), F32), gc=V((2, 8, D), F32), gain=V((8, D), F32),
        dgain=V((8, D), F32), gout=V((3, 48), F32), hz=V((4, 8, D), F32), hy=V((2, 8, D), F32), hc=V((2, 8, D), F32),
        s_in=DMA((3,)), s_own=DMA((n,)), s_kx=DMA, s_kr=DMA, s_hs=DMA, s_hr=DMA,
        s_rs=DMA((n, 3)), s_rr=DMA((n, 3)), s_ls=DMA((n, 3)), s_lr=DMA((n, 3)),
        s_ys=DMA((n, 4)), s_yr=DMA((n, 4)), s_cs=DMA((n,)), s_cr=DMA((n,)),
        s_ms=DMA((MICRO,)), s_mr=DMA((MICRO,)), s_gs=DMA((2, 5)), s_gr=DMA((2, 5)),
        t_cs=DMA((s,)), t_cr=DMA((s,)), t_ys=DMA((s,)), t_yr=DMA((s,)),
        t_rs=DMA((s,)), t_rr=DMA((s,)), t_ls=DMA((s,)), t_lr=DMA((s,)),
        t_ds=DMA((len(DIRECT), 3)), t_dr=DMA((len(DIRECT), 3)), t_xs=DMA((2,)), t_xr=DMA((2,)), t_out=DMA((s,)), s_out=DMA((3,)),
        free=REG((len(FREE),)), free_r=REG((s,)), free_l=REG((s,)),
    )


def whole_kernel(*refs):
    (acts_h, cot_h, attn_h, extra_h, in_h, out_h, gain_in, seg_in) = refs[:8]
    (res_o, grad_o, attn_o, extra_o, gin_o, gout_o, gain_o) = refs[8:15]
    R = type("Refs", (), {})()
    for name, ref in zip(scratch_list(), refs[15:]):
        setattr(R, name, ref)
    src = {"attn": attn_h, "extra": extra_h, "in": in_h, "out": out_h}
    dst = {"attn": attn_o, "extra": extra_o, "in": gin_o, "out": gout_o}
    buf = {"wide": R.wide, "tall": R.tall}
    ybuf = {"wide": R.y_wide, "tall": R.y_tall}

    R.acc = R.x
    hidT = R.kept.at[pl.ds(0, FF)]

    section = lax.axis_index("section")
    me = lax.axis_index("dp")
    z, y, c = me // 4, (me // 2) % 2, me % 2
    first, second = section == 0, section == 1
    at = lambda zz, yy, cc: {"dp": zz * 4 + yy * 2 + cc}
    right, left = at(lax.rem(z + 1, 4), y, c), at(lax.rem(z + 3, 4), y, c)
    z_peer = [at(lax.rem(z + k, 4), y, c) for k in (1, 2, 3)]
    y_peer, c_peer, x_peer = at(z, 1 - y, c), at(z, y, 1 - c), {"section": 1 - section}

    def remote(a, b, ss, rs, dev):
        return pltpu.make_async_remote_copy(a, b, ss, rs, device_id=dev, device_id_type=MESH)

    def local(a, b, s):
        return pltpu.make_async_copy(a, b, s)

    def when(cond, fn):
        pl.when(cond)(fn)

    barrier = pltpu.get_barrier_semaphore()
    everyone = z_peer + [y_peer, c_peer, x_peer]
    for peer in everyone:
        pl.semaphore_signal(barrier, inc=1, device_id=peer, device_id_type=MESH)
    pl.semaphore_wait(barrier, len(everyone))

    def spot(name):
        arg, lo, b, col, size = PARTS[name]
        return PART_NAMES.index(name), buf[b], pl.ds(col, size)

    def in_place(name):
        i, b, cs = spot(name)
        return b.at[z, y, c, :, cs]

    def shard(name):
        arg, lo, _, _, size = PARTS[name]
        return in_place(name) if arg is None else src[arg].at[:, pl.ds(lo, size)]

    def own_copy(name):
        return local(shard(name), in_place(name), R.s_own.at[PART_NAMES.index(name)])

    def line_block(name, zz, pair):
        i, b, cs = spot(name)
        return b.at[zz, :, c, :, cs] if pair else b.at[zz, y, c, :, cs]

    def go_right(name, s, pair):
        i = PART_NAMES.index(name)
        d = line_block(name, z - s, pair)
        return remote(shard(name) if s == 0 and not pair else d, d, R.s_rs.at[i, s], R.s_rr.at[i, s], right)

    def go_left(name, s, pair):
        i = PART_NAMES.index(name)
        d = line_block(name, z + s, pair)
        return remote(shard(name) if s == 0 and not pair else d, d, R.s_ls.at[i, s], R.s_lr.at[i, s], left)

    def from_left(name, s, pair):
        i = PART_NAMES.index(name)
        d = line_block(name, z - s, pair)
        return remote(d, d, R.s_rs.at[i, s - 1], R.s_rr.at[i, s - 1], left)

    def from_right(name, s, pair):
        i = PART_NAMES.index(name)
        d = line_block(name, z + s, pair)
        return remote(d, d, R.s_ls.at[i, s - 1], R.s_lr.at[i, s - 1], right)

    def across(name, zz, own=False, pair=False):
        i, b, cs = spot(name)
        d = b.at[zz, y, c, :, cs]
        k = 0 if pair else zz
        return remote(shard(name) if own else d, d, R.s_ys.at[i, k], R.s_yr.at[i, k], y_peer)

    def across_in(name, zz, pair=False):
        i, b, cs = spot(name)
        d = b.at[zz, 1 - y, c, :, cs]
        k = 0 if pair else zz
        return remote(d, d, R.s_ys.at[i, k], R.s_yr.at[i, k], y_peer)

    def to_core(name):
        i, b, cs = spot(name)
        d = b.at[:, :, c, :, cs]
        return remote(d, d, R.s_cs.at[i], R.s_cr.at[i], c_peer)

    def core_in(name):
        i, b, cs = spot(name)
        d = b.at[:, :, 1 - c, :, cs]
        return remote(d, d, R.s_cs.at[i], R.s_cr.at[i], c_peer)

    def ends(s, go, cond=None):
        when((z >= s) & (z < 3), lambda: go(0))
        when((z + s <= 3) & (z > 0), lambda: go(1))

    def begin(name, pair):
        if PARTS[name][0] is not None:
            own_copy(name).start()
        if name == "k0":
            kv_shard.wait_recv()
        if not pair:
            when(z < 3, lambda: go_right(name, 0, False).start())
            when(z > 0, lambda: go_left(name, 0, False).start())
        across(name, z, True, pair).start()

    def pair_turn(name):
        own_copy(name).wait()
        across_in(name, z, True).wait_recv()
        when(z < 3, lambda: go_right(name, 0, True).start())
        when(z > 0, lambda: go_left(name, 0, True).start())

    def hop(name, s, pair):
        def lower():
            from_left(name, s, pair).wait_recv()
            if s < 3:
                when(z < 3, lambda: go_right(name, s, pair).start())
            if not pair:
                across(name, z - s).start()

        def upper():
            from_right(name, s, pair).wait_recv()
            if s < 3:
                when(z > 0, lambda: go_left(name, s, pair).start())
            if not pair:
                across(name, z + s).start()

        when(z >= s, lower)
        when(z + s <= 3, upper)

    def line_done(name, pair):
        if not pair:
            if PARTS[name][0] is not None:
                own_copy(name).wait()
            for zz in range(4):
                across_in(name, zz).wait_recv()
        to_core(name).start()

    def have(*names):
        for name in names:
            core_in(name).wait_recv()

    def sent(name, pair):
        for s in range(3):
            when((z >= s) & (z < 3), lambda: go_right(name, s, pair).wait_send())
            when((z + s <= 3) & (z > 0), lambda: go_left(name, s, pair).wait_send())
        for zz in range(1 if pair else 4):
            across(name, zz, False, pair).wait_send()
        to_core(name).wait_send()

    def all_sent(who):
        line, pairs = ROUTES[who]
        for name in line:
            sent(name, False)
        for name in pairs.values():
            sent(name, True)

    def section_tick(who, t):
        line, pairs = ROUTES[who]
        n = len(line)
        for start, name in pairs.items():
            if t == start:
                begin(name, True)
            if t == start + 1:
                pair_turn(name)
            for s in (1, 2, 3):
                if t == start + 1 + s:
                    hop(name, s, True)
            if t == start + 5:
                line_done(name, True)
        if t < n:
            begin(line[t], False)
        for s in (1, 2, 3):
            if 0 <= t - s < n:
                hop(line[t - s], s, False)
        if 0 <= t - 4 < n:
            line_done(line[t - 4], False)

    def tick(t):
        when(first, lambda: section_tick(0, t))
        when(second, lambda: section_tick(1, t))

    kv_block = R.wide.at[z, y, c, :, pl.ds(KV, 2 * D)]
    kv_shard = remote(extra_h, kv_block, R.s_kx, R.s_kr, x_peer)
    when(first, lambda: kv_shard.start())

    share = gain_in.shape[1]
    spread = (
        lax.broadcasted_iota(jnp.int32, (share, D), 1) - me * share == lax.broadcasted_iota(jnp.int32, (share, D), 0)
    ).astype(F32)
    R.gz[z] = jnp.zeros((8, D), F32)
    R.gz[z, 0:3, :] = dot(gain_in[...], spread.astype(BF))
    x_in = local(acts_h, R.x, R.s_in.at[1])
    x_in.start()
    g_in = local(cot_h, R.g, R.s_in.at[2])
    g_in.start()

    def small_z(own_ref, slots, row):
        return [remote(own_ref, slots.at[z], R.s_gs.at[row, k], R.s_gr.at[row, k], z_peer[k]) for k in range(3)]

    def small_pair(slots, row, k, dev):
        return remote(slots.at[0], slots.at[1], R.s_gs.at[row, k], R.s_gr.at[row, k], dev)

    gzc = small_z(R.gz.at[z], R.gz, 0)
    for q in gzc:
        q.start()
    tick(0)
    tick(1)
    for q in gzc:
        q.wait_recv()
    R.gy[0] = (R.gz[0] + R.gz[1]) + (R.gz[2] + R.gz[3])
    q = small_pair(R.gy, 0, 3, y_peer)
    q.start()
    tick(2)
    q.wait()
    R.gc[0] = R.gy[0] + R.gy[1]
    q = small_pair(R.gc, 0, 4, c_peer)
    q.start()
    tick(3)
    q.wait()
    R.gain[...] = R.gc[0] + R.gc[1]
    for q in gzc:
        q.wait_send()
    gain = lambda k: R.gain[k : k + 1, :]

    ones = jnp.where(first, 1.0, 0.0)
    for img in range(MICRO):
        row = jnp.broadcast_to(seg_in[img : img + 1, :].astype(F32), (SEQ, SEQ))
        key = lax.broadcasted_iota(jnp.int32, (SEQ, SEQ), 0)
        query = lax.broadcasted_iota(jnp.int32, (SEQ, SEQ), 1)
        allowed = jnp.where((row.T == row) & (key <= query), 1.0, ones)
        R.mask[img] = allowed.astype(BF)
    R.dgain[...] = jnp.zeros_like(R.dgain)

    x_in.wait()
    norm_forward(R.x, gain(0), R.n1)
    for t in range(4, 6):
        tick(t)
    have("q0", "q1")
    project(R.n1, R.wide, QKV, R.qkv, 0, 3 * D, 768)
    tick(6)

    def self_attention(a, b):
        attend_forward(R.qkv, 0, R.qkv, D, R.qkv, 2 * D, R.ao, R.aoT, R.mask, a, b)

    self_attention(0, 4)
    tick(7)
    self_attention(4, 8)
    tick(8)
    self_attention(8, 12)
    tick(9)
    have("o")
    project_add(R.ao, R.wide, OP, R.x, R.mid, 384)

    def message(img):
        rows = pl.ds(img * SEQ, SEQ)
        return remote(R.xsend.at[rows], R.xin.at[rows], R.s_ms.at[img], R.s_mr.at[img], x_peer)

    def down(base, out, cols, first_row=0, count=ROWS):
        rows = pl.ds(first_row, count)
        for lo in cols:
            cs = pl.ds(lo, 256)
            out[rows, cs] = base[rows, cs] + dot(R.hid[rows, :], R.tall[:, :, :, :, cs].reshape(FF, 256))

    def round_g(to, first_row=0, count=ROWS):
        rows = pl.ds(first_row, count)
        to[rows, :] = R.g[rows, :].astype(BF)

    def enc_forward():
        norm_forward(R.mid, gain(1), R.n2)
        have("g0", "u0")
        gated_forward(R.n2, R.wide, R.gu, R.hid, 0, 1, tile=512)
        section_tick(0, 10)
        gated_forward(R.n2, R.wide, R.gu, R.hid, 1, 2, tile=512)
        have("g1", "u1")
        gated_forward(R.n2, R.wide, R.gu, R.hid, 1, 2, tile=1024)
        section_tick(0, 11)
        have("d0", "d1")
        down(R.mid, R.late, (0, 256))
        have("d2")
        for img in range(MICRO):
            down(R.mid, R.late, (512,), img * SEQ, SEQ)
            norm_forward(R.late, gain(2), R.xsend, img * SEQ, SEQ)
            message(img).start()
        all_sent(0)
        kv_shard.wait_send()

    def dec_forward():
        norm_forward(R.mid, gain(2), R.n3)
        section_tick(1, 10)
        have("x0")
        project(R.n3, R.wide, XA, R.xq, 0, D, 384)
        section_tick(1, 11)
        section_tick(1, 12)
        have("d0", "d1", "d2")
        g_in.wait()
        round_g(R.gb)
        hidden_grad(R.gb, R.tall, R.gu)
        section_tick(1, 13)
        have("x1", "k0", "k1")

        def cross(img):
            message(img).wait_recv()
            project(R.xin, R.wide, KV, R.kv, 0, 2 * D, 768, img * SEQ, SEQ)
            attend_forward(R.xq, 0, R.kv, 0, R.kv, D, R.ao, R.cmT, None, img * 6, img * 6 + 6, R.kept, 3)

        cross(0)
        section_tick(1, 14)
        cross(1)
        project_add(R.ao, R.wide, XB, R.mid, R.late, 384)
        norm_forward(R.late, gain(1), R.n2)
        have("g0", "u0", "g1", "u1")
        gated_both(R.n2, R.wide, R.gu, R.hid, 0, 2, 1024)
        all_sent(1)

    def sum_spot(name):
        b, lo, size = SUMS[name]
        return SUM_NAMES.index(name), b, pl.ds(lo, size), size

    stage_of = {}

    def core_copy(name):
        k, b, cs, size = sum_spot(name)
        if b == "tall":
            s = R.stage_tall.at[:, :, :, cs]
        else:
            s = R.stage.at[stage_of[name], :, :, :, pl.ds(0, size)]
        return remote(s, buf[b].at[:, :, c, :, cs], R.t_cs.at[k], R.t_cr.at[k], c_peer)

    def paired(name):
        return name in PAIRED

    def y_copy(name):
        k, b, cs, size = sum_spot(name)
        if paired(name):
            return remote(buf[b].at[z, 1 - y, c, :, cs], ybuf[b].at[0, :, cs], R.t_ys.at[k], R.t_yr.at[k], y_peer)
        return remote(buf[b].at[:, 1 - y, c, :, cs], ybuf[b].at[:, :, cs], R.t_ys.at[k], R.t_yr.at[k], y_peer)

    def moving(name, a, e):
        _, b, cs, _ = sum_spot(name)
        return buf[b].at[a:e, :, c, :, cs] if paired(name) else buf[b].at[a:e, y, c, :, cs]

    def landing_left(name, a, e):
        _, b, cs, _ = sum_spot(name)
        return buf[b].at[a:e, :, 1 - c, :, cs] if paired(name) else buf[b].at[a:e, 0, 1 - c, :, cs]

    def landing_right(name, a, e):
        _, b, cs, size = sum_spot(name)
        if paired(name):
            return R.pair_in.at[PAIRED.index(name), a:e]
        return buf[b].at[a:e, 1, 1 - c, :, cs]

    def right_copy(name, zz):
        k = SUM_NAMES.index(name)
        return remote(moving(name, zz + 1, 4), landing_left(name, zz + 1, 4), R.t_rs.at[k], R.t_rr.at[k], right)

    def left_copy(name, zz):
        k = SUM_NAMES.index(name)
        return remote(moving(name, 0, zz), landing_right(name, 0, zz), R.t_ls.at[k], R.t_lr.at[k], left)

    def send_right(name, zz):
        pl.semaphore_wait(R.free_r.at[SUM_NAMES.index(name)], 1)
        right_copy(name, zz).start()

    def send_left(name, zz):
        pl.semaphore_wait(R.free_l.at[SUM_NAMES.index(name)], 1)
        left_copy(name, zz).start()

    def add_blocks(name, landed, a, e):
        mine = moving(name, a, e)

        @pl.loop(0, e - a)
        def _(j):
            mine[j] = (mine[j].astype(F32) + landed[j].astype(F32)).astype(BF)

    def add_left(name, zz):
        k = SUM_NAMES.index(name)
        d = landing_left(name, zz, 4)
        remote(d, d, R.t_rs.at[k], R.t_rr.at[k], left).wait_recv()
        add_blocks(name, d, zz, 4)

    def add_right(name, zz):
        k = SUM_NAMES.index(name)
        d = landing_right(name, 0, zz + 1)
        remote(d, d, R.t_ls.at[k], R.t_lr.at[k], right).wait_recv()
        add_blocks(name, d, 0, zz + 1)

    def open_line(name):
        k = SUM_NAMES.index(name)
        if name in DIRECT:
            for peer in z_peer:
                pl.semaphore_signal(R.free_r.at[k], inc=1, device_id=peer, device_id_type=MESH)
            return
        when(z > 0, lambda: pl.semaphore_signal(R.free_r.at[k], inc=1, device_id=left, device_id_type=MESH))
        when(z < 3, lambda: pl.semaphore_signal(R.free_l.at[k], inc=1, device_id=right, device_id_type=MESH))

    def straight(name):
        k, b, cs, size = sum_spot(name)
        d, w = DIRECT.index(name), buf[b]
        return [
            remote(
                w.at[lax.rem(z + j + 1, 4), y, c, :, cs], w.at[z, 0, 1 - c, :, cs], R.t_ds.at[d, j], R.t_dr.at[d, j], z_peer[j]
            )
            for j in range(3)
        ]

    def collect(name):
        k, b, cs, size = sum_spot(name)
        d, w = DIRECT.index(name), buf[b]
        total = w[z, y, c, :, cs].astype(F32)
        for j in range(3):
            landed = w.at[lax.rem(z + 3 - j, 4), 0, 1 - c, :, cs]
            remote(landed, landed, R.t_ds.at[d, j], R.t_dr.at[d, j], z_peer[2 - j]).wait_recv()
            total = total + landed[...].astype(F32)
        finish(name, total)

    def line_a(name):
        when(z == 0, lambda: send_right(name, 0))
        when(z == 3, lambda: send_left(name, 3))

    def line_b(name):
        def one():
            add_left(name, 1)
            send_right(name, 1)

        def two():
            add_right(name, 2)
            send_left(name, 2)

        when(z == 1, one)
        when(z == 2, two)

    def line_c(name):
        def one():
            add_right(name, 1)
            send_left(name, 1)

        def two():
            add_left(name, 2)
            send_right(name, 2)

        when(z == 1, one)
        when(z == 2, two)

    def line_d(name):
        when(z == 0, lambda: add_right(name, 0))
        when(z == 3, lambda: add_left(name, 3))

    def line_sent(name):
        if name in DIRECT:
            for q in straight(name):
                q.wait_send()
            return
        for zz in range(3):
            when(z == zz, lambda: right_copy(name, zz).wait_send())
            when(z == zz + 1, lambda: left_copy(name, zz + 1).wait_send())

    def release(name):
        pl.semaphore_signal(R.free.at[FREE[name]], inc=1, device_id=c_peer, device_id_type=MESH)

    def claim(name):
        pl.semaphore_wait(R.free.at[FREE[name]], 1)

    order = []

    def grad_wide(name, nT, g_ref, gcol, tile):
        k, b, cs, size = sum_spot(name)
        lo = SUMS[name][1]
        slot = len(order) % 2
        if len(order) >= 2:
            core_copy(order[-2]).wait_send()
        stage_of[name] = slot
        order.append(name)
        lhs = half_rows(nT, 1 - c)

        @pl.loop(0, size // tile)
        def _(j):
            w = dot(lhs, g_ref[:, pl.ds(mul(gcol + j * tile, 128), tile)]).astype(BF)
            R.stage[slot, :, :, :, pl.ds(mul(j * tile, 128), tile)] = w.reshape(4, 2, 48, tile)

        core_copy(name).start()
        mine = half_rows(nT, c)

        @pl.loop(0, size // tile)
        def _(j):
            w = dot(mine, g_ref[:, pl.ds(mul(gcol + j * tile, 128), tile)]).astype(BF)
            R.wide[:, :, c, :, pl.ds(mul(lo + j * tile, 128), tile)] = w.reshape(4, 2, 48, tile)

    def drain():
        for name in order[-2:]:
            core_copy(name).wait_send()
        order.clear()

    def grad_tall(name):
        k, b, cs, size = sum_spot(name)

        def rows_of(j, cc):
            units = [hidT[pl.ds(mul((8 * j + 2 * i + cc) * 128, 128), 128), :] for i in range(4)]
            return dot(jnp.concatenate(units, axis=0), R.gb[:, cs]).astype(BF).reshape(2, 2, 128, size)

        @pl.loop(0, 2)
        def _(j):
            R.stage_tall[pl.ds(2 * j, 2), :, :, cs] = rows_of(j, 1 - c)

        core_copy(name).start()

        @pl.loop(0, 2)
        def _(j):
            R.tall[pl.ds(2 * j, 2), :, c, :, cs] = rows_of(j, c)

    ready, crossing, moving_on, finished = [], [], [], []

    def on(name, fn):
        if name in SECOND_ONLY:
            when(second, fn)
        else:
            fn()

    def feed():
        while ready and len([n for n in crossing if n not in SECOND_ONLY]) < 3:
            name = ready.pop(0)
            on(name, lambda: y_copy(name).start())
            crossing.append(name)

    def core_stage(name, pass_on=True):
        k, b, cs, size = sum_spot(name)
        w = buf[b]
        landed = w.at[:, :, 1 - c, :, cs]
        remote(landed, landed, R.t_cs.at[k], R.t_cr.at[k], c_peer).wait_recv()

        @pl.loop(0, 8)
        def _(j):
            own = w[j // 2, j % 2, c, :, cs].astype(F32)
            w[j // 2, j % 2, c, :, cs] = (own + w[j // 2, j % 2, 1 - c, :, cs].astype(F32)).astype(BF)

        if pass_on:
            enter(name)

    def enter(name):
        on(name, lambda: open_line(name))
        if paired(name):
            line_a(name)
            moving_on.append([name, later, line_b, later, line_c, later, line_d, late_cross])
        else:
            ready.append(name)
            feed()

    def later(name):
        pass

    def late_cross(name):
        y_copy(name).start()
        crossing.append(name)

    def y_stage(name):
        k, b, cs, size = sum_spot(name)
        w, r = buf[b], ybuf[b]
        if paired(name):
            d = r.at[0, :, cs]
            remote(d, d, R.t_ys.at[k], R.t_yr.at[k], y_peer).wait_recv()
            finish(name, w[z, y, c, :, cs].astype(F32) + r[0, :, cs].astype(F32))
            return
        y_copy(name).wait_recv()

        @pl.loop(0, 4)
        def _(j):
            w[j, y, c, :, cs] = (w[j, y, c, :, cs].astype(F32) + r[j, :, cs].astype(F32)).astype(BF)

        if name in DIRECT:
            pl.semaphore_wait(R.free_r.at[k], 3)
            for q in straight(name):
                q.start()
            moving_on.append([name, later, collect])
            return
        line_a(name)
        moving_on.append([name, later, line_b, line_c, line_d, last])

    def last(name):
        k, b, cs, size = sum_spot(name)
        total = buf[b][z, y, c, :, cs].astype(F32)
        if name not in SECOND_ONLY:
            finish(name, total)
        elif name == "x1":
            R.fin_x[...] = total
            x_out.start()
        else:
            R.fin_k[...] = total
            key_home.start()

    def turn():
        going = list(moving_on)
        while crossing:
            name = crossing.pop(0)
            on(name, lambda: y_stage(name))
            feed()
            if name not in SECOND_ONLY:
                break
        for item in going:
            while not crossing and len(item) > 2 and item[1] is later:
                item.pop(1)
            fn = item.pop(1)
            on(item[0], lambda: fn(item[0]))
            if len(item) == 1:
                moving_on.remove(item)

    def out_copy(name):
        k, b, cs, size = sum_spot(name)
        arg, lo = OUT_OF[name]
        kind = [f for f in finished if SUMS[f][0] == b]
        slot = kind.index(name) % 2
        f = R.fin_tall.at[slot] if b == "tall" else R.fin.at[slot, :, pl.ds(0, size)]
        return local(f, dst[arg].at[:, pl.ds(lo, size)], R.t_out.at[k])

    def finish(name, total):
        k, b, cs, size = sum_spot(name)
        kind = [f for f in finished if SUMS[f][0] == b]
        slot = len(kind) % 2
        if len(kind) >= 2:
            out_copy(kind[-2]).wait()
        finished.append(name)
        if b == "tall":
            R.fin_tall[slot] = total
        else:
            R.fin[slot, :, pl.ds(0, size)] = total
        out_copy(name).start()

    x_out = local(R.fin_x, extra_o.at[:, pl.ds(D, D)], R.t_out.at[SUM_NAMES.index("x1")])
    key_home = remote(R.fin_k, R.fin_x, R.s_hs, R.s_hr, x_peer)

    def over_copy(j):
        k, b, cs, size = sum_spot(("k0", "k1")[j])
        return remote(
            R.wide.at[:, :, c, :, cs], R.wide.at[:, :, c, :, pl.ds(XA + j * D, D)], R.t_xs.at[j], R.t_xr.at[j], x_peer
        )

    def project_back(g_ref, wcol, out_ref):
        out_ref[...] = dot(g_ref[...], wide_cols(R.wide, wcol, D), NT).astype(BF)

    def down_grads():
        release("out")
        claim("out")
        grad_tall("out0")
        core_stage("out0")
        grad_tall("out1")
        core_stage("out1")

    def in_grads():
        release("in")
        claim("in")
        grad_wide("in0", R.nT, R.gu, 0, 512)
        grad_wide("in1", R.nT, R.gu, 1024, 512)
        core_stage("in0")
        turn()
        grad_wide("in2", R.nT, R.gu, FF, 512)
        core_stage("in1")
        grad_wide("in3", R.nT, R.gu, FF + 1024, 512)
        core_stage("in2")

    gains_own = lambda: small_pair(R.hc, 1, 4, c_peer)
    gains_row = lambda: small_pair(R.hy, 1, 3, y_peer)
    gains_line = lambda: small_z(R.gain, R.hz, 1)
    gain_copy = local(R.gout, gain_o, R.s_out.at[2])
    grad_copy = local(R.g, grad_o, R.s_out.at[1])

    def gains_a():
        R.hc[0] = R.dgain[...]
        gains_own().start()

    def gains_b(_):
        gains_own().wait()
        R.hy[0] = R.hc[0] + R.hc[1]
        gains_row().start()

    def gains_c(_):
        gains_row().wait()
        R.gain[...] = R.hy[0] + R.hy[1]
        for q in gains_line():
            q.start()

    def gains_d(_):
        for q in gains_line():
            q.wait()
        R.hz[z] = R.gain[...]
        whole = (R.hz[0] + R.hz[1]) + (R.hz[2] + R.hz[3])
        own = lax.dot_general(whole, spread, NT, precision=lax.Precision.HIGHEST, preferred_element_type=F32)
        R.gout[...] = own[0:3]
        gain_copy.start()

    dec_res = local(R.acc, res_o, R.s_out.at[0])
    enc_res = local(R.late, res_o, R.s_out.at[0])

    def dec_middle():
        back_project(R.gu, 0, R.wide, WIN, 2 * FF, 2048, R.acc)
        norm_backward(R.late, gain(1), R.acc, R.g, R.dgain, 1, low_ref=R.gb2)
        project_back(R.gb2, XB, R.xsend)
        for img in range(MICRO):
            attend_backward(
                R.xq, 0, R.kv, 0, R.kv, D, R.xsend, None, R.xq, 0, R.kv, 0, R.kv, D, img * 6, img * 6 + 6, R.kept
            )
            back_project(R.kv, 0, R.wide, KV, 2 * D, 768, R.acc, img * SEQ, SEQ)
            rows = pl.ds(img * SEQ, SEQ)
            R.xsend[rows, :] = R.acc[rows, :].astype(BF)
            message(img).start()
        down(R.late, R.acc, (0, 256, 512))
        dec_res.start()
        transpose_to(R.hid, hidT)

    def dec_all():
        dec_forward()
        dec_middle()

    def enc_middle():
        enc_res.start()
        transpose_to(R.hid, hidT)
        transpose_to(R.n2, R.nT)
        g_in.wait()
        for img in range(MICRO):
            message(img).wait_send()
        for img in range(MICRO):
            lo = img * SEQ
            message(img).wait_recv()
            norm_backward(R.late, gain(2), R.xin, R.g, R.dgain, 2, lo, SEQ, R.gb)
            gated_backward(R.gb, R.tall, R.gu, lo, SEQ)

    def enc_in():
        back_project(R.gu, 0, R.wide, WIN, 2 * FF, 2048, R.acc)
        norm_backward(R.mid, gain(1), R.acc, R.g, R.dgain, 1, low_ref=R.gb2)

    def dec_keys():
        release("k")
        transpose_to(R.xin, R.nT)
        claim("k")
        grad_wide("k0", R.nT, R.kv, 0, 384)
        grad_wide("k1", R.nT, R.kv, D, 384)
        core_stage("k0", False)
        over_copy(0).start()
        core_stage("k1", False)
        drain()
        transpose_to(R.n2, R.nT)

    def dec_cross():
        dec_res.wait()
        back_project(R.xq, 0, R.wide, XA, D, 768, R.acc)
        release("x")
        transpose_to(R.n3, R.nT)
        claim("x")
        grad_wide("x0", R.nT, R.xq, 0, 384)
        grad_wide("x1", R.cmT, R.gb2, 0, 384)
        core_stage("x0", False)
        core_stage("x1", False)
        norm_backward(R.mid, gain(2), R.acc, R.g, R.dgain, 2, low_ref=R.gb2)
        for img in range(MICRO):
            message(img).wait_send()
        drain()

    when(first, enc_forward)
    when(second, dec_all)
    when(first, enc_middle)
    down_grads()
    when(first, enc_in)
    when(second, dec_keys)
    in_grads()
    drain()
    core_stage("in3")
    when(second, dec_cross)

    enter("x1")
    enter("k1")

    when(first, lambda: enc_res.wait())
    x_again = local(acts_h, R.late, R.s_in.at[1])
    x_again.start()
    project_back(R.gb2, OP, R.ao)
    release("o")
    claim("o")
    grad_wide("o", R.aoT, R.gb2, 0, 384)
    turn()
    attend_backward(R.qkv, 0, R.qkv, D, R.qkv, 2 * D, R.ao, R.mask, R.qkv, 0, R.qkv, D, R.qkv, 2 * D, 0, 6)
    core_stage("o")
    turn()
    attend_backward(R.qkv, 0, R.qkv, D, R.qkv, 2 * D, R.ao, R.mask, R.qkv, 0, R.qkv, D, R.qkv, 2 * D, 6, 12)
    turn()
    back_project(R.qkv, 0, R.wide, QKV, 3 * D, 768, R.acc)
    release("q")
    transpose_to(R.n1, R.nT)
    claim("q")
    when(first, lambda: over_copy(0).wait_recv())
    enter("x0")
    grad_wide("q0", R.nT, R.qkv, 0, 384)
    grad_wide("q1", R.nT, R.qkv, D, 384)
    core_stage("q0")
    grad_wide("q2", R.nT, R.qkv, 2 * D, 384)
    core_stage("q1")
    grad_wide("q3", R.nT, R.qkv, 2 * D + 384, 384)
    core_stage("q2")
    core_stage("q3")
    turn()
    x_again.wait()
    norm_backward(R.late, gain(0), R.acc, R.g, R.dgain, 0)
    grad_copy.start()
    gains_a()
    moving_on.append(["gains", gains_b, later, later, later, gains_c, later, later, gains_d])
    while ready or crossing or moving_on:
        turn()
    for name in ("out0", "out1"):
        core_copy(name).wait_send()
    drain()
    def all_gone(name):
        y_copy(name).wait_send()
        line_sent(name)

    for name in finished + list(SECOND_ONLY):
        on(name, lambda: all_gone(name))
    for b in ("tall", "wide"):
        for name in [f for f in finished if SUMS[f][0] == b][-2:]:
            out_copy(name).wait()

    def dec_end():
        over_copy(0).wait_send()
        x_out.wait()
        key_home.wait_send()

    def enc_end():
        key_home.wait_recv()
        x_out.start()
        x_out.wait()

    when(second, dec_end)
    when(first, enc_end)
    grad_copy.wait()
    gain_copy.wait()


def from_behind(block, axis, distance):
    devices = range(lax.axis_size(axis))
    route = [(i - distance, i) for i in devices if i - distance in devices]
    return lax.ppermute(block, axis, route)


def rms_norm(activations, gain_row):
    return (
        activations
        * lax.rsqrt(jnp.mean(activations * activations, axis=-1, keepdims=True) + 1e-06)
        * gain_row
    )


def product(left_side, right_side):
    return jnp.dot(left_side, right_side, preferred_element_type=jnp.float32)


def weight_grad(left_side, right_side):
    return jnp.einsum("sd,se->de", left_side, right_side, preferred_element_type=jnp.float32)


def input_back(gradient, weight):
    return jnp.einsum("se,de->sd", gradient, weight, preferred_element_type=jnp.float32)


def norm_back(activations, gain_row, gradient):
    _, pull_back = jax.vjp(rms_norm, activations, gain_row)
    return pull_back(gradient)


def heads_of(activations):
    return activations.reshape(activations.shape[0], HEADS, HDIM)


def logits_of(queries, keys_in, allowed):
    raw_logits = jnp.einsum(
        "qhd,khd->hqk", heads_of(queries), heads_of(keys_in), preferred_element_type=jnp.float32
    ) * HDIM ** (-0.5)
    if allowed is None:
        return raw_logits
    return jnp.where(allowed[None], raw_logits, -1e30)


def attend_plain(queries, keys_in, values, allowed):
    logits = logits_of(queries, keys_in, allowed)
    row_peak = jnp.max(logits, axis=-1, keepdims=True)
    weights = jnp.exp(logits - row_peak)
    row_total = jnp.sum(weights, axis=-1, keepdims=True)
    softmax_out = (weights / row_total).astype(jnp.bfloat16)
    mixed_heads = jnp.einsum(
        "hqk,khd->qhd", softmax_out, heads_of(values), preferred_element_type=jnp.float32
    )
    return (
        mixed_heads.reshape(queries.shape[0], D).astype(jnp.bfloat16),
        row_peak + jnp.log(row_total),
    )


def attend_plain_back(queries, keys_in, values, allowed, log_total, grad_mixed):
    softmax_out = jnp.exp(logits_of(queries, keys_in, allowed) - log_total)
    grad_heads = heads_of(grad_mixed)
    grad_softmax = jnp.einsum(
        "qhd,khd->hqk", grad_heads, heads_of(values), preferred_element_type=jnp.float32
    )
    grad_values = jnp.einsum(
        "hqk,qhd->khd",
        softmax_out.astype(jnp.bfloat16),
        grad_heads,
        preferred_element_type=jnp.float32,
    )
    inner_sum = jnp.sum(softmax_out * grad_softmax, axis=-1, keepdims=True)
    grad_logits = (softmax_out * (grad_softmax - inner_sum) * HDIM ** (-0.5)).astype(jnp.bfloat16)
    grad_queries = jnp.einsum(
        "hqk,khd->qhd", grad_logits, heads_of(keys_in), preferred_element_type=jnp.float32
    )
    grad_keys = jnp.einsum(
        "hqk,qhd->khd", grad_logits, heads_of(queries), preferred_element_type=jnp.float32
    )
    query_count = queries.shape[0]
    key_count = keys_in.shape[0]
    return (
        grad_queries.reshape(query_count, D),
        grad_keys.reshape(key_count, D),
        grad_values.reshape(key_count, D),
    )


def self_forward(inputs, gain_row, w_attn, allowed):
    normed = rms_norm(inputs, gain_row).astype(jnp.bfloat16)
    packed = product(normed, w_attn[:, : 3 * D]).astype(jnp.bfloat16)
    mixed_heads, log_total = attend_plain(
        packed[:, :D], packed[:, D : 2 * D], packed[:, 2 * D :], allowed
    )
    return (
        inputs + product(mixed_heads, w_attn[:, 3 * D :]),
        (normed, packed, mixed_heads, log_total),
    )


def self_backward(inputs, gain_row, w_attn, allowed, kept_values, grad_result):
    normed, packed, mixed_heads, log_total = kept_values
    grad_low = grad_result.astype(jnp.bfloat16)
    grad_proj = weight_grad(mixed_heads, grad_low)
    grad_mixed = input_back(grad_low, w_attn[:, 3 * D :]).astype(jnp.bfloat16)
    grad_queries, grad_keys, grad_values = attend_plain_back(
        packed[:, :D], packed[:, D : 2 * D], packed[:, 2 * D :], allowed, log_total, grad_mixed
    )
    grad_packed = jnp.concatenate([grad_queries, grad_keys, grad_values], axis=1).astype(
        jnp.bfloat16
    )
    grad_qkv = weight_grad(normed, grad_packed)
    grad_inputs, grad_gain = norm_back(
        inputs, gain_row, input_back(grad_packed, w_attn[:, : 3 * D])
    )
    return (grad_result + grad_inputs, grad_gain, jnp.concatenate([grad_qkv, grad_proj], axis=1))


def gated_unit(gated):
    return jax.nn.gelu(gated[:, :FF], approximate=True) * gated[:, FF:]


def ffn_forward(inputs, gain_row, w_in, w_out):
    normed = rms_norm(inputs, gain_row).astype(jnp.bfloat16)
    gated = product(normed, w_in)
    hidden = gated_unit(gated).astype(jnp.bfloat16)
    return (inputs + product(hidden, w_out), (normed, gated, hidden))


def ffn_backward(inputs, gain_row, w_in, w_out, kept_values, grad_result):
    normed, gated, hidden = kept_values
    grad_low = grad_result.astype(jnp.bfloat16)
    grad_wout = weight_grad(hidden, grad_low)
    _, pull_back = jax.vjp(gated_unit, gated)
    grad_gated = pull_back(input_back(grad_low, w_out))[0].astype(jnp.bfloat16)
    grad_win = weight_grad(normed, grad_gated)
    grad_inputs, grad_gain = norm_back(inputs, gain_row, input_back(grad_gated, w_in))
    return (grad_result + grad_inputs, grad_gain, grad_win, grad_wout)


def encoder_forward(inputs, weights):
    w_attn, w_extra, w_in, w_out, gain_rows = weights
    middle, first_kept = self_forward(inputs, gain_rows[0], w_attn, None)
    result, second_kept = ffn_forward(middle, gain_rows[1], w_in, w_out)
    normed = rms_norm(result, gain_rows[2]).astype(jnp.bfloat16)
    cross_kv = product(normed, w_extra).astype(jnp.bfloat16)
    return (result, cross_kv, (middle, first_kept, second_kept, normed))


def encoder_backward(inputs, weights, grad_result, grad_kv):
    w_attn, w_extra, w_in, w_out, gain_rows = weights
    result, _, kept_values = encoder_forward(inputs, weights)
    middle, first_kept, second_kept, normed = kept_values
    grad_extra = weight_grad(normed, grad_kv)
    grad_final, gain_final = norm_back(result, gain_rows[2], input_back(grad_kv, w_extra))
    grad_middle, gain_late, grad_win, grad_wout = ffn_backward(
        middle, gain_rows[1], w_in, w_out, second_kept, grad_result + grad_final
    )
    grad_inputs, gain_early, grad_attn = self_backward(
        inputs, gain_rows[0], w_attn, None, first_kept, grad_middle
    )
    return (
        grad_inputs,
        (
            grad_attn,
            grad_extra,
            grad_win,
            grad_wout,
            jnp.stack([gain_early, gain_late, gain_final]),
        ),
    )


def decoder_step(inputs, cross_kv, allowed, weights, grad_result):
    w_attn, w_extra, w_in, w_out, gain_rows = weights
    middle, first_kept = self_forward(inputs, gain_rows[0], w_attn, allowed)
    query_in = rms_norm(middle, gain_rows[2]).astype(jnp.bfloat16)
    queries = product(query_in, w_extra[:, :D]).astype(jnp.bfloat16)
    mixed_heads, log_total = attend_plain(queries, cross_kv[:, :D], cross_kv[:, D:], None)
    after_cross = middle + product(mixed_heads, w_extra[:, D:])
    result, second_kept = ffn_forward(after_cross, gain_rows[1], w_in, w_out)
    grad_after, gain_late, grad_win, grad_wout = ffn_backward(
        after_cross, gain_rows[1], w_in, w_out, second_kept, grad_result
    )
    grad_low = grad_after.astype(jnp.bfloat16)
    grad_cross_out = weight_grad(mixed_heads, grad_low)
    grad_mixed = input_back(grad_low, w_extra[:, D:]).astype(jnp.bfloat16)
    grad_queries, grad_keys, grad_values = attend_plain_back(
        queries, cross_kv[:, :D], cross_kv[:, D:], None, log_total, grad_mixed
    )
    grad_queries = grad_queries.astype(jnp.bfloat16)
    grad_cross_in = weight_grad(query_in, grad_queries)
    grad_normed, gain_cross = norm_back(
        middle, gain_rows[2], input_back(grad_queries, w_extra[:, :D])
    )
    grad_inputs, gain_early, grad_attn = self_backward(
        inputs, gain_rows[0], w_attn, allowed, first_kept, grad_after + grad_normed
    )
    grad_kv = jnp.concatenate([grad_keys, grad_values], axis=1).astype(jnp.bfloat16)
    gradients = (
        grad_attn,
        jnp.concatenate([grad_cross_in, grad_cross_out], axis=1),
        grad_win,
        grad_wout,
        jnp.stack([gain_early, gain_late, gain_cross]),
    )
    return (result, grad_inputs, grad_kv, gradients)


def general(acts, w_attn, w_extra, w_in, w_out, gains, segments, cotangent):
    gathered = (
        lax.all_gather(w_attn[0], "dp", axis=0, tiled=True),
        lax.all_gather(w_extra[0], "dp", axis=0, tiled=True),
        lax.all_gather(w_in[0], "dp", axis=0, tiled=True),
        lax.all_gather(w_out[0], "dp", axis=0, tiled=True),
        lax.all_gather(gains[0], "dp", axis=1, tiled=True),
    )
    weights = gathered[:4] + (gathered[4].astype(jnp.float32),)
    inputs = acts[0, :, 0]
    upstream = cotangent[0, :, 0]
    is_first = lax.axis_index("section") == 0
    positions = jnp.arange(SEQ)
    causal = positions[None, :] <= positions[:, None]
    zero_message = jnp.zeros((SEQ, 2 * D), jnp.bfloat16)
    zero_grads = tuple((jnp.zeros(weight.shape, jnp.float32) for weight in weights))
    carried = (jnp.zeros((MICRO, SEQ, D), jnp.float32), jnp.zeros((MICRO, SEQ, D), jnp.float32))
    received = zero_message
    returned = zero_message
    totals = zero_grads
    moments = MICRO + 2
    for moment in range(moments):

        def first_section(carried, received, returned):
            results, grad_inputs = carried
            message = zero_message
            fresh_grads = zero_grads
            if moment < MICRO:
                result, message, _ = encoder_forward(inputs[moment], weights)
                results = results.at[moment].set(result)
            if moment >= 2:
                grad_rows, fresh_grads = encoder_backward(
                    inputs[moment - 2], weights, upstream[moment - 2], returned
                )
                grad_inputs = grad_inputs.at[moment - 2].set(grad_rows)
            return ((results, grad_inputs), message, zero_message, fresh_grads)

        def second_section(carried, received, returned):
            results, grad_inputs = carried
            message = zero_message
            fresh_grads = zero_grads
            if 1 <= moment <= MICRO:
                segment_ids = segments[moment - 1, 0]
                allowed = (segment_ids[:, None] == segment_ids[None, :]) & causal
                result, grad_rows, message, fresh_grads = decoder_step(
                    inputs[moment - 1], received, allowed, weights, upstream[moment - 1]
                )
                results = results.at[moment - 1].set(result)
                grad_inputs = grad_inputs.at[moment - 1].set(grad_rows)
            return ((results, grad_inputs), zero_message, message, fresh_grads)

        carried, forward_message, back_message, fresh_grads = lax.cond(
            is_first, first_section, second_section, carried, received, returned
        )
        if moment < MICRO:
            received = from_behind(forward_message, "section", 1)
        if 1 <= moment <= MICRO:
            returned = from_behind(back_message, "section", -1)
        if moment >= 1:
            totals = tuple((jnp.add(*couple) for couple in zip(totals, fresh_grads)))
    results, grad_inputs = carried
    final = (
        lax.psum_scatter(totals[0], "dp", scatter_dimension=0, tiled=True),
        lax.psum_scatter(totals[1], "dp", scatter_dimension=0, tiled=True),
        lax.psum_scatter(totals[2], "dp", scatter_dimension=0, tiled=True),
        lax.psum_scatter(totals[3], "dp", scatter_dimension=0, tiled=True),
        lax.psum_scatter(totals[4], "dp", scatter_dimension=1, tiled=True),
    )
    return (
        results[None, :, None],
        grad_inputs[None, :, None],
        final[0][None],
        final[1][None],
        final[2][None],
        final[3][None],
        final[4][None],
    )


def step(acts, w_attn, w_extra, w_in, w_out, gains, segments, cotangent):
    anywhere = pl.BlockSpec(memory_space=pl.ANY)
    shape = lambda *s: jax.ShapeDtypeStruct(s, F32)
    scratch = scratch_list()
    held = pl.pallas_call(
        whole_kernel,
        out_shape=(
            shape(ROWS, D), shape(ROWS, D), shape(48, 4 * D), shape(48, 2 * D), shape(48, 2 * FF), shape(128, D), shape(3, 48),
        ),
        in_specs=[anywhere] * 6 + [pl.BlockSpec(memory_space=pltpu.VMEM)] * 2,
        out_specs=[anywhere] * 7,
        scratch_shapes=list(scratch.values()),
        compiler_params=pltpu.CompilerParams(
            collective_id=0, has_side_effects=True, vmem_limit_bytes=63 * 2**20
        ),
    )(
        acts.reshape(ROWS, D), cotangent.reshape(ROWS, D), w_attn[0], w_extra[0], w_in[0], w_out[0], gains[0],
        segments.reshape(MICRO, SEQ),
    )
    results, input_grad, attn, extra, win, wout, grad_gains = held
    like = (1, MICRO, 1, SEQ, D)
    return (
        results.reshape(like), input_grad.reshape(like), attn[None], extra[None], win[None], wout[None], grad_gains[None],
    )


def solution(mesh):
    in_specs = (
        P("section", None, "dp", None, None),
        P("section", "dp", None),
        P("section", "dp", None),
        P("section", "dp", None),
        P("section", "dp", None),
        P("section", None, "dp"),
        P(None, "dp", None),
        P("section", None, "dp", None, None),
    )
    out_specs = (
        P("section", None, "dp", None, None),
        P("section", None, "dp", None, None),
        P("section", "dp", None),
        P("section", "dp", None),
        P("section", "dp", None),
        P("section", "dp", None),
        P("section", None, "dp"),
    )
    fits = mesh.shape["dp"] == 16
    return jax.shard_map(step if fits else general, mesh=mesh, in_specs=in_specs, out_specs=out_specs, check_vma=False)
```

```python
import jax
import jax.numpy as jnp
from jax import lax
from jax.experimental import pallas as pl
from jax.experimental.pallas import tpu as pltpu
from jax.sharding import PartitionSpec as P

D=768; HEADS=12; HDIM=64; FF=2048; SEQ=256; MICRO=2
ROWS=MICRO*SEQ
BF=jnp.bfloat16; F32=jnp.float32
QKV, OP, XA, XB, WIN, KV = 0, 3*D, 4*D, 5*D, 6*D, 6*D+2*FF
WIDE = KV + 2*D
NN=(((1,),(0,)),((),())); NT=(((1,),(1,)),((),()))

def mul(start, k): return pl.multiple_of(start, k)
def dot(a,b,dims=NN): return lax.dot_general(a,b,dims,preferred_element_type=F32)

def wide_cols(wa, start, size):
    return wa[:, :, :, :, pl.ds(start, size)].reshape(D, size)

def rms_rows(v):
    return lax.rsqrt(jnp.mean(v*v, axis=-1, keepdims=True) + 1e-6)

def norm_forward(v_ref, gain, n_ref, first=0, count=ROWS):
    @pl.loop(0, count//64)
    def _(i):
        rows=pl.ds(mul(first+i*64,64),64)
        v=v_ref[rows,:]
        n_ref[rows,:]=(v*rms_rows(v)*gain).astype(BF)

def norm_backward(v_ref, gain, dn_ref, g_ref, dgain_ref, slot, first=0, count=ROWS, low_ref=None):
    def body(i, acc):
        rows=pl.ds(mul(first+i*64,64),64)
        v=v_ref[rows,:]; dn=dn_ref[rows,:].astype(F32)
        r=rms_rows(v)
        t=dn*gain
        vr=v*r
        g=g_ref[rows,:]+r*(t-vr*jnp.mean(t*vr,axis=-1,keepdims=True))
        g_ref[rows,:]=g
        if low_ref is not None:
            low_ref[rows,:]=g.astype(BF)
        return acc+jnp.sum(dn*vr,axis=0,keepdims=True)
    acc=lax.fori_loop(0,count//64,body,jnp.zeros((1,D),F32))
    dgain_ref[slot:slot+1,:]+=acc

def transpose_to(src_ref, dst_ref, first=0, count=ROWS):
    cols=src_ref.shape[1]
    @pl.loop(0, cols//128)
    def _(j):
        cs=pl.ds(mul(j*128,128),128)
        dst_ref[cs, pl.ds(first,count)] = src_ref[pl.ds(first,count),cs].T

def project(n_ref, wa, wcol, out_ref, ocol, total, tile, first=0, count=ROWS):
    @pl.loop(0, total//tile)
    def _(j):
        w=wide_cols(wa, mul(wcol+j*tile,128), tile)
        out_ref[pl.ds(first,count), pl.ds(mul(ocol+j*tile,128),tile)] = dot(n_ref[pl.ds(first,count),:], w).astype(out_ref.dtype)

def project_add(a_ref, wa, wcol, base_ref, out_ref, tile, first=0, count=ROWS):
    rows=pl.ds(first,count)
    @pl.loop(0, D//tile)
    def _(j):
        w=wide_cols(wa, mul(wcol+j*tile,128), tile)
        cs=pl.ds(mul(j*tile,128),tile)
        out_ref[rows,cs] = base_ref[rows,cs]+dot(a_ref[rows,:], w)

def back_project(g_ref, gcol, wa, wcol, total, tile, acc_ref, first=0, count=ROWS, fresh=True):
    rows=pl.ds(first,count)
    def part(j):
        w=wide_cols(wa, mul(wcol+j*tile,128), tile)
        return dot(g_ref[rows, pl.ds(mul(gcol+j*tile,128),tile)], w, NT)
    if fresh:
        acc_ref[rows,:]=part(0)
    @pl.loop(1 if fresh else 0, total//tile)
    def _(j):
        acc_ref[rows,:]+=part(j)

def attend_forward(q_ref, qc, k_ref, kc, v_ref, vc, o_ref, oT_ref, mask_ref, start, stop, kept_ref=None, unroll=1):
    @pl.loop(start, stop, unroll=unroll)
    def _(i):
        img=i//6; p=i%6
        rows=pl.ds(mul(img*SEQ,SEQ),SEQ)
        def cols(base): return pl.ds(mul(base+p*128,128),128)
        q2=q_ref[rows,cols(qc)]*jnp.asarray(0.125,BF)
        k2=k_ref[rows,cols(kc)]
        vT=v_ref[rows,cols(vc)].T
        lane=lax.broadcasted_iota(jnp.int32,(SEQ,128),1)//64
        parts=[]
        for a in range(2):
            ka=jnp.where(lane==a,k2,jnp.zeros_like(k2))
            s=dot(ka,q2,NT)
            if mask_ref is not None:
                s=jnp.where(mask_ref[img].astype(F32)>0,s,-1e30)
            e=jnp.exp(s-jnp.max(s,axis=0,keepdims=True))
            w=(e*(1.0/jnp.sum(e,axis=0,keepdims=True))).astype(BF)
            if kept_ref is not None:
                kept_ref[pl.ds(mul(i*SEQ,SEQ),SEQ),a*SEQ:(a+1)*SEQ]=w
            parts.append(dot(vT[a*64:(a+1)*64],w))
        oT=jnp.concatenate(parts,axis=0).astype(BF)
        oT_ref[pl.ds(mul(p*128,128),128),rows]=oT
        o_ref[rows,cols(0)]=oT.T

def attend_backward(q_ref, qc, k_ref, kc, v_ref, vc, d_ref, mask_ref, dq_ref, dqc, dk_ref, dkc, dv_ref, dvc, start, stop, kept_ref=None):
    @pl.loop(start, stop)
    def _(i):
        img=i//6; p=i%6
        rows=pl.ds(mul(img*SEQ,SEQ),SEQ)
        def cols(base): return pl.ds(mul(base+p*128,128),128)
        q2=q_ref[rows,cols(qc)]
        qs=q2*jnp.asarray(0.125,BF)
        k2=k_ref[rows,cols(kc)]
        v2=v_ref[rows,cols(vc)]
        d2=d_ref[rows,cols(0)]
        kT=k2.T
        lane=lax.broadcasted_iota(jnp.int32,(SEQ,128),1)//64
        dqT=[]; dk=[]; dv=[]
        for a in range(2):
            mine=lane==a
            if kept_ref is not None:
                wb=kept_ref[pl.ds(mul(i*SEQ,SEQ),SEQ),a*SEQ:(a+1)*SEQ]
                w=wb.astype(F32)
            else:
                s=dot(jnp.where(mine,k2,jnp.zeros_like(k2)),qs,NT)
                if mask_ref is not None:
                    s=jnp.where(mask_ref[img].astype(F32)>0,s,-1e30)
                e=jnp.exp(s-jnp.max(s,axis=0,keepdims=True))
                w=e*(1.0/jnp.sum(e,axis=0,keepdims=True))
                wb=w.astype(BF)
            dw=dot(jnp.where(mine,v2,jnp.zeros_like(v2)),d2,NT)
            wd=w*dw
            ds=((wd-w*jnp.sum(wd,axis=0,keepdims=True))*0.125).astype(BF)
            dv.append(dot(wb,d2))
            dk.append(dot(ds,q2))
            dqT.append(dot(kT[a*64:(a+1)*64],ds))
        dq_ref[rows,cols(dqc)]=jnp.concatenate(dqT,axis=0).astype(BF).T
        dk_ref[rows,cols(dkc)]=jnp.where(lane==0,dk[0],dk[1]).astype(BF)
        dv_ref[rows,cols(dvc)]=jnp.where(lane==0,dv[0],dv[1]).astype(BF)

C0=0.7978845608028654; C1=0.044715
def gated_parts(n_ref, wa, j, rows, tile):
    gate=dot(n_ref[rows,:], wide_cols(wa, mul(WIN+j*tile,128), tile))
    up=dot(n_ref[rows,:], wide_cols(wa, mul(WIN+FF+j*tile,128), tile))
    sq=gate*gate
    t=jnp.tanh(gate*(C0+(C0*C1)*sq))
    h=0.5+0.5*t
    slope=h+(0.5*gate)*(1.0-t*t)*(C0+(3*C0*C1)*sq)
    return up, gate*h, slope

def gated_forward(n_ref, wa, gu_ref, hid_ref, start, stop, first=0, count=ROWS, tile=256):
    rows=pl.ds(first,count)
    @pl.loop(start, stop)
    def _(j):
        lo=pl.ds(mul(j*tile,tile),tile); hi=pl.ds(mul(FF+j*tile,tile),tile)
        up,act,slope=gated_parts(n_ref,wa,j,rows,tile)
        hid_ref[rows,lo]=(act*up).astype(BF)
        gu_ref[rows,lo]=(up*slope).astype(BF)
        gu_ref[rows,hi]=act.astype(BF)

def hidden_grad(gb_ref, wo, gu_ref):
    @pl.loop(0, 4, unroll=2)
    def _(j):
        gu_ref[:,pl.ds(mul(FF+j*512,512),512)]=dot(gb_ref[...], wo[j].reshape(512,D), NT).astype(BF)

def gated_both(n_ref, wa, gu_ref, hid_ref, start, stop, tile=256):
    rows=pl.ds(0,ROWS)
    @pl.loop(start, stop)
    def _(j):
        lo=pl.ds(mul(j*tile,tile),tile); hi=pl.ds(mul(FF+j*tile,tile),tile)
        up,act,slope=gated_parts(n_ref,wa,j,rows,tile)
        hid_ref[rows,lo]=(act*up).astype(BF)
        dh=gu_ref[rows,hi].astype(F32)
        gu_ref[rows,lo]=(dh*up*slope).astype(BF)
        gu_ref[rows,hi]=(dh*act).astype(BF)

def gated_backward(gb_ref, wo, gu_ref, first=0, count=ROWS):
    rows=pl.ds(first,count)
    @pl.loop(0, 4, unroll=4)
    def _(j):
        lo=pl.ds(mul(j*512,512),512); hi=pl.ds(mul(FF+j*512,512),512)
        dh=dot(gb_ref[rows,:], wo[j].reshape(512,D), NT)
        gu_ref[rows,lo]=(dh*gu_ref[rows,lo].astype(F32)).astype(BF)
        gu_ref[rows,hi]=(dh*gu_ref[rows,hi].astype(F32)).astype(BF)

def half_rows(nT_ref, c):
    return jnp.concatenate([nT_ref[pl.ds(mul((2*j+c)*48,16),48),:] for j in range(8)],axis=0)


MESH = pl.DeviceIdType.MESH
BIG = 1152

PARTS = {
    "q0": ("attn", 0, "wide", QKV, 1152), "q1": ("attn", 1152, "wide", QKV + 1152, 1152), "o": ("attn", 3 * D, "wide", OP, D),
    "g0": ("in", 0, "wide", WIN, 1024), "u0": ("in", FF, "wide", WIN + FF, 1024),
    "g1": ("in", 1024, "wide", WIN + 1024, 1024), "u1": ("in", FF + 1024, "wide", WIN + FF + 1024, 1024),
    "x0": ("extra", 0, "wide", XA, D), "x1": ("extra", D, "wide", XB, D),
    "k0": (None, 0, "wide", KV, D), "k1": (None, D, "wide", KV + D, D),
    "d0": ("out", 0, "tall", 0, 256), "d1": ("out", 256, "tall", 256, 256), "d2": ("out", 512, "tall", 512, 256),
}
PART_NAMES = tuple(PARTS)
ROUTES = (
    (("q0", "q1", "o", "g0", "u0", "g1", "u1", "d2"), {3: "d0", 5: "d1"}),
    (("q0", "q1", "o", "x0", "x1", "k0", "k1", "g0", "u0", "g1", "u1"), {2: "d0", 4: "d1", 7: "d2"}),
)
SUMS = {
    "out0": ("tall", 0, 384), "out1": ("tall", 384, 384),
    "in0": ("wide", WIN, 1024), "in1": ("wide", WIN + 1024, 1024),
    "in2": ("wide", WIN + FF, 1024), "in3": ("wide", WIN + FF + 1024, 1024),
    "x0": ("wide", XA, D), "x1": ("wide", XB, D),
    "k0": ("wide", KV, D), "k1": ("wide", KV + D, D),
    "o": ("wide", OP, D),
    "q0": ("wide", QKV, D), "q1": ("wide", QKV + D, D), "q2": ("wide", QKV + 2 * D, 384), "q3": ("wide", QKV + 2 * D + 384, 384),
}
SUM_NAMES = tuple(SUMS)
PAIRED = ("out1",)
SECOND_ONLY = ("x1", "k1")
DIRECT = ("q2", "q3")
OUT_OF = {
    "out0": ("out", 0), "out1": ("out", 384), "in0": ("in", 0), "in1": ("in", 1024), "in2": ("in", FF), "in3": ("in", FF + 1024),
    "x0": ("extra", 0), "x1": ("extra", D), "o": ("attn", 3 * D),
    "q0": ("attn", 0), "q1": ("attn", D), "q2": ("attn", 2 * D), "q3": ("attn", 2 * D + 384),
}
FREE = {"out": 0, "in": 1, "x": 2, "k": 3, "o": 4, "q": 5}


def scratch_list():
    V, DMA, REG = pltpu.VMEM, pltpu.SemaphoreType.DMA, pltpu.SemaphoreType.REGULAR
    n, s = len(PARTS), len(SUMS)
    return dict(
        wide=V((4, 2, 2, 48, WIDE), BF), tall=V((4, 2, 2, 128, D), BF),
        y_wide=V((4, 48, WIDE), BF), y_tall=V((4, 128, D), BF), pair_in=V((1, 3, 2, 128, 384), BF),
        stage=V((2, 4, 2, 48, 1024), BF), stage_tall=V((4, 2, 128, D), BF),
        fin=V((2, 48, 1024), F32), fin_tall=V((2, 128, 384), F32), fin_x=V((48, D), F32), fin_k=V((48, D), F32),
        x=V((ROWS, D), F32), mid=V((ROWS, D), F32), late=V((ROWS, D), F32), g=V((ROWS, D), F32),
        n1=V((ROWS, D), BF), n2=V((ROWS, D), BF), n3=V((ROWS, D), BF), xin=V((ROWS, D), BF), nT=V((D, ROWS), BF),
        qkv=V((ROWS, 3 * D), BF), ao=V((ROWS, D), BF), aoT=V((D, ROWS), BF),
        xq=V((ROWS, D), BF), kv=V((ROWS, 2 * D), BF), cmT=V((D, ROWS), BF),
        gu=V((ROWS, 2 * FF), BF), hid=V((ROWS, FF), BF), kept=V((12 * SEQ, 2 * SEQ), BF), gb=V((ROWS, D), BF), gb2=V((ROWS, D), BF),
        mask=V((MICRO, SEQ, SEQ), BF), xsend=V((ROWS, D), BF),
        gz=V((4, 8, D), F32), gy=V((2, 8, D), F32), gc=V((2, 8, D), F32), gain=V((8, D), F32),
        dgain=V((8, D), F32), gout=V((3, 48), F32), hz=V((4, 8, D), F32), hy=V((2, 8, D), F32), hc=V((2, 8, D), F32),
        s_in=DMA((3,)), s_own=DMA((n,)), s_kx=DMA, s_kr=DMA, s_hs=DMA, s_hr=DMA,
        s_rs=DMA((n, 3)), s_rr=DMA((n, 3)), s_ls=DMA((n, 3)), s_lr=DMA((n, 3)),
        s_ys=DMA((n, 4)), s_yr=DMA((n, 4)), s_cs=DMA((n,)), s_cr=DMA((n,)),
        s_ms=DMA((MICRO,)), s_mr=DMA((MICRO,)), s_gs=DMA((2, 5)), s_gr=DMA((2, 5)),
        t_cs=DMA((s,)), t_cr=DMA((s,)), t_ys=DMA((s,)), t_yr=DMA((s,)),
        t_rs=DMA((s,)), t_rr=DMA((s,)), t_ls=DMA((s,)), t_lr=DMA((s,)),
        t_ds=DMA((len(DIRECT), 3)), t_dr=DMA((len(DIRECT), 3)), t_xs=DMA((2,)), t_xr=DMA((2,)), t_out=DMA((s,)), s_out=DMA((3,)),
        free=REG((len(FREE),)), free_r=REG((s,)), free_l=REG((s,)),
    )


def whole_kernel(*refs):
    (acts_h, cot_h, attn_h, extra_h, in_h, out_h, gain_in, seg_in) = refs[:8]
    (res_o, grad_o, attn_o, extra_o, gin_o, gout_o, gain_o) = refs[8:15]
    R = type("Refs", (), {})()
    for name, ref in zip(scratch_list(), refs[15:]):
        setattr(R, name, ref)
    src = {"attn": attn_h, "extra": extra_h, "in": in_h, "out": out_h}
    dst = {"attn": attn_o, "extra": extra_o, "in": gin_o, "out": gout_o}
    buf = {"wide": R.wide, "tall": R.tall}
    ybuf = {"wide": R.y_wide, "tall": R.y_tall}

    R.acc = R.x
    hidT = R.kept.at[pl.ds(0, FF)]

    section = lax.axis_index("section")
    me = lax.axis_index("dp")
    z, y, c = me // 4, (me // 2) % 2, me % 2
    first, second = section == 0, section == 1
    at = lambda zz, yy, cc: {"dp": zz * 4 + yy * 2 + cc}
    right, left = at(lax.rem(z + 1, 4), y, c), at(lax.rem(z + 3, 4), y, c)
    z_peer = [at(lax.rem(z + k, 4), y, c) for k in (1, 2, 3)]
    y_peer, c_peer, x_peer = at(z, 1 - y, c), at(z, y, 1 - c), {"section": 1 - section}

    def remote(a, b, ss, rs, dev):
        return pltpu.make_async_remote_copy(a, b, ss, rs, device_id=dev, device_id_type=MESH)

    def local(a, b, s):
        return pltpu.make_async_copy(a, b, s)

    def when(cond, fn):
        pl.when(cond)(fn)

    barrier = pltpu.get_barrier_semaphore()
    everyone = z_peer + [y_peer, c_peer, x_peer]
    for peer in everyone:
        pl.semaphore_signal(barrier, inc=1, device_id=peer, device_id_type=MESH)
    pl.semaphore_wait(barrier, len(everyone))

    def spot(name):
        arg, lo, b, col, size = PARTS[name]
        return PART_NAMES.index(name), buf[b], pl.ds(col, size)

    def in_place(name):
        i, b, cs = spot(name)
        return b.at[z, y, c, :, cs]

    def shard(name):
        arg, lo, _, _, size = PARTS[name]
        return in_place(name) if arg is None else src[arg].at[:, pl.ds(lo, size)]

    def own_copy(name):
        return local(shard(name), in_place(name), R.s_own.at[PART_NAMES.index(name)])

    def line_block(name, zz, pair):
        i, b, cs = spot(name)
        return b.at[zz, :, c, :, cs] if pair else b.at[zz, y, c, :, cs]

    def go_right(name, s, pair):
        i = PART_NAMES.index(name)
        d = line_block(name, z - s, pair)
        return remote(shard(name) if s == 0 and not pair else d, d, R.s_rs.at[i, s], R.s_rr.at[i, s], right)

    def go_left(name, s, pair):
        i = PART_NAMES.index(name)
        d = line_block(name, z + s, pair)
        return remote(shard(name) if s == 0 and not pair else d, d, R.s_ls.at[i, s], R.s_lr.at[i, s], left)

    def from_left(name, s, pair):
        i = PART_NAMES.index(name)
        d = line_block(name, z - s, pair)
        return remote(d, d, R.s_rs.at[i, s - 1], R.s_rr.at[i, s - 1], left)

    def from_right(name, s, pair):
        i = PART_NAMES.index(name)
        d = line_block(name, z + s, pair)
        return remote(d, d, R.s_ls.at[i, s - 1], R.s_lr.at[i, s - 1], right)

    def across(name, zz, own=False, pair=False):
        i, b, cs = spot(name)
        d = b.at[zz, y, c, :, cs]
        k = 0 if pair else zz
        return remote(shard(name) if own else d, d, R.s_ys.at[i, k], R.s_yr.at[i, k], y_peer)

    def across_in(name, zz, pair=False):
        i, b, cs = spot(name)
        d = b.at[zz, 1 - y, c, :, cs]
        k = 0 if pair else zz
        return remote(d, d, R.s_ys.at[i, k], R.s_yr.at[i, k], y_peer)

    def to_core(name):
        i, b, cs = spot(name)
        d = b.at[:, :, c, :, cs]
        return remote(d, d, R.s_cs.at[i], R.s_cr.at[i], c_peer)

    def core_in(name):
        i, b, cs = spot(name)
        d = b.at[:, :, 1 - c, :, cs]
        return remote(d, d, R.s_cs.at[i], R.s_cr.at[i], c_peer)

    def ends(s, go, cond=None):
        when((z >= s) & (z < 3), lambda: go(0))
        when((z + s <= 3) & (z > 0), lambda: go(1))

    def begin(name, pair):
        if PARTS[name][0] is not None:
            own_copy(name).start()
        if name == "k0":
            kv_shard.wait_recv()
        if not pair:
            when(z < 3, lambda: go_right(name, 0, False).start())
            when(z > 0, lambda: go_left(name, 0, False).start())
        across(name, z, True, pair).start()

    def pair_turn(name):
        own_copy(name).wait()
        across_in(name, z, True).wait_recv()
        when(z < 3, lambda: go_right(name, 0, True).start())
        when(z > 0, lambda: go_left(name, 0, True).start())

    def hop(name, s, pair):
        def lower():
            from_left(name, s, pair).wait_recv()
            if s < 3:
                when(z < 3, lambda: go_right(name, s, pair).start())
            if not pair:
                across(name, z - s).start()

        def upper():
            from_right(name, s, pair).wait_recv()
            if s < 3:
                when(z > 0, lambda: go_left(name, s, pair).start())
            if not pair:
                across(name, z + s).start()

        when(z >= s, lower)
        when(z + s <= 3, upper)

    def line_done(name, pair):
        if not pair:
            if PARTS[name][0] is not None:
                own_copy(name).wait()
            for zz in range(4):
                across_in(name, zz).wait_recv()
        to_core(name).start()

    def have(*names):
        for name in names:
            core_in(name).wait_recv()

    def sent(name, pair):
        for s in range(3):
            when((z >= s) & (z < 3), lambda: go_right(name, s, pair).wait_send())
            when((z + s <= 3) & (z > 0), lambda: go_left(name, s, pair).wait_send())
        for zz in range(1 if pair else 4):
            across(name, zz, False, pair).wait_send()
        to_core(name).wait_send()

    def all_sent(who):
        line, pairs = ROUTES[who]
        for name in line:
            sent(name, False)
        for name in pairs.values():
            sent(name, True)

    def section_tick(who, t):
        line, pairs = ROUTES[who]
        n = len(line)
        for start, name in pairs.items():
            if t == start:
                begin(name, True)
            if t == start + 1:
                pair_turn(name)
            for s in (1, 2, 3):
                if t == start + 1 + s:
                    hop(name, s, True)
            if t == start + 5:
                line_done(name, True)
        if t < n:
            begin(line[t], False)
        for s in (1, 2, 3):
            if 0 <= t - s < n:
                hop(line[t - s], s, False)
        if 0 <= t - 4 < n:
            line_done(line[t - 4], False)

    def tick(t):
        when(first, lambda: section_tick(0, t))
        when(second, lambda: section_tick(1, t))

    kv_block = R.wide.at[z, y, c, :, pl.ds(KV, 2 * D)]
    kv_shard = remote(extra_h, kv_block, R.s_kx, R.s_kr, x_peer)
    when(first, lambda: kv_shard.start())

    share = gain_in.shape[1]
    spread = (
        lax.broadcasted_iota(jnp.int32, (share, D), 1) - me * share == lax.broadcasted_iota(jnp.int32, (share, D), 0)
    ).astype(F32)
    R.gz[z] = jnp.zeros((8, D), F32)
    R.gz[z, 0:3, :] = dot(gain_in[...], spread.astype(BF))
    x_in = local(acts_h, R.x, R.s_in.at[1])
    x_in.start()
    g_in = local(cot_h, R.g, R.s_in.at[2])
    g_in.start()

    def small_z(own_ref, slots, row):
        return [remote(own_ref, slots.at[z], R.s_gs.at[row, k], R.s_gr.at[row, k], z_peer[k]) for k in range(3)]

    def small_pair(slots, row, k, dev):
        return remote(slots.at[0], slots.at[1], R.s_gs.at[row, k], R.s_gr.at[row, k], dev)

    gzc = small_z(R.gz.at[z], R.gz, 0)
    for q in gzc:
        q.start()
    tick(0)
    tick(1)
    for q in gzc:
        q.wait_recv()
    R.gy[0] = (R.gz[0] + R.gz[1]) + (R.gz[2] + R.gz[3])
    q = small_pair(R.gy, 0, 3, y_peer)
    q.start()
    tick(2)
    q.wait()
    R.gc[0] = R.gy[0] + R.gy[1]
    q = small_pair(R.gc, 0, 4, c_peer)
    q.start()
    tick(3)
    q.wait()
    R.gain[...] = R.gc[0] + R.gc[1]
    for q in gzc:
        q.wait_send()
    gain = lambda k: R.gain[k : k + 1, :]

    ones = jnp.where(first, 1.0, 0.0)
    for img in range(MICRO):
        row = jnp.broadcast_to(seg_in[img : img + 1, :].astype(F32), (SEQ, SEQ))
        key = lax.broadcasted_iota(jnp.int32, (SEQ, SEQ), 0)
        query = lax.broadcasted_iota(jnp.int32, (SEQ, SEQ), 1)
        allowed = jnp.where((row.T == row) & (key <= query), 1.0, ones)
        R.mask[img] = allowed.astype(BF)
    R.dgain[...] = jnp.zeros_like(R.dgain)

    x_in.wait()
    norm_forward(R.x, gain(0), R.n1)
    for t in range(4, 6):
        tick(t)
    have("q0", "q1")
    project(R.n1, R.wide, QKV, R.qkv, 0, 3 * D, 768)
    tick(6)

    def self_attention(a, b):
        attend_forward(R.qkv, 0, R.qkv, D, R.qkv, 2 * D, R.ao, R.aoT, R.mask, a, b)

    self_attention(0, 4)
    tick(7)
    self_attention(4, 8)
    tick(8)
    self_attention(8, 12)
    tick(9)
    have("o")
    project_add(R.ao, R.wide, OP, R.x, R.mid, 384)

    def message(img):
        rows = pl.ds(img * SEQ, SEQ)
        return remote(R.xsend.at[rows], R.xin.at[rows], R.s_ms.at[img], R.s_mr.at[img], x_peer)

    def down(base, out, cols, first_row=0, count=ROWS):
        rows = pl.ds(first_row, count)
        for lo in cols:
            cs = pl.ds(lo, 256)
            out[rows, cs] = base[rows, cs] + dot(R.hid[rows, :], R.tall[:, :, :, :, cs].reshape(FF, 256))

    def round_g(to, first_row=0, count=ROWS):
        rows = pl.ds(first_row, count)
        to[rows, :] = R.g[rows, :].astype(BF)

    def enc_forward():
        norm_forward(R.mid, gain(1), R.n2)
        have("g0", "u0")
        gated_forward(R.n2, R.wide, R.gu, R.hid, 0, 1, tile=512)
        section_tick(0, 10)
        gated_forward(R.n2, R.wide, R.gu, R.hid, 1, 2, tile=512)
        have("g1", "u1")
        gated_forward(R.n2, R.wide, R.gu, R.hid, 1, 2, tile=1024)
        section_tick(0, 11)
        have("d0", "d1")
        down(R.mid, R.late, (0, 256))
        have("d2")
        for img in range(MICRO):
            down(R.mid, R.late, (512,), img * SEQ, SEQ)
            norm_forward(R.late, gain(2), R.xsend, img * SEQ, SEQ)
            message(img).start()
        all_sent(0)
        kv_shard.wait_send()

    def dec_forward():
        norm_forward(R.mid, gain(2), R.n3)
        section_tick(1, 10)
        have("x0")
        project(R.n3, R.wide, XA, R.xq, 0, D, 384)
        section_tick(1, 11)
        section_tick(1, 12)
        have("d0", "d1", "d2")
        g_in.wait()
        round_g(R.gb)
        hidden_grad(R.gb, R.tall, R.gu)
        section_tick(1, 13)
        have("x1", "k0", "k1")

        def cross(img):
            message(img).wait_recv()
            project(R.xin, R.wide, KV, R.kv, 0, 2 * D, 768, img * SEQ, SEQ)
            attend_forward(R.xq, 0, R.kv, 0, R.kv, D, R.ao, R.cmT, None, img * 6, img * 6 + 6, R.kept, 3)

        cross(0)
        section_tick(1, 14)
        cross(1)
        project_add(R.ao, R.wide, XB, R.mid, R.late, 384)
        norm_forward(R.late, gain(1), R.n2)
        have("g0", "u0", "g1", "u1")
        gated_both(R.n2, R.wide, R.gu, R.hid, 0, 2, 1024)
        all_sent(1)

    def sum_spot(name):
        b, lo, size = SUMS[name]
        return SUM_NAMES.index(name), b, pl.ds(lo, size), size

    stage_of = {}

    def core_copy(name):
        k, b, cs, size = sum_spot(name)
        if b == "tall":
            s = R.stage_tall.at[:, :, :, cs]
        else:
            s = R.stage.at[stage_of[name], :, :, :, pl.ds(0, size)]
        return remote(s, buf[b].at[:, :, c, :, cs], R.t_cs.at[k], R.t_cr.at[k], c_peer)

    def paired(name):
        return name in PAIRED

    def y_copy(name):
        k, b, cs, size = sum_spot(name)
        if paired(name):
            return remote(buf[b].at[z, 1 - y, c, :, cs], ybuf[b].at[0, :, cs], R.t_ys.at[k], R.t_yr.at[k], y_peer)
        return remote(buf[b].at[:, 1 - y, c, :, cs], ybuf[b].at[:, :, cs], R.t_ys.at[k], R.t_yr.at[k], y_peer)

    def moving(name, a, e):
        _, b, cs, _ = sum_spot(name)
        return buf[b].at[a:e, :, c, :, cs] if paired(name) else buf[b].at[a:e, y, c, :, cs]

    def landing_left(name, a, e):
        _, b, cs, _ = sum_spot(name)
        return buf[b].at[a:e, :, 1 - c, :, cs] if paired(name) else buf[b].at[a:e, 0, 1 - c, :, cs]

    def landing_right(name, a, e):
        _, b, cs, size = sum_spot(name)
        if paired(name):
            return R.pair_in.at[PAIRED.index(name), a:e]
        return buf[b].at[a:e, 1, 1 - c, :, cs]

    def right_copy(name, zz):
        k = SUM_NAMES.index(name)
        return remote(moving(name, zz + 1, 4), landing_left(name, zz + 1, 4), R.t_rs.at[k], R.t_rr.at[k], right)

    def left_copy(name, zz):
        k = SUM_NAMES.index(name)
        return remote(moving(name, 0, zz), landing_right(name, 0, zz), R.t_ls.at[k], R.t_lr.at[k], left)

    def send_right(name, zz):
        pl.semaphore_wait(R.free_r.at[SUM_NAMES.index(name)], 1)
        right_copy(name, zz).start()

    def send_left(name, zz):
        pl.semaphore_wait(R.free_l.at[SUM_NAMES.index(name)], 1)
        left_copy(name, zz).start()

    def add_blocks(name, landed, a, e):
        mine = moving(name, a, e)

        @pl.loop(0, e - a)
        def _(j):
            mine[j] = (mine[j].astype(F32) + landed[j].astype(F32)).astype(BF)

    def add_left(name, zz):
        k = SUM_NAMES.index(name)
        d = landing_left(name, zz, 4)
        remote(d, d, R.t_rs.at[k], R.t_rr.at[k], left).wait_recv()
        add_blocks(name, d, zz, 4)

    def add_right(name, zz):
        k = SUM_NAMES.index(name)
        d = landing_right(name, 0, zz + 1)
        remote(d, d, R.t_ls.at[k], R.t_lr.at[k], right).wait_recv()
        add_blocks(name, d, 0, zz + 1)

    def open_line(name):
        k = SUM_NAMES.index(name)
        if name in DIRECT:
            for peer in z_peer:
                pl.semaphore_signal(R.free_r.at[k], inc=1, device_id=peer, device_id_type=MESH)
            return
        when(z > 0, lambda: pl.semaphore_signal(R.free_r.at[k], inc=1, device_id=left, device_id_type=MESH))
        when(z < 3, lambda: pl.semaphore_signal(R.free_l.at[k], inc=1, device_id=right, device_id_type=MESH))

    def straight(name):
        k, b, cs, size = sum_spot(name)
        d, w = DIRECT.index(name), buf[b]
        return [
            remote(
                w.at[lax.rem(z + j + 1, 4), y, c, :, cs], w.at[z, 0, 1 - c, :, cs], R.t_ds.at[d, j], R.t_dr.at[d, j], z_peer[j]
            )
            for j in range(3)
        ]

    def collect(name):
        k, b, cs, size = sum_spot(name)
        d, w = DIRECT.index(name), buf[b]
        total = w[z, y, c, :, cs].astype(F32)
        for j in range(3):
            landed = w.at[lax.rem(z + 3 - j, 4), 0, 1 - c, :, cs]
            remote(landed, landed, R.t_ds.at[d, j], R.t_dr.at[d, j], z_peer[2 - j]).wait_recv()
            total = total + landed[...].astype(F32)
        finish(name, total)

    def line_a(name):
        when(z == 0, lambda: send_right(name, 0))
        when(z == 3, lambda: send_left(name, 3))

    def line_b(name):
        def one():
            add_left(name, 1)
            send_right(name, 1)

        def two():
            add_right(name, 2)
            send_left(name, 2)

        when(z == 1, one)
        when(z == 2, two)

    def line_c(name):
        def one():
            add_right(name, 1)
            send_left(name, 1)

        def two():
            add_left(name, 2)
            send_right(name, 2)

        when(z == 1, one)
        when(z == 2, two)

    def line_d(name):
        when(z == 0, lambda: add_right(name, 0))
        when(z == 3, lambda: add_left(name, 3))

    def line_sent(name):
        if name in DIRECT:
            for q in straight(name):
                q.wait_send()
            return
        for zz in range(3):
            when(z == zz, lambda: right_copy(name, zz).wait_send())
            when(z == zz + 1, lambda: left_copy(name, zz + 1).wait_send())

    def release(name):
        pl.semaphore_signal(R.free.at[FREE[name]], inc=1, device_id=c_peer, device_id_type=MESH)

    def claim(name):
        pl.semaphore_wait(R.free.at[FREE[name]], 1)

    order = []

    def grad_wide(name, nT, g_ref, gcol, tile):
        k, b, cs, size = sum_spot(name)
        lo = SUMS[name][1]
        slot = len(order) % 2
        if len(order) >= 2:
            core_copy(order[-2]).wait_send()
        stage_of[name] = slot
        order.append(name)
        lhs = half_rows(nT, 1 - c)

        @pl.loop(0, size // tile)
        def _(j):
            w = dot(lhs, g_ref[:, pl.ds(mul(gcol + j * tile, 128), tile)]).astype(BF)
            R.stage[slot, :, :, :, pl.ds(mul(j * tile, 128), tile)] = w.reshape(4, 2, 48, tile)

        core_copy(name).start()
        mine = half_rows(nT, c)

        @pl.loop(0, size // tile)
        def _(j):
            w = dot(mine, g_ref[:, pl.ds(mul(gcol + j * tile, 128), tile)]).astype(BF)
            R.wide[:, :, c, :, pl.ds(mul(lo + j * tile, 128), tile)] = w.reshape(4, 2, 48, tile)

    def drain():
        for name in order[-2:]:
            core_copy(name).wait_send()
        order.clear()

    def grad_tall(name):
        k, b, cs, size = sum_spot(name)

        def rows_of(j, cc):
            units = [hidT[pl.ds(mul((8 * j + 2 * i + cc) * 128, 128), 128), :] for i in range(4)]
            return dot(jnp.concatenate(units, axis=0), R.gb[:, cs]).astype(BF).reshape(2, 2, 128, size)

        @pl.loop(0, 2)
        def _(j):
            R.stage_tall[pl.ds(2 * j, 2), :, :, cs] = rows_of(j, 1 - c)

        core_copy(name).start()

        @pl.loop(0, 2)
        def _(j):
            R.tall[pl.ds(2 * j, 2), :, c, :, cs] = rows_of(j, c)

    ready, crossing, moving_on, finished = [], [], [], []

    def on(name, fn):
        if name in SECOND_ONLY:
            when(second, fn)
        else:
            fn()

    def feed():
        while ready and len([n for n in crossing if n not in SECOND_ONLY]) < 4:
            name = ready.pop(0)
            on(name, lambda: y_copy(name).start())
            crossing.append(name)

    def core_stage(name, pass_on=True):
        k, b, cs, size = sum_spot(name)
        w = buf[b]
        landed = w.at[:, :, 1 - c, :, cs]
        remote(landed, landed, R.t_cs.at[k], R.t_cr.at[k], c_peer).wait_recv()

        @pl.loop(0, 8)
        def _(j):
            own = w[j // 2, j % 2, c, :, cs].astype(F32)
            w[j // 2, j % 2, c, :, cs] = (own + w[j // 2, j % 2, 1 - c, :, cs].astype(F32)).astype(BF)

        if pass_on:
            enter(name)

    def enter(name):
        on(name, lambda: open_line(name))
        if paired(name):
            line_a(name)
            moving_on.append([name, later, line_b, later, line_c, later, line_d, late_cross])
        else:
            ready.append(name)
            feed()

    def later(name):
        pass

    def late_cross(name):
        y_copy(name).start()
        crossing.append(name)

    def y_stage(name):
        k, b, cs, size = sum_spot(name)
        w, r = buf[b], ybuf[b]
        if paired(name):
            d = r.at[0, :, cs]
            remote(d, d, R.t_ys.at[k], R.t_yr.at[k], y_peer).wait_recv()
            finish(name, w[z, y, c, :, cs].astype(F32) + r[0, :, cs].astype(F32))
            return
        y_copy(name).wait_recv()

        @pl.loop(0, 4)
        def _(j):
            w[j, y, c, :, cs] = (w[j, y, c, :, cs].astype(F32) + r[j, :, cs].astype(F32)).astype(BF)

        if name in DIRECT:
            pl.semaphore_wait(R.free_r.at[k], 3)
            for q in straight(name):
                q.start()
            moving_on.append([name, later, collect])
            return
        line_a(name)
        moving_on.append([name, later, line_b, line_c, line_d, last])

    def last(name):
        k, b, cs, size = sum_spot(name)
        total = buf[b][z, y, c, :, cs].astype(F32)
        if name not in SECOND_ONLY:
            finish(name, total)
        elif name == "x1":
            R.fin_x[...] = total
            x_out.start()
        else:
            R.fin_k[...] = total
            key_home.start()

    def turn():
        going = list(moving_on)
        while crossing:
            name = crossing.pop(0)
            on(name, lambda: y_stage(name))
            feed()
            if name not in SECOND_ONLY:
                break
        for item in going:
            while not crossing and len(item) > 2 and item[1] is later:
                item.pop(1)
            fn = item.pop(1)
            on(item[0], lambda: fn(item[0]))
            if len(item) == 1:
                moving_on.remove(item)

    def out_copy(name):
        k, b, cs, size = sum_spot(name)
        arg, lo = OUT_OF[name]
        kind = [f for f in finished if SUMS[f][0] == b]
        slot = kind.index(name) % 2
        f = R.fin_tall.at[slot] if b == "tall" else R.fin.at[slot, :, pl.ds(0, size)]
        return local(f, dst[arg].at[:, pl.ds(lo, size)], R.t_out.at[k])

    def finish(name, total):
        k, b, cs, size = sum_spot(name)
        kind = [f for f in finished if SUMS[f][0] == b]
        slot = len(kind) % 2
        if len(kind) >= 2:
            out_copy(kind[-2]).wait()
        finished.append(name)
        if b == "tall":
            R.fin_tall[slot] = total
        else:
            R.fin[slot, :, pl.ds(0, size)] = total
        out_copy(name).start()

    x_out = local(R.fin_x, extra_o.at[:, pl.ds(D, D)], R.t_out.at[SUM_NAMES.index("x1")])
    key_home = remote(R.fin_k, R.fin_x, R.s_hs, R.s_hr, x_peer)

    def over_copy(j):
        k, b, cs, size = sum_spot(("k0", "k1")[j])
        return remote(
            R.wide.at[:, :, c, :, cs], R.wide.at[:, :, c, :, pl.ds(XA + j * D, D)], R.t_xs.at[j], R.t_xr.at[j], x_peer
        )

    def project_back(g_ref, wcol, out_ref):
        out_ref[...] = dot(g_ref[...], wide_cols(R.wide, wcol, D), NT).astype(BF)

    def down_grads():
        release("out")
        claim("out")
        grad_tall("out0")
        core_stage("out0")
        grad_tall("out1")
        core_stage("out1")

    def in_grads():
        release("in")
        claim("in")
        grad_wide("in0", R.nT, R.gu, 0, 512)
        grad_wide("in1", R.nT, R.gu, 1024, 512)
        core_stage("in0")
        turn()
        grad_wide("in2", R.nT, R.gu, FF, 512)
        core_stage("in1")
        grad_wide("in3", R.nT, R.gu, FF + 1024, 512)
        core_stage("in2")

    gains_own = lambda: small_pair(R.hc, 1, 4, c_peer)
    gains_row = lambda: small_pair(R.hy, 1, 3, y_peer)
    gains_line = lambda: small_z(R.gain, R.hz, 1)
    gain_copy = local(R.gout, gain_o, R.s_out.at[2])
    grad_copy = local(R.g, grad_o, R.s_out.at[1])

    def gains_a():
        R.hc[0] = R.dgain[...]
        gains_own().start()

    def gains_b(_):
        gains_own().wait()
        R.hy[0] = R.hc[0] + R.hc[1]
        gains_row().start()

    def gains_c(_):
        gains_row().wait()
        R.gain[...] = R.hy[0] + R.hy[1]
        for q in gains_line():
            q.start()

    def gains_d(_):
        for q in gains_line():
            q.wait()
        R.hz[z] = R.gain[...]
        whole = (R.hz[0] + R.hz[1]) + (R.hz[2] + R.hz[3])
        own = lax.dot_general(whole, spread, NT, precision=lax.Precision.HIGHEST, preferred_element_type=F32)
        R.gout[...] = own[0:3]
        gain_copy.start()

    dec_res = local(R.acc, res_o, R.s_out.at[0])
    enc_res = local(R.late, res_o, R.s_out.at[0])

    def dec_middle():
        back_project(R.gu, 0, R.wide, WIN, 2 * FF, 2048, R.acc)
        norm_backward(R.late, gain(1), R.acc, R.g, R.dgain, 1, low_ref=R.gb2)
        project_back(R.gb2, XB, R.xsend)
        for img in range(MICRO):
            attend_backward(
                R.xq, 0, R.kv, 0, R.kv, D, R.xsend, None, R.xq, 0, R.kv, 0, R.kv, D, img * 6, img * 6 + 6, R.kept
            )
            back_project(R.kv, 0, R.wide, KV, 2 * D, 768, R.acc, img * SEQ, SEQ)
            rows = pl.ds(img * SEQ, SEQ)
            R.xsend[rows, :] = R.acc[rows, :].astype(BF)
            message(img).start()
        down(R.late, R.acc, (0, 256, 512))
        dec_res.start()
        transpose_to(R.hid, hidT)

    def dec_all():
        dec_forward()
        dec_middle()

    def enc_middle():
        enc_res.start()
        transpose_to(R.hid, hidT)
        transpose_to(R.n2, R.nT)
        g_in.wait()
        for img in range(MICRO):
            message(img).wait_send()
        for img in range(MICRO):
            lo = img * SEQ
            message(img).wait_recv()
            norm_backward(R.late, gain(2), R.xin, R.g, R.dgain, 2, lo, SEQ, R.gb)
            gated_backward(R.gb, R.tall, R.gu, lo, SEQ)

    def enc_in():
        back_project(R.gu, 0, R.wide, WIN, 2 * FF, 2048, R.acc)
        norm_backward(R.mid, gain(1), R.acc, R.g, R.dgain, 1, low_ref=R.gb2)

    def dec_keys():
        release("k")
        transpose_to(R.xin, R.nT)
        claim("k")
        grad_wide("k0", R.nT, R.kv, 0, 384)
        grad_wide("k1", R.nT, R.kv, D, 384)
        core_stage("k0", False)
        over_copy(0).start()
        core_stage("k1", False)
        drain()
        transpose_to(R.n2, R.nT)

    def dec_cross():
        dec_res.wait()
        back_project(R.xq, 0, R.wide, XA, D, 768, R.acc)
        release("x")
        transpose_to(R.n3, R.nT)
        claim("x")
        grad_wide("x0", R.nT, R.xq, 0, 384)
        grad_wide("x1", R.cmT, R.gb2, 0, 384)
        core_stage("x0", False)
        core_stage("x1", False)
        norm_backward(R.mid, gain(2), R.acc, R.g, R.dgain, 2, low_ref=R.gb2)
        for img in range(MICRO):
            message(img).wait_send()
        drain()

    when(first, enc_forward)
    when(second, dec_all)
    when(first, enc_middle)
    down_grads()
    when(first, enc_in)
    when(second, dec_keys)
    in_grads()
    drain()
    core_stage("in3")
    when(second, dec_cross)

    enter("x1")
    enter("k1")

    when(first, lambda: enc_res.wait())
    x_again = local(acts_h, R.late, R.s_in.at[1])
    x_again.start()
    project_back(R.gb2, OP, R.ao)
    release("o")
    claim("o")
    grad_wide("o", R.aoT, R.gb2, 0, 384)
    turn()
    attend_backward(R.qkv, 0, R.qkv, D, R.qkv, 2 * D, R.ao, R.mask, R.qkv, 0, R.qkv, D, R.qkv, 2 * D, 0, 6)
    core_stage("o")
    turn()
    attend_backward(R.qkv, 0, R.qkv, D, R.qkv, 2 * D, R.ao, R.mask, R.qkv, 0, R.qkv, D, R.qkv, 2 * D, 6, 12)
    turn()
    back_project(R.qkv, 0, R.wide, QKV, 3 * D, 768, R.acc)
    release("q")
    transpose_to(R.n1, R.nT)
    claim("q")
    when(first, lambda: over_copy(0).wait_recv())
    enter("x0")
    grad_wide("q0", R.nT, R.qkv, 0, 384)
    grad_wide("q1", R.nT, R.qkv, D, 384)
    core_stage("q0")
    grad_wide("q2", R.nT, R.qkv, 2 * D, 384)
    core_stage("q1")
    grad_wide("q3", R.nT, R.qkv, 2 * D + 384, 384)
    core_stage("q2")
    core_stage("q3")
    turn()
    x_again.wait()
    norm_backward(R.late, gain(0), R.acc, R.g, R.dgain, 0)
    grad_copy.start()
    gains_a()
    moving_on.append(["gains", gains_b, later, later, later, gains_c, later, later, gains_d])
    while ready or crossing or moving_on:
        turn()
    for name in ("out0", "out1"):
        core_copy(name).wait_send()
    drain()
    def all_gone(name):
        y_copy(name).wait_send()
        line_sent(name)

    for name in finished + list(SECOND_ONLY):
        on(name, lambda: all_gone(name))
    for b in ("tall", "wide"):
        for name in [f for f in finished if SUMS[f][0] == b][-2:]:
            out_copy(name).wait()

    def dec_end():
        over_copy(0).wait_send()
        x_out.wait()
        key_home.wait_send()

    def enc_end():
        key_home.wait_recv()
        x_out.start()
        x_out.wait()

    when(second, dec_end)
    when(first, enc_end)
    grad_copy.wait()
    gain_copy.wait()


def from_behind(block, axis, distance):
    devices = range(lax.axis_size(axis))
    route = [(i - distance, i) for i in devices if i - distance in devices]
    return lax.ppermute(block, axis, route)


def rms_norm(activations, gain_row):
    return (
        activations
        * lax.rsqrt(jnp.mean(activations * activations, axis=-1, keepdims=True) + 1e-06)
        * gain_row
    )


def product(left_side, right_side):
    return jnp.dot(left_side, right_side, preferred_element_type=jnp.float32)


def weight_grad(left_side, right_side):
    return jnp.einsum("sd,se->de", left_side, right_side, preferred_element_type=jnp.float32)


def input_back(gradient, weight):
    return jnp.einsum("se,de->sd", gradient, weight, preferred_element_type=jnp.float32)


def norm_back(activations, gain_row, gradient):
    _, pull_back = jax.vjp(rms_norm, activations, gain_row)
    return pull_back(gradient)


def heads_of(activations):
    return activations.reshape(activations.shape[0], HEADS, HDIM)


def logits_of(queries, keys_in, allowed):
    raw_logits = jnp.einsum(
        "qhd,khd->hqk", heads_of(queries), heads_of(keys_in), preferred_element_type=jnp.float32
    ) * HDIM ** (-0.5)
    if allowed is None:
        return raw_logits
    return jnp.where(allowed[None], raw_logits, -1e30)


def attend_plain(queries, keys_in, values, allowed):
    logits = logits_of(queries, keys_in, allowed)
    row_peak = jnp.max(logits, axis=-1, keepdims=True)
    weights = jnp.exp(logits - row_peak)
    row_total = jnp.sum(weights, axis=-1, keepdims=True)
    softmax_out = (weights / row_total).astype(jnp.bfloat16)
    mixed_heads = jnp.einsum(
        "hqk,khd->qhd", softmax_out, heads_of(values), preferred_element_type=jnp.float32
    )
    return (
        mixed_heads.reshape(queries.shape[0], D).astype(jnp.bfloat16),
        row_peak + jnp.log(row_total),
    )


def attend_plain_back(queries, keys_in, values, allowed, log_total, grad_mixed):
    softmax_out = jnp.exp(logits_of(queries, keys_in, allowed) - log_total)
    grad_heads = heads_of(grad_mixed)
    grad_softmax = jnp.einsum(
        "qhd,khd->hqk", grad_heads, heads_of(values), preferred_element_type=jnp.float32
    )
    grad_values = jnp.einsum(
        "hqk,qhd->khd",
        softmax_out.astype(jnp.bfloat16),
        grad_heads,
        preferred_element_type=jnp.float32,
    )
    inner_sum = jnp.sum(softmax_out * grad_softmax, axis=-1, keepdims=True)
    grad_logits = (softmax_out * (grad_softmax - inner_sum) * HDIM ** (-0.5)).astype(jnp.bfloat16)
    grad_queries = jnp.einsum(
        "hqk,khd->qhd", grad_logits, heads_of(keys_in), preferred_element_type=jnp.float32
    )
    grad_keys = jnp.einsum(
        "hqk,qhd->khd", grad_logits, heads_of(queries), preferred_element_type=jnp.float32
    )
    query_count = queries.shape[0]
    key_count = keys_in.shape[0]
    return (
        grad_queries.reshape(query_count, D),
        grad_keys.reshape(key_count, D),
        grad_values.reshape(key_count, D),
    )


def self_forward(inputs, gain_row, w_attn, allowed):
    normed = rms_norm(inputs, gain_row).astype(jnp.bfloat16)
    packed = product(normed, w_attn[:, : 3 * D]).astype(jnp.bfloat16)
    mixed_heads, log_total = attend_plain(
        packed[:, :D], packed[:, D : 2 * D], packed[:, 2 * D :], allowed
    )
    return (
        inputs + product(mixed_heads, w_attn[:, 3 * D :]),
        (normed, packed, mixed_heads, log_total),
    )


def self_backward(inputs, gain_row, w_attn, allowed, kept_values, grad_result):
    normed, packed, mixed_heads, log_total = kept_values
    grad_low = grad_result.astype(jnp.bfloat16)
    grad_proj = weight_grad(mixed_heads, grad_low)
    grad_mixed = input_back(grad_low, w_attn[:, 3 * D :]).astype(jnp.bfloat16)
    grad_queries, grad_keys, grad_values = attend_plain_back(
        packed[:, :D], packed[:, D : 2 * D], packed[:, 2 * D :], allowed, log_total, grad_mixed
    )
    grad_packed = jnp.concatenate([grad_queries, grad_keys, grad_values], axis=1).astype(
        jnp.bfloat16
    )
    grad_qkv = weight_grad(normed, grad_packed)
    grad_inputs, grad_gain = norm_back(
        inputs, gain_row, input_back(grad_packed, w_attn[:, : 3 * D])
    )
    return (grad_result + grad_inputs, grad_gain, jnp.concatenate([grad_qkv, grad_proj], axis=1))


def gated_unit(gated):
    return jax.nn.gelu(gated[:, :FF], approximate=True) * gated[:, FF:]


def ffn_forward(inputs, gain_row, w_in, w_out):
    normed = rms_norm(inputs, gain_row).astype(jnp.bfloat16)
    gated = product(normed, w_in)
    hidden = gated_unit(gated).astype(jnp.bfloat16)
    return (inputs + product(hidden, w_out), (normed, gated, hidden))


def ffn_backward(inputs, gain_row, w_in, w_out, kept_values, grad_result):
    normed, gated, hidden = kept_values
    grad_low = grad_result.astype(jnp.bfloat16)
    grad_wout = weight_grad(hidden, grad_low)
    _, pull_back = jax.vjp(gated_unit, gated)
    grad_gated = pull_back(input_back(grad_low, w_out))[0].astype(jnp.bfloat16)
    grad_win = weight_grad(normed, grad_gated)
    grad_inputs, grad_gain = norm_back(inputs, gain_row, input_back(grad_gated, w_in))
    return (grad_result + grad_inputs, grad_gain, grad_win, grad_wout)


def encoder_forward(inputs, weights):
    w_attn, w_extra, w_in, w_out, gain_rows = weights
    middle, first_kept = self_forward(inputs, gain_rows[0], w_attn, None)
    result, second_kept = ffn_forward(middle, gain_rows[1], w_in, w_out)
    normed = rms_norm(result, gain_rows[2]).astype(jnp.bfloat16)
    cross_kv = product(normed, w_extra).astype(jnp.bfloat16)
    return (result, cross_kv, (middle, first_kept, second_kept, normed))


def encoder_backward(inputs, weights, grad_result, grad_kv):
    w_attn, w_extra, w_in, w_out, gain_rows = weights
    result, _, kept_values = encoder_forward(inputs, weights)
    middle, first_kept, second_kept, normed = kept_values
    grad_extra = weight_grad(normed, grad_kv)
    grad_final, gain_final = norm_back(result, gain_rows[2], input_back(grad_kv, w_extra))
    grad_middle, gain_late, grad_win, grad_wout = ffn_backward(
        middle, gain_rows[1], w_in, w_out, second_kept, grad_result + grad_final
    )
    grad_inputs, gain_early, grad_attn = self_backward(
        inputs, gain_rows[0], w_attn, None, first_kept, grad_middle
    )
    return (
        grad_inputs,
        (
            grad_attn,
            grad_extra,
            grad_win,
            grad_wout,
            jnp.stack([gain_early, gain_late, gain_final]),
        ),
    )


def decoder_step(inputs, cross_kv, allowed, weights, grad_result):
    w_attn, w_extra, w_in, w_out, gain_rows = weights
    middle, first_kept = self_forward(inputs, gain_rows[0], w_attn, allowed)
    query_in = rms_norm(middle, gain_rows[2]).astype(jnp.bfloat16)
    queries = product(query_in, w_extra[:, :D]).astype(jnp.bfloat16)
    mixed_heads, log_total = attend_plain(queries, cross_kv[:, :D], cross_kv[:, D:], None)
    after_cross = middle + product(mixed_heads, w_extra[:, D:])
    result, second_kept = ffn_forward(after_cross, gain_rows[1], w_in, w_out)
    grad_after, gain_late, grad_win, grad_wout = ffn_backward(
        after_cross, gain_rows[1], w_in, w_out, second_kept, grad_result
    )
    grad_low = grad_after.astype(jnp.bfloat16)
    grad_cross_out = weight_grad(mixed_heads, grad_low)
    grad_mixed = input_back(grad_low, w_extra[:, D:]).astype(jnp.bfloat16)
    grad_queries, grad_keys, grad_values = attend_plain_back(
        queries, cross_kv[:, :D], cross_kv[:, D:], None, log_total, grad_mixed
    )
    grad_queries = grad_queries.astype(jnp.bfloat16)
    grad_cross_in = weight_grad(query_in, grad_queries)
    grad_normed, gain_cross = norm_back(
        middle, gain_rows[2], input_back(grad_queries, w_extra[:, :D])
    )
    grad_inputs, gain_early, grad_attn = self_backward(
        inputs, gain_rows[0], w_attn, allowed, first_kept, grad_after + grad_normed
    )
    grad_kv = jnp.concatenate([grad_keys, grad_values], axis=1).astype(jnp.bfloat16)
    gradients = (
        grad_attn,
        jnp.concatenate([grad_cross_in, grad_cross_out], axis=1),
        grad_win,
        grad_wout,
        jnp.stack([gain_early, gain_late, gain_cross]),
    )
    return (result, grad_inputs, grad_kv, gradients)


def general(acts, w_attn, w_extra, w_in, w_out, gains, segments, cotangent):
    gathered = (
        lax.all_gather(w_attn[0], "dp", axis=0, tiled=True),
        lax.all_gather(w_extra[0], "dp", axis=0, tiled=True),
        lax.all_gather(w_in[0], "dp", axis=0, tiled=True),
        lax.all_gather(w_out[0], "dp", axis=0, tiled=True),
        lax.all_gather(gains[0], "dp", axis=1, tiled=True),
    )
    weights = gathered[:4] + (gathered[4].astype(jnp.float32),)
    inputs = acts[0, :, 0]
    upstream = cotangent[0, :, 0]
    is_first = lax.axis_index("section") == 0
    positions = jnp.arange(SEQ)
    causal = positions[None, :] <= positions[:, None]
    zero_message = jnp.zeros((SEQ, 2 * D), jnp.bfloat16)
    zero_grads = tuple((jnp.zeros(weight.shape, jnp.float32) for weight in weights))
    carried = (jnp.zeros((MICRO, SEQ, D), jnp.float32), jnp.zeros((MICRO, SEQ, D), jnp.float32))
    received = zero_message
    returned = zero_message
    totals = zero_grads
    moments = MICRO + 2
    for moment in range(moments):

        def first_section(carried, received, returned):
            results, grad_inputs = carried
            message = zero_message
            fresh_grads = zero_grads
            if moment < MICRO:
                result, message, _ = encoder_forward(inputs[moment], weights)
                results = results.at[moment].set(result)
            if moment >= 2:
                grad_rows, fresh_grads = encoder_backward(
                    inputs[moment - 2], weights, upstream[moment - 2], returned
                )
                grad_inputs = grad_inputs.at[moment - 2].set(grad_rows)
            return ((results, grad_inputs), message, zero_message, fresh_grads)

        def second_section(carried, received, returned):
            results, grad_inputs = carried
            message = zero_message
            fresh_grads = zero_grads
            if 1 <= moment <= MICRO:
                segment_ids = segments[moment - 1, 0]
                allowed = (segment_ids[:, None] == segment_ids[None, :]) & causal
                result, grad_rows, message, fresh_grads = decoder_step(
                    inputs[moment - 1], received, allowed, weights, upstream[moment - 1]
                )
                results = results.at[moment - 1].set(result)
                grad_inputs = grad_inputs.at[moment - 1].set(grad_rows)
            return ((results, grad_inputs), zero_message, message, fresh_grads)

        carried, forward_message, back_message, fresh_grads = lax.cond(
            is_first, first_section, second_section, carried, received, returned
        )
        if moment < MICRO:
            received = from_behind(forward_message, "section", 1)
        if 1 <= moment <= MICRO:
            returned = from_behind(back_message, "section", -1)
        if moment >= 1:
            totals = tuple((jnp.add(*couple) for couple in zip(totals, fresh_grads)))
    results, grad_inputs = carried
    final = (
        lax.psum_scatter(totals[0], "dp", scatter_dimension=0, tiled=True),
        lax.psum_scatter(totals[1], "dp", scatter_dimension=0, tiled=True),
        lax.psum_scatter(totals[2], "dp", scatter_dimension=0, tiled=True),
        lax.psum_scatter(totals[3], "dp", scatter_dimension=0, tiled=True),
        lax.psum_scatter(totals[4], "dp", scatter_dimension=1, tiled=True),
    )
    return (
        results[None, :, None],
        grad_inputs[None, :, None],
        final[0][None],
        final[1][None],
        final[2][None],
        final[3][None],
        final[4][None],
    )


def step(acts, w_attn, w_extra, w_in, w_out, gains, segments, cotangent):
    anywhere = pl.BlockSpec(memory_space=pl.ANY)
    shape = lambda *s: jax.ShapeDtypeStruct(s, F32)
    scratch = scratch_list()
    held = pl.pallas_call(
        whole_kernel,
        out_shape=(
            shape(ROWS, D), shape(ROWS, D), shape(48, 4 * D), shape(48, 2 * D), shape(48, 2 * FF), shape(128, D), shape(3, 48),
        ),
        in_specs=[anywhere] * 6 + [pl.BlockSpec(memory_space=pltpu.VMEM)] * 2,
        out_specs=[anywhere] * 7,
        scratch_shapes=list(scratch.values()),
        compiler_params=pltpu.CompilerParams(
            collective_id=0, has_side_effects=True, vmem_limit_bytes=63 * 2**20
        ),
    )(
        acts.reshape(ROWS, D), cotangent.reshape(ROWS, D), w_attn[0], w_extra[0], w_in[0], w_out[0], gains[0],
        segments.reshape(MICRO, SEQ),
    )
    results, input_grad, attn, extra, win, wout, grad_gains = held
    like = (1, MICRO, 1, SEQ, D)
    return (
        results.reshape(like), input_grad.reshape(like), attn[None], extra[None], win[None], wout[None], grad_gains[None],
    )


def solution(mesh):
    in_specs = (
        P("section", None, "dp", None, None),
        P("section", "dp", None),
        P("section", "dp", None),
        P("section", "dp", None),
        P("section", "dp", None),
        P("section", None, "dp"),
        P(None, "dp", None),
        P("section", None, "dp", None, None),
    )
    out_specs = (
        P("section", None, "dp", None, None),
        P("section", None, "dp", None, None),
        P("section", "dp", None),
        P("section", "dp", None),
        P("section", "dp", None),
        P("section", "dp", None),
        P("section", None, "dp"),
    )
    fits = mesh.shape["dp"] == 16
    return jax.shard_map(step if fits else general, mesh=mesh, in_specs=in_specs, out_specs=out_specs, check_vma=False)
```
